32 devices in a mesh: dp: 8 (over z, y), seq: 4 (over x, core).
Axes of the slice: x: 2, y: 2, z: 4, core: 2. Of those that a mesh axis runs over, the one named last changes fastest.
Arguments:
- clean_ids: int32 [32, 1024], P('dp', 'seq'), may hold values from 0 to 50303
- lengths: int32 [32], replicated, may hold values from 256 to 1024, as said below
- masked: int32 [32, 256], replicated, may hold values from 0 to 1023, as said below
- attn_in: float32 [768, 2304], P('dp'), may hold values from -0.21875 to 0.21875
- attn_out: float32 [768, 768], P('dp'), may hold values from -2.5 to 2.5
- mlp_in: float32 [768, 3072], P('dp'), may hold values from -0.21875 to 0.21875
- mlp_out: float32 [3072, 768], P('dp'), may hold values from -0.109375 to 0.109375
- table: float32 [50304, 768], P('dp')
- positions: float32 [1024, 768], P('dp'), may hold values from -0.75 to 0.75
- vectors: float32 [14, 768], replicated
- first_attn_in: float32 [768, 2304], P('dp'), may hold values from -2.0861626e-07 to 2.0861626e-07
- first_attn_out: float32 [768, 768], P('dp'), may hold values from -2.0861626e-07 to 2.0861626e-07
- first_mlp_in: float32 [768, 3072], P('dp'), may hold values from -2.0861626e-07 to 2.0861626e-07
- first_mlp_out: float32 [3072, 768], P('dp'), may hold values from -2.0861626e-07 to 2.0861626e-07
- first_table: float32 [50304, 768], P('dp'), may hold values from -2.0861626e-07 to 2.0861626e-07
- first_positions: float32 [1024, 768], P('dp'), may hold values from -2.0861626e-07 to 2.0861626e-07
- first_vectors: float32 [14, 768], replicated, may hold values from -8.34465e-07 to 8.34465e-07
- second_attn_in: float32 [768, 2304], P('dp'), may hold values from 8.60057e-17 to 3.440228e-16
- second_attn_out: float32 [768, 768], P('dp'), may hold values from 8.60057e-17 to 3.440228e-16
- second_mlp_in: float32 [768, 3072], P('dp'), may hold values from 8.60057e-17 to 3.440228e-16
- second_mlp_out: float32 [3072, 768], P('dp'), may hold values from 8.60057e-17 to 3.440228e-16
- second_table: float32 [50304, 768], P('dp'), may hold values from 8.60057e-17 to 3.440228e-16
- second_positions: float32 [1024, 768], P('dp'), may hold values from 8.60057e-17 to 3.440228e-16
- second_vectors: float32 [14, 768], replicated, may hold values from 1.3760912e-15 to 5.504365e-15
Outputs:
- new_attn_in: float32 [768, 2304], P('dp')
- new_attn_out: float32 [768, 768], P('dp')
- new_mlp_in: float32 [768, 3072], P('dp')
- new_mlp_out: float32 [3072, 768], P('dp')
- new_table: float32 [50304, 768], P('dp')
- new_positions: float32 [1024, 768], P('dp')
- new_vectors: float32 [14, 768], replicated
- moment_attn_in: float32 [768, 2304], P('dp')
- moment_attn_out: float32 [768, 768], P('dp')
- moment_mlp_in: float32 [768, 3072], P('dp')
- moment_mlp_out: float32 [3072, 768], P('dp')
- moment_table: float32 [50304, 768], P('dp')
- moment_positions: float32 [1024, 768], P('dp')
- moment_vectors: float32 [14, 768], replicated
- square_attn_in: float32 [768, 2304], P('dp')
- square_attn_out: float32 [768, 768], P('dp')
- square_mlp_in: float32 [768, 3072], P('dp')
- square_mlp_out: float32 [3072, 768], P('dp')
- square_table: float32 [50304, 768], P('dp')
- square_positions: float32 [1024, 768], P('dp')
- square_vectors: float32 [14, 768], replicated
- loss_sum: float32 [], replicated
- masked_count: float32 [], replicated
- grad_norm: float32 [], replicated
The draws below stay inside these ranges and needn't reach their ends.
Inputs may be any that keep to these rules, and one draw needn't show every extreme that they name: `lengths`: each row's length is 256, 512, or between 897 and 1024; in every aligned block of 4 rows one row is longer than 896; some row has length 1024. `masked`: entries k * 64 to (k + 1) * 64 - 1 of a row are distinct slots of k * 256 to (k + 1) * 256 - 1, the first of them k * 256.
All inputs are finite; a program needn't handle non-finite values.
Results may differ from the reference program's by a relative error of at most 0.012.
The reference program's roundings to bfloat16 on the way count: a program that leaves them out, or rounds other values in their place, can miss the bound.
Values may be sent and summed in bfloat16 or wider, within the bound.
A program may use at most 576 MiB of HBM per device.

```python
import math
import jax
import jax.numpy as jnp
import numpy as np
from jax import lax

D = 768
H = 12
HD = 64
FF = 3072
V = 50304
L = 1024
ROWS_DEV = 4
STEP = 10
SLOTS = 256
MASKS = 64
ROWS = 32
NPARAM = 46508544


def draw_lengths(key, part):
    key = jax.random.fold_in(key, 1)
    first_key, second_key, third_key, fourth_key = jax.random.split(key, 4)
    pick = jax.random.randint(first_key, (ROWS,), 0, 3)
    base = jnp.where(pick == 0, L // 4, jnp.where(pick == 1, L // 2, L)).astype(jnp.int32)
    forced = jax.random.randint(second_key, (ROWS // ROWS_DEV,), 0, ROWS_DEV)
    index = jnp.arange(ROWS, dtype=jnp.int32)
    chosen = forced[index // ROWS_DEV] == index % ROWS_DEV
    long_len = L - jax.random.randint(third_key, (ROWS,), 0, SLOTS // 2)
    full_group = jax.random.randint(fourth_key, (), 0, ROWS // ROWS_DEV)
    long_len = jnp.where(index // ROWS_DEV == full_group, L, long_len)
    return jnp.where(chosen, long_len, base).astype(jnp.int32)


def draw_masked(key, part):
    key = jax.random.fold_in(key, 2)
    blocks = L // SLOTS
    keys = jax.random.split(key, ROWS * blocks)

    def block_picks(block_key):
        return jax.random.permutation(block_key, SLOTS - 1)[:MASKS - 1]
    rest = jax.vmap(block_picks)(keys).astype(jnp.int32) + 1
    picks = jnp.concatenate([jnp.zeros((ROWS * blocks, 1), jnp.int32), rest], axis=1)
    offsets = jnp.arange(ROWS * blocks, dtype=jnp.int32) % blocks * SLOTS
    return (picks + offsets[:, None]).reshape(ROWS, blocks * MASKS).astype(jnp.int32)


def draw_table(key, part):
    key = jax.random.fold_in(key, 3)
    rows = jnp.arange(V, dtype=jnp.float32)[:, None] / V
    base = jax.random.normal(key, (V, D), jnp.float32)
    scale = 1.0 + 2.0 * rows
    return base * scale * D ** (-0.5)


def draw_vectors(key, part):
    key = jax.random.fold_in(key, 4)
    first_key, second_key = jax.random.split(key)
    cols = jnp.arange(D, dtype=jnp.float32)[None, :] / D
    rough = jax.random.uniform(first_key, (14, D), jnp.float32, 0.8, 1.2)
    rise = 0.6 + 1.2 * cols
    noise = 0.1 * jax.random.normal(second_key, (14, D), jnp.float32)
    row = jnp.arange(14)[:, None]
    is_gain = (row < 6) & (row % 2 == 0)
    return jnp.where(is_gain, rise * rough, noise)


def touch_ends(entries, own_key, low, top_value):
    extent = entries.shape
    spot = [jax.random.randint(jax.random.fold_in(own_key, axis), (), 0, extent[axis]) for axis in range(len(extent))]
    entries = entries.at[tuple(spot)].set(low)
    longest = extent.index(max(extent))
    spot[longest] = (spot[longest] + 1) % extent[longest]
    return entries.at[tuple(spot)].set(top_value)


def level_of(own_key, shape, cuts, low, high):
    def one(position, parts):
        heights = jax.random.uniform(jax.random.fold_in(jax.random.fold_in(own_key, 6), position), (parts,), jnp.float32, low / len(cuts), high / len(cuts))
        return jnp.repeat(jnp.exp(heights), shape[position] // parts).reshape((-1,) + (1,) * (len(shape) - position - 1))

    level = one(*cuts[0])
    for cut in cuts[1:]:
        level = level * one(*cut)
    return level


def cumulative_ranks(number_of, slope):
    weights = [(1 << 20) // math.isqrt(rank ** slope) + 1 for rank in range(1, number_of + 1)]
    deviation = 1 + sum(weights) // (1 << 30)
    return np.cumsum(np.array([max(1, weight // deviation) for weight in weights]))


def ranked(rng, extent, number_of, lean):
    table = cumulative_ranks(number_of, lean)
    ticket = jax.random.randint(jax.random.fold_in(rng, 1), extent, 0, int(table[number_of - 1]))
    grade = jnp.searchsorted(jnp.asarray(table, jnp.int32), ticket, side="right")
    return jax.random.permutation(jax.random.fold_in(rng, 2), number_of)[grade].astype(jnp.int32)


def bell_draw(key, dims, width, reach, shards=(), kind=jnp.bfloat16):
    drawn = width * jax.random.normal(key, dims, jnp.float32)
    if shards:
        drawn = drawn * level_of(key, dims, shards, -0.22, 0.18)
    return jnp.clip(drawn, -reach, reach).astype(kind)


def setup_inputs(seed: int = 0) -> dict:
    splits = jax.random.split(jax.random.key(seed), 25)
    clean_ids = touch_ends(ranked(splits[0], (ROWS, L), V, 2), jax.random.fold_in(splits[0], 3), 0, V - 1).astype(jnp.int32)
    lengths = draw_lengths(jax.random.fold_in(splits[24], 71), 0)
    masked = draw_masked(jax.random.fold_in(splits[24], 71), 0)
    attn_in = bell_draw(splits[3], (D, 3 * D), D ** -0.5, 0.21875, ((0, 8),), jnp.float32)
    attn_out = bell_draw(splits[4], (D, D), (D * 8 // L) ** -0.5, 2.5, ((0, 8),), jnp.float32)
    mlp_in = bell_draw(splits[5], (D, FF), D ** -0.5, 0.21875, ((0, 8),), jnp.float32)
    mlp_out = bell_draw(splits[6], (FF, D), FF ** -0.5, 0.109375, ((0, 8),), jnp.float32)
    table = draw_table(jax.random.fold_in(splits[24], 71), 0)
    positions = bell_draw(splits[8], (L, D), 0.05, 0.75, ((0, 8),), jnp.float32)
    vectors = draw_vectors(jax.random.fold_in(splits[24], 71), 0)
    first_attn_in = bell_draw(splits[10], (D, 3 * D), (0.00024 * NPARAM ** -0.5), 2.086162567138672e-07, ((0, 8),), jnp.float32)
    first_attn_out = bell_draw(splits[11], (D, D), (0.00024 * NPARAM ** -0.5), 2.086162567138672e-07, ((0, 8),), jnp.float32)
    first_mlp_in = bell_draw(splits[12], (D, FF), (0.00024 * NPARAM ** -0.5), 2.086162567138672e-07, ((0, 8),), jnp.float32)
    first_mlp_out = bell_draw(splits[13], (FF, D), (0.00024 * NPARAM ** -0.5), 2.086162567138672e-07, ((0, 8),), jnp.float32)
    first_table = bell_draw(splits[14], (V, D), (0.00024 * NPARAM ** -0.5), 2.086162567138672e-07, ((0, 8),), jnp.float32)
    first_positions = bell_draw(splits[15], (L, D), (0.00024 * NPARAM ** -0.5), 2.086162567138672e-07, ((0, 8),), jnp.float32)
    first_vectors = bell_draw(splits[16], (14, D), (0.001 * NPARAM ** -0.5), 8.344650268554688e-07, (), jnp.float32)
    second_attn_in = jnp.clip(jnp.exp(math.log(3.440228021042485e-16) - 1.3862944 * jax.random.uniform(splits[17], (D, 3 * D), jnp.float32) ** level_of(splits[17], (D, 3 * D), ((0, 8),), -0.2, 0.2)), 8.600570052606213e-17, 3.440228021042485e-16)
    second_attn_out = jnp.clip(jnp.exp(math.log(3.440228021042485e-16) - 1.3862944 * jax.random.uniform(splits[18], (D, D), jnp.float32) ** level_of(splits[18], (D, D), ((0, 8),), -0.2, 0.2)), 8.600570052606213e-17, 3.440228021042485e-16)
    second_mlp_in = jnp.clip(jnp.exp(math.log(3.440228021042485e-16) - 1.3862944 * jax.random.uniform(splits[19], (D, FF), jnp.float32) ** level_of(splits[19], (D, FF), ((0, 8),), -0.2, 0.2)), 8.600570052606213e-17, 3.440228021042485e-16)
    second_mlp_out = jnp.clip(jnp.exp(math.log(3.440228021042485e-16) - 1.3862944 * jax.random.uniform(splits[20], (FF, D), jnp.float32) ** level_of(splits[20], (FF, D), ((0, 8),), -0.2, 0.2)), 8.600570052606213e-17, 3.440228021042485e-16)
    second_table = jnp.clip(jnp.exp(math.log(3.440228021042485e-16) - 1.3862944 * jax.random.uniform(splits[21], (V, D), jnp.float32) ** level_of(splits[21], (V, D), ((0, 8),), -0.2, 0.2)), 8.600570052606213e-17, 3.440228021042485e-16)
    second_positions = jnp.clip(jnp.exp(math.log(3.440228021042485e-16) - 1.3862944 * jax.random.uniform(splits[22], (L, D), jnp.float32) ** level_of(splits[22], (L, D), ((0, 8),), -0.2, 0.2)), 8.600570052606213e-17, 3.440228021042485e-16)
    second_vectors = jnp.clip(jnp.exp(jax.random.uniform(splits[23], (14, D), jnp.float32, math.log(1.376091208416994e-15), math.log(5.504364833667976e-15))), 1.376091208416994e-15, 5.504364833667976e-15)
    return {"clean_ids": clean_ids, "lengths": lengths, "masked": masked, "attn_in": attn_in, "attn_out": attn_out, "mlp_in": mlp_in, "mlp_out": mlp_out, "table": table, "positions": positions, "vectors": vectors, "first_attn_in": first_attn_in, "first_attn_out": first_attn_out, "first_mlp_in": first_mlp_in, "first_mlp_out": first_mlp_out, "first_table": first_table, "first_positions": first_positions, "first_vectors": first_vectors, "second_attn_in": second_attn_in, "second_attn_out": second_attn_out, "second_mlp_in": second_mlp_in, "second_mlp_out": second_mlp_out, "second_table": second_table, "second_positions": second_positions, "second_vectors": second_vectors}


mask_fill = -1000000000.0
clip_at = 0.002
beta_one = 0.9
beta_two = 0.999
adam_eps = 1e-08

@jax.custom_vjp
def low(v):
    return lax.optimization_barrier(v.astype(jnp.bfloat16)).astype(jnp.float32)

@jax.custom_vjp
def low_back(v):
    return v

def low_keep(v):
    return (low(v), None)

def low_pass(kept, grad):
    return (grad,)

def back_keep(v):
    return (v, None)

def back_low(kept, grad):
    return (low(grad),)
low.defvjp(low_keep, low_pass)
low_back.defvjp(back_keep, back_low)

def matmul_high(left, right):
    return jnp.matmul(left, right, precision=lax.Precision.HIGHEST)

def layer_norm(x, gain, shift):
    centre = x - lax.optimization_barrier(jnp.mean(x, axis=-1, keepdims=True))
    var = lax.optimization_barrier(jnp.mean(centre * centre, axis=-1, keepdims=True))
    return centre * lax.rsqrt(var + 1e-05) * gain + shift

def row_loss(weights, row):
    w_in, w_out, w_up, w_down, table_low, pos_low, vec = weights
    ids, length, picks, target, valid = row
    model = vec.shape[1]
    start = low_back(table_low[ids]) + pos_low
    attn_low = low(layer_norm(start, vec[0], vec[1]))
    in_bias = jnp.concatenate([vec[6], jnp.zeros_like(vec[6]), vec[7]])
    qkv = low(low_back(matmul_high(attn_low, w_in) + in_bias))
    query = qkv[:, :model].reshape(L, H, HD)
    keys = qkv[:, model:2 * model].reshape(L, H, HD)
    values = qkv[:, 2 * model:].reshape(L, H, HD)
    keep = jnp.arange(L) < length
    scores = jnp.einsum('shd,khd->hsk', query, keys, precision=lax.Precision.HIGHEST) * 0.125
    scores = low_back(jnp.where(keep[None, None, :], scores, mask_fill))
    probs = low(jax.nn.softmax(scores, axis=-1))
    mixed = jnp.einsum('hsk,khd->shd', probs, values, precision=lax.Precision.HIGHEST).reshape(L, model)
    mixed = low(low_back(mixed))
    after_attn = start + low_back(matmul_high(mixed, w_out) + vec[8])
    mlp_low = low(layer_norm(after_attn, vec[2], vec[3]))
    up_pre = low_back(matmul_high(mlp_low, w_up) + vec[10:14].reshape(-1))
    act_low = low(jax.nn.gelu(up_pre, approximate=True))
    final_in = after_attn + low_back(matmul_high(act_low, w_down) + vec[9])
    final_low = low(layer_norm(final_in, vec[4], vec[5]))
    sources = final_low[jnp.maximum(picks - 1, 0)]
    logits = low_back(matmul_high(sources, table_low.T))
    log_norm = jax.nn.logsumexp(logits, axis=-1)
    hit = jnp.take_along_axis(logits, target[:, None], axis=1)[:, 0]
    return jnp.sum(valid * (log_norm - hit))

def adam_update(weight, grad, first, second, rate, decay):
    first_new = beta_one * first + (1.0 - beta_one) * grad
    second_new = beta_two * second + (1.0 - beta_two) * grad * grad
    mhat = first_new / (1.0 - beta_one ** STEP)
    vhat = second_new / (1.0 - beta_two ** STEP)
    return (weight - rate * (mhat / (jnp.sqrt(vhat) + adam_eps) + decay * weight), first_new, second_new)

def reference(clean_ids, lengths, masked, attn_in, attn_out, mlp_in, mlp_out, table, positions, vectors, first_attn_in, first_attn_out, first_mlp_in, first_mlp_out, first_table, first_positions, first_vectors, second_attn_in, second_attn_out, second_mlp_in, second_mlp_out, second_table, second_positions, second_vectors):
    valid = ((masked >= 1) & (masked < lengths[:, None])).astype(jnp.float32)
    masked_count = jnp.sum(valid)
    row_ix = jnp.arange(ROWS, dtype=jnp.int32)[:, None]
    is_masked = jnp.zeros((ROWS, L), jnp.int32).at[row_ix, masked].set(1)
    noisy = jnp.where(is_masked > 0, V - 1, clean_ids).astype(jnp.int32)
    target = jnp.take_along_axis(clean_ids, masked, axis=1)
    params = (attn_in, attn_out, mlp_in, mlp_out, table, positions, vectors)

    def loss_fn(weights):
        lowered = tuple((low(w) for w in weights[:6])) + (weights[6],)

        def step_fn(carry, row):
            return (carry + row_loss(lowered, row), None)
        total, unused = lax.scan(jax.checkpoint(step_fn), jnp.zeros((), jnp.float32), (noisy, lengths, masked, target, valid))
        return (total / masked_count, total)
    loss, vjp_fn, loss_sum = jax.vjp(loss_fn, params, has_aux=True)
    grads = vjp_fn(jnp.ones((), jnp.float32))[0]
    grad_norm = jnp.sqrt(sum((jnp.sum(g * g) for g in grads)))
    factor = clip_at / jnp.maximum(grad_norm, clip_at)
    firsts = (first_attn_in, first_attn_out, first_mlp_in, first_mlp_out, first_table, first_positions, first_vectors)
    seconds = (second_attn_in, second_attn_out, second_mlp_in, second_mlp_out, second_table, second_positions, second_vectors)
    news, moments, squares = ([], [], [])
    for index in range(7):
        rate, decay = (1.0, 0.0) if index == 6 else (0.1, 0.1)
        new_w, new_m, new_v = adam_update(params[index], grads[index] * factor, firsts[index], seconds[index], rate, decay)
        news.append(new_w)
        moments.append(new_m)
        squares.append(new_v)
    return (news[0], news[1], news[2], news[3], news[4], news[5], news[6], moments[0], moments[1], moments[2], moments[3], moments[4], moments[5], moments[6], squares[0], squares[1], squares[2], squares[3], squares[4], squares[5], squares[6], loss_sum, masked_count, grad_norm)
```

```python
import math

import jax
import jax.numpy as jnp
from jax import lax
from jax.experimental import pallas as pl
from jax.experimental.pallas import tpu as pltpu
from jax.sharding import PartitionSpec as P

H = 12
STEP = 10
FETCH = 96
GIVE = 64

mask_fill = -1000000000.0
clip_at = 0.002
beta_one = 0.9
beta_two = 0.999
adam_eps = 1e-08

f32 = jnp.float32
bf16 = jnp.bfloat16
i32 = jnp.int32
HBM = pl.BlockSpec(memory_space=pl.ANY)
MESH = pl.DeviceIdType.MESH


def deliver(x, axes, call_id, block_of=None):
    sizes = [lax.axis_size(axis) for axis in axes]
    count = math.prod(sizes)
    block = x.shape if block_of is None else x.shape[1:]

    def body(x_ref, o_ref, sent, came, own):
        here = [lax.axis_index(axis) for axis in axes]

        def flat(place):
            index = place[0]
            for size, along in zip(sizes[1:], place[1:]):
                index = index * size + along
            return index

        def peer(step):
            place = []
            for size, at in zip(reversed(sizes), reversed(here)):
                place.append(lax.rem(at + lax.rem(step, size), size))
                step = step // size
            return place[::-1]

        def source(place):
            return x_ref if block_of is None else x_ref.at[block_of(place)]

        mine = flat(here)

        def copy(step):
            place = peer(step)
            return pltpu.make_async_remote_copy(
                source(place),
                o_ref.at[mine],
                sent.at[step],
                came.at[step],
                device_id=dict(zip(axes, place)),
                device_id_type=MESH,
            )

        barrier = pltpu.get_barrier_semaphore()

        @pl.loop(1, count)
        def _(step):
            pl.semaphore_signal(
                barrier, inc=1, device_id=dict(zip(axes, peer(step))), device_id_type=MESH
            )

        local = pltpu.make_async_copy(source(here), o_ref.at[mine], own)
        local.start()
        pl.semaphore_wait(barrier, count - 1)

        @pl.loop(1, count)
        def _(step):
            copy(step).start()

        local.wait()

        @pl.loop(1, count)
        def _(step):
            copy(step).wait()

    return pl.pallas_call(
        body,
        out_shape=jax.ShapeDtypeStruct((count,) + block, x.dtype),
        in_specs=[HBM],
        out_specs=HBM,
        scratch_shapes=[
            pltpu.SemaphoreType.DMA((count,)),
            pltpu.SemaphoreType.DMA((count,)),
            pltpu.SemaphoreType.DMA,
        ],
        compiler_params=pltpu.CompilerParams(collective_id=call_id, has_side_effects=True),
    )(x)


def flip(x, axis, span):
    count = lax.axis_size(axis)
    pairs = [(at, at // (2 * span) * 2 * span + (at + span) % (2 * span)) for at in range(count)]
    return lax.ppermute(x, axis, pairs)


def layer_norm(x, gain, shift):
    centre = x - jnp.mean(x, axis=-1, keepdims=True)
    var = jnp.mean(centre * centre, axis=-1, keepdims=True)
    return centre * lax.rsqrt(var + 1e-05) * gain + shift


def gelu_fn(x):
    return jax.nn.gelu(x, approximate=True)


def adam_update(weight, grad, first, second, rate, decay):
    first_new = beta_one * first + (1.0 - beta_one) * grad
    second_new = beta_two * second + (1.0 - beta_two) * grad * grad
    mhat = first_new / (1.0 - beta_one**STEP)
    vhat = second_new / (1.0 - beta_two**STEP)
    return (
        weight - rate * (mhat / (jnp.sqrt(vhat) + adam_eps) + decay * weight),
        first_new,
        second_new,
    )


def as_rows(flat):
    return jnp.pad(flat, (0, -flat.size % 1024)).reshape(-1, 128)


def on_device(
    clean_ids,
    lengths,
    masked,
    attn_in,
    attn_out,
    mlp_in,
    mlp_out,
    table,
    positions,
    vectors,
    first_attn_in,
    first_attn_out,
    first_mlp_in,
    first_mlp_out,
    first_table,
    first_positions,
    first_vectors,
    second_attn_in,
    second_attn_out,
    second_mlp_in,
    second_mlp_out,
    second_table,
    second_positions,
    second_vectors,
):
    rows, slots = clean_ids.shape
    n_dp = lax.axis_size("dp")
    n_seq = lax.axis_size("seq")
    dp_at = lax.axis_index("dp")
    seq_at = lax.axis_index("seq")
    core = lax.rem(seq_at, 2)
    length = slots * n_seq
    vocab_part, model = table.shape
    vocab = vocab_part * n_dp
    head_dim = model // H
    sharers = max(1, n_seq // rows)
    n_pick = masked.shape[1] // sharers
    row_at = seq_at // sharers
    share = lax.rem(seq_at, sharers)
    half = -(-vocab_part // 32) * 16

    def gathered(weight):
        piece = weight.shape[0] // n_seq
        part = lax.dynamic_slice_in_dim(weight, seq_at * piece, piece, 0).astype(bf16)
        return lax.all_gather(part, ("dp", "seq"), axis=0, tiled=True)

    pos_all = gathered(positions)
    w_in = gathered(attn_in)
    w_out = gathered(attn_out)
    w_up = gathered(mlp_in)
    w_down = gathered(mlp_out)

    all_rows = deliver(clean_ids, ("seq",), 1)
    row_ids = lax.dynamic_index_in_dim(all_rows, row_at, 1, keepdims=False).reshape(length)
    row = dp_at * rows + row_at
    row_length = lax.dynamic_index_in_dim(lengths, row, 0, keepdims=False)
    row_masked = lax.dynamic_index_in_dim(masked, row, 0, keepdims=False)
    picks = lax.dynamic_slice_in_dim(row_masked, share * n_pick, n_pick, 0)
    slot = jnp.arange(length, dtype=i32)
    is_masked = jnp.any(slot[:, None] == row_masked[None, :], axis=1)
    noisy = jnp.where(is_masked, vocab - 1, row_ids)
    targets = jnp.sum(jnp.where(picks[:, None] == slot[None, :], row_ids[None, :], 0), axis=1)
    valid_all = ((masked >= 1) & (masked < lengths[:, None])).astype(f32)
    masked_count = jnp.sum(valid_all)

    owner = noisy // vocab_part
    within = noisy - owner * vocab_part
    owner_half = owner * 2 + (within >= half).astype(i32)
    within_half = jnp.where(within >= half, within - half, within)
    same = noisy[:, None] == noisy[None, :]
    leader = jnp.min(jnp.where(same, slot[None, :], length), axis=1)
    leads = leader == slot
    before = (slot[None, :] < slot[:, None]) & leads[None, :]
    rank = jnp.sum((before & (owner[:, None] == owner[None, :])).astype(i32), axis=1)
    rank_half = jnp.sum((before & (owner_half[:, None] == owner_half[None, :])).astype(i32), axis=1)
    lead_of = leader[:, None] == slot[None, :]
    place = jnp.sum(jnp.where(lead_of, rank[None, :], 0), axis=1)
    place_half = jnp.sum(jnp.where(lead_of, rank_half[None, :], 0), axis=1)

    def asked(owners, ranks, names, count, size, turn):
        spot = jnp.where(ranks // size == turn, owners * size + lax.rem(ranks, size), -1)
        spots = jnp.arange(count * size, dtype=i32)
        listed = leads[None, :] & (spots[:, None] == spot[None, :])
        return spot, jnp.sum(jnp.where(listed, names[None, :], 0), axis=1)

    spot, ask = asked(owner, place, within, n_dp, FETCH, 0)
    spot_half, ask_half = asked(owner_half, place_half, within_half, 2 * n_dp, GIVE, 0)
    turns = jnp.stack([jnp.max(place) // FETCH + 1, jnp.max(place_half) // GIVE + 1])
    pieces = [as_rows(piece) for piece in (ask, ask_half, targets, turns)]
    ends = [0]
    for piece in pieces:
        ends.append(ends[-1] + piece.shape[0])
    told = deliver(jnp.concatenate(pieces), ("dp", "seq"), 2)

    def heard(index, size):
        return told[:, ends[index] : ends[index + 1]].reshape(n_dp * n_seq, -1)[:, :size]

    turns = jnp.max(heard(3, 2), axis=0)
    asks = lax.dynamic_index_in_dim(heard(0, n_dp * FETCH).reshape(n_dp, n_seq, n_dp, FETCH), seq_at, 1, False)
    asks = lax.dynamic_index_in_dim(asks, dp_at, 1, False)
    half_at = dp_at * 2 + core
    asks_half = lax.dynamic_index_in_dim(heard(1, 2 * n_dp * GIVE).reshape(-1, 2 * n_dp, GIVE), half_at, 1, False)
    all_targets = lax.dynamic_index_in_dim(heard(2, n_pick).reshape(n_dp, n_seq, n_pick), seq_at, 1, False)

    def one_hot(spots, count):
        return (spots[:, None] == jnp.arange(count, dtype=i32)[None, :]).astype(bf16)

    found = jnp.take(table, asks, axis=0).astype(bf16)
    fetched = deliver(found, ("dp",), 3, lambda place: place[0]).reshape(n_dp * FETCH, model)
    embedded = jnp.dot(one_hot(spot, n_dp * FETCH), fetched, preferred_element_type=f32)

    def fetch_more(state):
        turn, total = state
        next_spot, next_ask = asked(owner, place, within, n_dp, FETCH, turn)
        wanted = lax.all_to_all(next_ask.reshape(n_dp, FETCH), "dp", 0, 0)
        sent = jnp.take(table, wanted, axis=0).astype(bf16)
        got = lax.all_to_all(sent, "dp", 0, 0).reshape(n_dp * FETCH, model)
        return turn + 1, total + jnp.dot(one_hot(next_spot, n_dp * FETCH), got, preferred_element_type=f32)

    _, embedded = lax.while_loop(lambda state: state[0] < turns[0], fetch_more, (jnp.int32(1), embedded))

    start = embedded + pos_all.astype(f32)
    attn_normed, norm_one_back = jax.vjp(layer_norm, start, vectors[0], vectors[1])
    attn_low = attn_normed.astype(bf16)
    in_bias = jnp.concatenate([vectors[6], jnp.zeros_like(vectors[6]), vectors[7]])
    qkv = (jnp.dot(attn_low, w_in, preferred_element_type=f32) + in_bias).astype(bf16)
    chosen = one_hot(picks - 1, length)
    query = jnp.dot(chosen, qkv[:, :model], preferred_element_type=f32).astype(bf16)
    start_picked = jnp.dot(chosen.astype(f32), start, precision=lax.Precision.HIGHEST)
    q_heads = query.reshape(n_pick, H, head_dim)
    k_heads = qkv[:, model : 2 * model].reshape(length, H, head_dim)
    v_heads = qkv[:, 2 * model :].reshape(length, H, head_dim)
    key_keep = (slot < row_length)[None, None, :]
    raw = jnp.einsum("shd,khd->hsk", q_heads, k_heads, preferred_element_type=f32) * 0.125
    scores = jnp.where(key_keep, raw, mask_fill)
    log_total = jax.nn.logsumexp(scores, axis=-1, keepdims=True)
    probs = jnp.exp(scores - log_total)
    probs_low = probs.astype(bf16)
    mixed = jnp.einsum("hsk,khd->shd", probs_low, v_heads, preferred_element_type=f32)
    mixed = mixed.reshape(n_pick, model).astype(bf16)
    after_attn = start_picked + jnp.dot(mixed, w_out, preferred_element_type=f32) + vectors[8]
    mlp_normed, norm_two_back = jax.vjp(layer_norm, after_attn, vectors[2], vectors[3])
    mlp_low = mlp_normed.astype(bf16)
    up_pre = jnp.dot(mlp_low, w_up, preferred_element_type=f32) + vectors[10:14].reshape(-1)
    activated, gelu_back = jax.vjp(gelu_fn, up_pre)
    act_low = activated.astype(bf16)
    final_in = after_attn + jnp.dot(act_low, w_down, preferred_element_type=f32) + vectors[9]
    final_normed, norm_end_back = jax.vjp(layer_norm, final_in, vectors[4], vectors[5])
    sources = final_normed.astype(bf16)

    table_low = table.astype(bf16)
    heads = deliver(sources, ("dp",), 4).reshape(n_dp * n_pick, model)
    logits = jnp.einsum("nd,vd->nv", heads, table_low, preferred_element_type=f32)
    flat_targets = all_targets.reshape(-1) - dp_at * vocab_part
    rows_here = valid_all.reshape(n_dp, rows, sharers, n_pick)
    rows_here = lax.dynamic_index_in_dim(rows_here, row_at, 1, False)
    flat_valid = lax.dynamic_index_in_dim(rows_here, share, 1, False).reshape(-1)
    hit_mask = flat_targets[:, None] == jnp.arange(vocab_part, dtype=i32)[None, :]
    part_max = jnp.max(logits, axis=1)
    part_sum = jnp.sum(jnp.exp(logits - part_max[:, None]), axis=1)
    part_hit = jnp.sum(jnp.where(hit_mask, logits, 0.0), axis=1)
    stats = jnp.stack([part_max, part_sum, part_hit]).reshape(3, -1, 128)
    stats = deliver(stats, ("dp",), 5).reshape(n_dp, 3, -1)
    top = jnp.max(stats[:, 0], axis=0)
    summed = jnp.sum(stats[:, 1] * jnp.exp(stats[:, 0] - top[None]), axis=0)
    log_norm = top + jnp.log(summed)
    loss_group = jnp.sum(flat_valid * (log_norm - jnp.sum(stats[:, 2], axis=0)))
    logit_grad = (
        (flat_valid / masked_count)[:, None]
        * (jnp.exp(logits - log_norm[:, None]) - hit_mask.astype(f32))
    ).astype(bf16)
    heads_grad = jnp.dot(logit_grad, table_low, preferred_element_type=f32)
    final_grad = deliver(
        heads_grad.astype(bf16).reshape(n_dp, n_pick, model), ("dp",), 6, lambda place: place[0]
    )
    final_grad = jnp.sum(final_grad.astype(f32), axis=0)
    table_grad = jnp.einsum("nv,nd->vd", logit_grad, heads, preferred_element_type=f32)
    table_grad = jnp.pad(table_grad, ((0, 2 * half - vocab_part), (0, 0)))
    half_own = lax.dynamic_slice_in_dim(table_grad, core * half, half, 0)
    half_other = lax.dynamic_slice_in_dim(table_grad, (1 - core) * half, half, 0).astype(bf16)
    half_low = (half_own + flip(half_other, "seq", 1).astype(f32)).astype(bf16)
    if n_seq == 4:
        half_sum = half_low.astype(f32) + flip(half_low, "seq", 2).astype(f32)
    else:
        groups = [list(range(at, n_seq, 2)) for at in range(2)]
        half_sum = jnp.sum(lax.all_gather(half_low, "seq", axis_index_groups=groups).astype(f32), axis=0)

    final_in_grad, gain_end, shift_end = norm_end_back(final_grad)
    down_grad = final_in_grad.astype(bf16)
    w_down_grad = jnp.einsum("sf,sd->fd", act_low, down_grad, preferred_element_type=f32)
    down_bias = jnp.sum(down_grad.astype(f32), axis=0)
    act_grad = jnp.einsum("sd,fd->sf", down_grad, w_down, preferred_element_type=f32)
    up_grad = gelu_back(act_grad)[0].astype(bf16)
    up_bias = jnp.sum(up_grad.astype(f32), axis=0)
    w_up_grad = jnp.einsum("sd,sf->df", mlp_low, up_grad, preferred_element_type=f32)
    mlp_grad = jnp.einsum("sf,df->sd", up_grad, w_up, preferred_element_type=f32)
    attn_res_grad, gain_two, shift_two = norm_two_back(mlp_grad)
    after_grad = final_in_grad + attn_res_grad
    out_grad = after_grad.astype(bf16)
    out_bias = jnp.sum(out_grad.astype(f32), axis=0)
    w_out_grad = jnp.einsum("se,sd->ed", mixed, out_grad, preferred_element_type=f32)
    mixed_grad = jnp.einsum("sd,ed->se", out_grad, w_out, preferred_element_type=f32).astype(bf16)
    mixed_grad = mixed_grad.reshape(n_pick, H, head_dim)
    prob_grad = jnp.einsum("shd,khd->hsk", mixed_grad, v_heads, preferred_element_type=f32)
    correction = jnp.sum(prob_grad * probs, axis=-1, keepdims=True)
    score_grad = (probs * (prob_grad - correction)).astype(bf16)
    query_grad = jnp.einsum("hsk,khd->shd", score_grad, k_heads, preferred_element_type=f32) * 0.125
    key_grad = jnp.einsum("hsk,shd->khd", score_grad, q_heads, preferred_element_type=f32) * 0.125
    value_grad = jnp.einsum("hsk,shd->khd", probs_low, mixed_grad, preferred_element_type=f32)
    query_grad = query_grad.reshape(n_pick, model).astype(bf16)
    query_full = jnp.einsum("st,sd->td", chosen, query_grad, preferred_element_type=f32).astype(bf16)
    qkv_grad = jnp.concatenate(
        [
            query_full,
            key_grad.reshape(length, model).astype(bf16),
            value_grad.reshape(length, model).astype(bf16),
        ],
        axis=-1,
    )
    qkv_bias = jnp.sum(qkv_grad.astype(f32), axis=0)
    w_in_grad = jnp.einsum("sd,se->de", attn_low, qkv_grad, preferred_element_type=f32)
    normed_grad = jnp.einsum("se,de->sd", qkv_grad, w_in, preferred_element_type=f32)
    start_extra, gain_one, shift_one = norm_one_back(normed_grad)
    after_full = jnp.einsum(
        "st,sd->td", chosen.astype(f32), after_grad, precision=lax.Precision.HIGHEST
    )
    start_grad = after_full + start_extra
    start_grad_low = start_grad.astype(bf16)

    def given(spots):
        summed_ids = jnp.einsum(
            "ts,td->sd", one_hot(spots, 2 * n_dp * GIVE), start_grad_low, preferred_element_type=f32
        )
        return summed_ids.astype(bf16).reshape(2 * n_dp, GIVE, model)

    def taken(names, values):
        names = names.reshape(1, -1)
        where = (jnp.arange(half, dtype=i32)[:, None] == names).astype(bf16)
        return jnp.dot(where, values.reshape(-1, model), preferred_element_type=f32)

    came = deliver(
        given(spot_half), ("dp", "seq"), 7, lambda place: place[0] * 2 + lax.rem(place[1], 2)
    )
    half_sum = half_sum + taken(asks_half, came)

    def give_more(state):
        turn, total = state
        next_spot, next_ask = asked(owner_half, place_half, within_half, 2 * n_dp, GIVE, turn)
        names = lax.all_gather(next_ask.reshape(2 * n_dp, GIVE), ("dp", "seq"))
        names = lax.dynamic_index_in_dim(names, half_at, 1, False)
        sent = given(next_spot).reshape(n_dp, 1, 2, GIVE, model)
        sent = jnp.broadcast_to(sent, (n_dp, n_seq // 2, 2, GIVE, model)).reshape(-1, GIVE, model)
        got = lax.all_to_all(sent, ("dp", "seq"), 0, 0)
        return turn + 1, total + taken(names, got)

    _, half_sum = lax.while_loop(lambda state: state[0] < turns[1], give_more, (jnp.int32(1), half_sum))

    def spread_sum(grad):
        pieces = grad.reshape(n_dp, n_seq, -1, grad.shape[1]).astype(bf16)
        pieces = pieces.reshape(-1, grad.shape[1])
        part = lax.psum_scatter(pieces, ("dp", "seq"), scatter_dimension=0, tiled=True)
        return lax.all_gather(part, "seq", axis=0, tiled=True).astype(f32)

    g_down = spread_sum(w_down_grad)
    g_up = spread_sum(w_up_grad)
    g_out = spread_sum(w_out_grad)
    g_in = spread_sum(w_in_grad)
    g_pos = spread_sum(start_grad)
    vec_grad = jnp.concatenate(
        [
            jnp.stack(
                [
                    gain_one,
                    shift_one,
                    gain_two,
                    shift_two,
                    gain_end,
                    shift_end,
                    qkv_bias[:model],
                    qkv_bias[2 * model :],
                    out_bias,
                    down_bias,
                ]
            ),
            up_bias.reshape(-1, model),
        ],
        axis=0,
    )
    vec_total = lax.psum(vec_grad, ("dp", "seq"))
    half_square = jnp.sum(half_sum * half_sum)
    half_low = half_sum.astype(bf16)
    half_pair = flip(half_low, "seq", 1)
    table_sum = jnp.where(
        core == 0, jnp.concatenate([half_low, half_pair]), jnp.concatenate([half_pair, half_low])
    )[:vocab_part].astype(f32)
    layer_grads = (g_in, g_out, g_up, g_down, g_pos)
    layer_square = sum(jnp.sum(g * g) for g in layer_grads)
    said = jnp.concatenate(
        [
            jnp.full((1, 128), half_square),
            jnp.full((1, 128), layer_square),
            jnp.full((1, 128), loss_group),
            jnp.zeros((5, 128), f32),
        ]
    )
    said = deliver(said, ("dp", "seq"), 8)[:, :3, 0].reshape(n_dp, n_seq, 3)
    square_total = jnp.sum(said[:, :2, 0]) + jnp.sum(said[:, 0, 1])
    loss_sum = jnp.sum(said[0, :, 2])
    grad_norm = jnp.sqrt(square_total + jnp.sum(vec_total * vec_total))
    factor = clip_at / jnp.maximum(grad_norm, clip_at)
    weights = (attn_in, attn_out, mlp_in, mlp_out, table, positions, vectors)
    all_grads = (g_in, g_out, g_up, g_down, table_sum, g_pos, vec_total)
    firsts = (
        first_attn_in,
        first_attn_out,
        first_mlp_in,
        first_mlp_out,
        first_table,
        first_positions,
        first_vectors,
    )
    seconds = (
        second_attn_in,
        second_attn_out,
        second_mlp_in,
        second_mlp_out,
        second_table,
        second_positions,
        second_vectors,
    )
    news, moments, squares = ([], [], [])
    for index in range(7):
        rate, decay = (1.0, 0.0) if index == 6 else (0.1, 0.1)
        new_w, new_m, new_v = adam_update(
            weights[index], all_grads[index] * factor, firsts[index], seconds[index], rate, decay
        )
        news.append(new_w)
        moments.append(new_m)
        squares.append(new_v)
    return (*news, *moments, *squares, loss_sum, masked_count, grad_norm)


def solution(mesh):
    part = P("dp", None)
    six = (part,) * 6 + (P(),)
    return jax.shard_map(
        on_device,
        mesh=mesh,
        in_specs=(P("dp", "seq"), P(), P()) + six * 3,
        out_specs=six * 3 + (P(), P(), P()),
        check_vma=False,
    )
```

```python
import math

import jax
import jax.numpy as jnp
from jax import lax
from jax.experimental import pallas as pl
from jax.experimental.pallas import tpu as pltpu
from jax.sharding import PartitionSpec as P

H = 12
STEP = 10
FETCH = 96
GIVE = 64

mask_fill = -1000000000.0
clip_at = 0.002
beta_one = 0.9
beta_two = 0.999
adam_eps = 1e-08

f32 = jnp.float32
bf16 = jnp.bfloat16
i32 = jnp.int32
HBM = pl.BlockSpec(memory_space=pl.ANY)
VMEM = pl.BlockSpec(memory_space=pltpu.VMEM)
MESH = pl.DeviceIdType.MESH


def deliver(x, axes, call_id, block_of=None):
    sizes = [lax.axis_size(axis) for axis in axes]
    count = math.prod(sizes)
    block = x.shape if block_of is None else x.shape[1:]

    def body(x_ref, o_ref, sent, came, own):
        here = [lax.axis_index(axis) for axis in axes]

        def flat(place):
            index = place[0]
            for size, along in zip(sizes[1:], place[1:]):
                index = index * size + along
            return index

        def peer(step):
            place = []
            for size, at in zip(reversed(sizes), reversed(here)):
                place.append(lax.rem(at + lax.rem(step, size), size))
                step = step // size
            return place[::-1]

        def source(place):
            return x_ref if block_of is None else x_ref.at[block_of(place)]

        mine = flat(here)

        def copy(step):
            place = peer(step)
            return pltpu.make_async_remote_copy(
                source(place),
                o_ref.at[mine],
                sent.at[step],
                came.at[step],
                device_id=dict(zip(axes, place)),
                device_id_type=MESH,
            )

        barrier = pltpu.get_barrier_semaphore()

        @pl.loop(1, count)
        def _(step):
            pl.semaphore_signal(
                barrier, inc=1, device_id=dict(zip(axes, peer(step))), device_id_type=MESH
            )

        local = pltpu.make_async_copy(source(here), o_ref.at[mine], own)
        local.start()
        pl.semaphore_wait(barrier, count - 1)

        @pl.loop(1, count)
        def _(step):
            copy(step).start()

        local.wait()

        @pl.loop(1, count)
        def _(step):
            copy(step).wait()

    return pl.pallas_call(
        body,
        out_shape=jax.ShapeDtypeStruct((count,) + block, x.dtype),
        in_specs=[HBM],
        out_specs=HBM,
        scratch_shapes=[
            pltpu.SemaphoreType.DMA((count,)),
            pltpu.SemaphoreType.DMA((count,)),
            pltpu.SemaphoreType.DMA,
        ],
        compiler_params=pltpu.CompilerParams(collective_id=call_id, has_side_effects=True),
    )(x)


def from_peer(x, axis, span, size, step):
    pairs = []
    for at in range(lax.axis_size(axis)):
        digit = at // span % size
        pairs.append((at, at + ((digit + step) % size - digit) * span))
    return lax.ppermute(x, axis, pairs)


def group_sum(x, dim, axis, span):
    size = x.shape[dim]
    at = lax.rem(lax.axis_index(axis) // span, size)
    total = lax.dynamic_index_in_dim(x, at, dim, False).astype(f32)
    for step in range(1, size):
        block = lax.dynamic_index_in_dim(x, lax.rem(at + step, size), dim, False)
        total = total + from_peer(block, axis, span, size, step).astype(f32)
    return total.astype(bf16)


def group_join(x, dim, axis, span, size):
    at = lax.rem(lax.axis_index(axis) // span, size)
    parts = [x] + [from_peer(x, axis, span, size, size - step) for step in range(1, size)]
    if size == 2:
        first = jnp.where(at == 0, parts[0], parts[1])
        second = jnp.where(at == 0, parts[1], parts[0])
        return jnp.stack([first, second], axis=dim)
    turned = jnp.stack(parts + parts, axis=dim)
    return lax.dynamic_slice_in_dim(turned, size - at, size, dim)


def settle(grads, given, vector, n_x, n_y, n_z, call_id):
    n_dp, _, _, chunks, height, width = grads.shape
    n_seq = 2 * n_x
    count = n_dp * n_seq
    near = n_dp * 2
    n_most = max(n_x, n_y)
    blocks = n_x * n_y * n_z

    def body(g_ref, e_ref, v_ref, o_ref, came_ref, vec_ref, *scratch):
        own, got, first, second, third = scratch[:5]
        v_core, v_x, v_y, v_z = scratch[5:9]
        core_out, core_in, core_own = scratch[9:12]
        one_out, one_in, two_out, two_in, three_out, three_in = scratch[12:18]
        x_out, x_in, pair_out, pair_in, last_own = scratch[18:23]
        e_out, e_in, far_out, far_in, v_out, v_in, side_own = scratch[23:]
        dp_at, seq_at = lax.axis_index("dp"), lax.axis_index("seq")
        x_at, c_at = seq_at // 2, lax.rem(seq_at, 2)
        z_at, y_at = dp_at // n_y, lax.rem(dp_at, n_y)
        partner = {"seq": x_at * 2 + 1 - c_at}

        def send(source, target, out_sem, in_sem, device):
            copy = pltpu.make_async_remote_copy(
                source, target, out_sem, in_sem, device_id=device, device_id_type=MESH
            )
            copy.start()
            return copy

        barrier = pltpu.get_barrier_semaphore()

        @pl.loop(1, count)
        def _(step):
            seq_to = lax.rem(seq_at + lax.rem(step, n_seq), n_seq)
            peer = {"dp": lax.rem(dp_at + step // n_seq, n_dp), "seq": seq_to}
            pl.semaphore_signal(barrier, inc=1, device_id=peer, device_id_type=MESH)

        def x_first(chunk):
            return chunk % 2 == 0

        def order(chunk):
            return (n_x, x_at, n_y, y_at) if x_first(chunk) else (n_y, y_at, n_x, x_at)

        def places(chunk, block):
            z, y, x = block // (n_y * n_x), lax.rem(block // n_x, n_y), lax.rem(block, n_x)
            at = (x * n_y + y) * n_z + z if x_first(chunk) else (y * n_x + x) * n_z + z
            return z * n_y + y, x, at

        for chunk in range(chunks):

            @pl.loop(0, blocks)
            def _(block):
                owner, x, at = places(chunk, block)
                source = g_ref.at[owner, c_at, x, chunk]
                pltpu.make_async_copy(source, own.at[chunk, at], core_own.at[chunk]).start()

        v_core[c_at] = v_ref[...]
        mine = came_ref.at[dp_at * n_seq + seq_at]
        side = pltpu.make_async_copy(e_ref.at[dp_at * 2 + c_at], mine, side_own)
        side.start()
        pl.semaphore_wait(barrier, count - 1)
        for chunk in range(chunks):

            @pl.loop(0, blocks)
            def _(block):
                owner, x, at = places(chunk, block)
                source = g_ref.at[owner, 1 - c_at, x, chunk]
                send(source, got.at[chunk, at], core_out.at[chunk], core_in.at[chunk], partner)

        v_turn = [
            (v_core, c_at, 2, lambda to: {"seq": x_at * 2 + to}),
            (v_x, x_at, n_x, lambda to: {"seq": to * 2 + c_at}),
            (v_y, y_at, n_y, lambda to: {"dp": z_at * n_y + to}),
            (v_z, z_at, n_z, lambda to: {"dp": to * n_y + y_at}),
        ]

        def vector_out(turn):
            buffer, at, size, device = v_turn[turn]
            return [
                send(
                    buffer.at[at],
                    buffer.at[at],
                    v_out.at[turn, step - 1],
                    v_in.at[turn, step - 1],
                    device(lax.rem(at + step, size)),
                )
                for step in range(1, size)
            ]

        def vector_sum(turn, copies):
            buffer, _, size, _ = v_turn[turn]
            for copy in copies:
                copy.wait()
            total = buffer[0]
            for place in range(1, size):
                total = total + buffer[place]
            return total

        v_copies = vector_out(0)

        def near_copy(step):
            owner = lax.rem(dp_at + step // 2, n_dp)
            core = lax.rem(c_at + lax.rem(step, 2), 2)
            return pltpu.make_async_remote_copy(
                e_ref.at[owner * 2 + core],
                mine,
                e_out.at[step],
                e_in.at[step],
                device_id={"dp": owner, "seq": x_at * 2 + core},
                device_id_type=MESH,
            )

        def far_copy(step, turn):
            origin = lax.rem(dp_at + n_dp - step // 2, n_dp)
            core = lax.rem(c_at + lax.rem(step, 2), 2)
            block = came_ref.at[origin * n_seq + x_at * 2 + core]
            to = lax.rem(x_at + turn, n_x) * 2 + c_at
            return pltpu.make_async_remote_copy(
                block,
                block,
                far_out.at[step, turn - 1],
                far_in.at[step, turn - 1],
                device_id={"seq": to},
                device_id_type=MESH,
            )

        @pl.loop(1, near)
        def _(step):
            near_copy(step).start()

        kept = {}
        for chunk in range(chunks):
            n_first, at_first, n_second, at_second = order(chunk)
            span = n_second * n_z
            whole = own.at[chunk]
            pltpu.make_async_copy(whole, whole, core_own.at[chunk]).wait()
            pltpu.make_async_remote_copy(
                whole, whole, core_out.at[chunk], core_in.at[chunk], device_id=partner, device_id_type=MESH
            ).wait()

            @pl.loop(0, blocks)
            def _(block):
                total = own[chunk, block].astype(f32) + got[chunk, block].astype(f32)
                own[chunk, block] = total.astype(bf16)

            for step in range(1, n_first):
                to = lax.rem(at_first + step, n_first)
                if x_first(chunk):
                    device = {"seq": to * 2 + c_at}
                else:
                    device = {"dp": z_at * n_y + to}
                copy = send(
                    own.at[chunk, pl.ds(to * span, span)],
                    first.at[chunk, step - 1, pl.ds(0, span)],
                    one_out.at[chunk, step - 1],
                    one_in.at[chunk, step - 1],
                    device,
                )
                kept[1, chunk, step] = copy
        v_x[x_at] = vector_sum(0, v_copies)
        v_copies = vector_out(1)
        side.wait()
        for turn in range(1, n_x):
            far_copy(0, turn).start()
        for chunk in range(chunks):
            n_first, at_first, n_second, at_second = order(chunk)
            span = n_second * n_z
            for step in range(1, n_first):
                kept[1, chunk, step].wait_recv()
            base = at_first * span

            @pl.loop(0, span)
            def _(block):
                total = own[chunk, base + block].astype(f32)
                for step in range(1, n_first):
                    total = total + first[chunk, step - 1, block].astype(f32)
                own[chunk, base + block] = total.astype(bf16)

            for step in range(1, n_second):
                to = lax.rem(at_second + step, n_second)
                if x_first(chunk):
                    device = {"dp": z_at * n_y + to}
                else:
                    device = {"seq": to * 2 + c_at}
                kept[2, chunk, step] = send(
                    own.at[chunk, pl.ds(base + to * n_z, n_z)],
                    second.at[chunk, step - 1],
                    two_out.at[chunk, step - 1],
                    two_in.at[chunk, step - 1],
                    device,
                )
            if chunk == 0:
                v_y[y_at] = vector_sum(1, v_copies)
                v_copies = vector_out(2)

                @pl.loop(1, near)
                def _(step):
                    near_copy(step).wait()
                    for turn in range(1, n_x):
                        far_copy(step, turn).start()

        v_z[z_at] = vector_sum(2, v_copies)
        v_copies = vector_out(3)
        for chunk in range(chunks):
            n_first, at_first, n_second, at_second = order(chunk)
            for step in range(1, n_second):
                kept[2, chunk, step].wait_recv()
            base = (at_first * n_second + at_second) * n_z

            @pl.loop(0, n_z)
            def _(block):
                total = own[chunk, base + block].astype(f32)
                for step in range(1, n_second):
                    total = total + second[chunk, step - 1, block].astype(f32)
                own[chunk, base + block] = total.astype(bf16)

            for step in range(1, n_z):
                to = lax.rem(z_at + step, n_z)
                kept[3, chunk, step] = send(
                    own.at[chunk, base + to],
                    third.at[chunk, step - 1],
                    three_out.at[chunk, step - 1],
                    three_in.at[chunk, step - 1],
                    {"dp": to * n_y + y_at},
                )
        vec_ref[...] = vector_sum(3, v_copies)
        for chunk in range(chunks):
            n_first, at_first, n_second, at_second = order(chunk)
            for step in range(1, n_z):
                kept[3, chunk, step].wait_recv()
            here = (at_first * n_second + at_second) * n_z + z_at
            total = own[chunk, here].astype(f32)
            for step in range(1, n_z):
                total = total + third[chunk, step - 1].astype(f32)
            own[chunk, here] = total.astype(bf16)
            result = o_ref.at[c_at, x_at, chunk]
            copy = pltpu.make_async_copy(own.at[chunk, here], result, last_own.at[chunk])
            copy.start()
            kept[0, chunk] = copy
            for step in range(1, n_x):
                to = lax.rem(x_at + step, n_x)
                kept[4, chunk, step] = send(
                    own.at[chunk, here],
                    result,
                    x_out.at[chunk, step - 1],
                    x_in.at[chunk, step - 1],
                    {"seq": to * 2 + c_at},
                )
            kept[5, chunk, 0] = send(
                own.at[chunk, here], result, pair_out.at[chunk, 0], pair_in.at[chunk, 0], partner
            )
        for chunk in range(chunks):
            for step in range(1, n_x):
                kept[4, chunk, step].wait_recv()
                origin = lax.rem(x_at + n_x - step, n_x)
                piece = o_ref.at[c_at, origin, chunk]
                kept[5, chunk, step] = send(
                    piece, piece, pair_out.at[chunk, step], pair_in.at[chunk, step], partner
                )

        @pl.loop(0, near)
        def _(step):
            for turn in range(1, n_x):
                far_copy(step, turn).wait()

        for chunk in range(chunks):
            kept[0, chunk].wait()
            for step in range(n_x):
                kept[5, chunk, step].wait()
        for key, copy in kept.items():
            if 1 <= key[0] <= 4:
                copy.wait_send()

    def dma(*shape):
        return pltpu.SemaphoreType.DMA(shape)

    most = n_most * n_z
    return pl.pallas_call(
        body,
        out_shape=(
            jax.ShapeDtypeStruct((2, n_x, chunks, height, width), bf16),
            jax.ShapeDtypeStruct((count,) + given.shape[1:], given.dtype),
            jax.ShapeDtypeStruct(vector.shape, vector.dtype),
        ),
        in_specs=[HBM, HBM, VMEM],
        out_specs=(HBM, HBM, VMEM),
        scratch_shapes=[
            pltpu.VMEM((chunks, blocks, height, width), bf16),
            pltpu.VMEM((chunks, blocks, height, width), bf16),
            pltpu.VMEM((chunks, n_most - 1, most, height, width), bf16),
            pltpu.VMEM((chunks, n_most - 1, n_z, height, width), bf16),
            pltpu.VMEM((chunks, n_z - 1, height, width), bf16),
            pltpu.VMEM((2,) + vector.shape, f32),
            pltpu.VMEM((n_x,) + vector.shape, f32),
            pltpu.VMEM((n_y,) + vector.shape, f32),
            pltpu.VMEM((n_z,) + vector.shape, f32),
            dma(chunks),
            dma(chunks),
            dma(chunks),
            dma(chunks, n_most - 1),
            dma(chunks, n_most - 1),
            dma(chunks, n_most - 1),
            dma(chunks, n_most - 1),
            dma(chunks, n_z - 1),
            dma(chunks, n_z - 1),
            dma(chunks, n_x - 1),
            dma(chunks, n_x - 1),
            dma(chunks, n_x),
            dma(chunks, n_x),
            dma(chunks),
            dma(near),
            dma(near),
            dma(near, n_x - 1),
            dma(near, n_x - 1),
            dma(4, max(n_most, n_z) - 1),
            dma(4, max(n_most, n_z) - 1),
            pltpu.SemaphoreType.DMA,
        ],
        compiler_params=pltpu.CompilerParams(
            collective_id=call_id, has_side_effects=True, vmem_limit_bytes=48 << 20
        ),
    )(grads, given, vector)


def close_half(own, other, names, values, tile):
    half, width = own.shape
    count = names.shape[1]

    def body(own_ref, other_ref, names_ref, values_ref, o_ref, square_ref):
        step = pl.program_id(0)
        row = lax.broadcasted_iota(i32, (tile, count), 0) + step * tile
        where = jnp.where(row == names_ref[...], 1.0, 0.0).astype(bf16)
        total = own_ref[...].astype(f32) + other_ref[...].astype(f32)
        total = total + jnp.dot(where, values_ref[...], preferred_element_type=f32)
        o_ref[...] = total.astype(bf16)

        @pl.when(step == 0)
        def _():
            square_ref[...] = jnp.zeros_like(square_ref)

        square_ref[...] += jnp.sum(total * total, axis=0, keepdims=True)

    rows = pl.BlockSpec((tile, width), lambda step: (step, 0))
    return pl.pallas_call(
        body,
        grid=(half // tile,),
        in_specs=[
            rows,
            rows,
            pl.BlockSpec((1, count), lambda step: (0, 0)),
            pl.BlockSpec((count, width), lambda step: (0, 0)),
        ],
        out_specs=(rows, pl.BlockSpec((1, width), lambda step: (0, 0))),
        out_shape=(jax.ShapeDtypeStruct((half, width), bf16), jax.ShapeDtypeStruct((1, width), f32)),
        compiler_params=pltpu.CompilerParams(vmem_limit_bytes=48 << 20),
    )(own, other, names, values)


def adam_table(core, factor, weight, first, second, mine, other, tile):
    size, width = weight.shape
    turns = mine.shape[0] // tile

    def body(core_ref, factor_ref, w_ref, m_ref, v_ref, mine_ref, other_ref, new_w, new_m, new_v):
        from_mine = pl.program_id(0) // turns == core_ref[0]
        grad = jnp.where(from_mine, mine_ref[...], other_ref[...]).astype(f32) * factor_ref[0]
        new_w[...], new_m[...], new_v[...] = adam_update(
            w_ref[...], grad, m_ref[...], v_ref[...], 0.1, 0.1
        )

    def mine_at(step, core_ref, factor_ref):
        return (jnp.clip(step - core_ref[0] * turns, 0, turns - 1), 0)

    def other_at(step, core_ref, factor_ref):
        return (jnp.clip(step - (1 - core_ref[0]) * turns, 0, turns - 1), 0)

    rows = pl.BlockSpec((tile, width), lambda step, core_ref, factor_ref: (step, 0))
    return pl.pallas_call(
        body,
        grid_spec=pltpu.PrefetchScalarGridSpec(
            num_scalar_prefetch=2,
            grid=(pl.cdiv(size, tile),),
            in_specs=[rows, rows, rows, pl.BlockSpec((tile, width), mine_at), pl.BlockSpec((tile, width), other_at)],
            out_specs=(rows, rows, rows),
        ),
        out_shape=(jax.ShapeDtypeStruct((size, width), f32),) * 3,
        compiler_params=pltpu.CompilerParams(vmem_limit_bytes=56 << 20),
    )(core.reshape(1), factor.reshape(1), weight, first, second, mine, other)


def layer_norm(x, gain, shift):
    centre = x - jnp.mean(x, axis=-1, keepdims=True)
    var = jnp.mean(centre * centre, axis=-1, keepdims=True)
    return centre * lax.rsqrt(var + 1e-05) * gain + shift


def gelu_fn(x):
    return jax.nn.gelu(x, approximate=True)


def adam_update(weight, grad, first, second, rate, decay):
    first_new = beta_one * first + (1.0 - beta_one) * grad
    second_new = beta_two * second + (1.0 - beta_two) * grad * grad
    mhat = first_new / (1.0 - beta_one**STEP)
    vhat = second_new / (1.0 - beta_two**STEP)
    return (
        weight - rate * (mhat / (jnp.sqrt(vhat) + adam_eps) + decay * weight),
        first_new,
        second_new,
    )


def as_rows(flat):
    return jnp.pad(flat, (0, -flat.size % 1024)).reshape(-1, 128)


def on_device(
    clean_ids,
    lengths,
    masked,
    attn_in,
    attn_out,
    mlp_in,
    mlp_out,
    table,
    positions,
    vectors,
    first_attn_in,
    first_attn_out,
    first_mlp_in,
    first_mlp_out,
    first_table,
    first_positions,
    first_vectors,
    second_attn_in,
    second_attn_out,
    second_mlp_in,
    second_mlp_out,
    second_table,
    second_positions,
    second_vectors,
):
    rows, slots = clean_ids.shape
    n_dp = lax.axis_size("dp")
    n_seq = lax.axis_size("seq")
    dp_at = lax.axis_index("dp")
    seq_at = lax.axis_index("seq")
    core = lax.rem(seq_at, 2)
    length = slots * n_seq
    vocab_part, model = table.shape
    vocab = vocab_part * n_dp
    head_dim = model // H
    sharers = max(1, n_seq // rows)
    n_pick = masked.shape[1] // sharers
    row_at = seq_at // sharers
    share = lax.rem(seq_at, sharers)
    tiles = -(-vocab_part // 1056)
    tile = -(-vocab_part // (32 * tiles)) * 16
    half = tiles * tile
    n_x = n_seq // 2
    n_y = 1 << (n_dp.bit_length() - 1) // 2
    n_z = n_dp // n_y

    def piece_of(weight):
        piece = weight.shape[0] // n_seq
        return lax.dynamic_slice_in_dim(weight, seq_at * piece, piece, 0).astype(bf16)

    thin = attn_in.shape[0] // n_seq
    hidden = mlp_in.shape[1]

    def blocks_of(piece):
        return [piece[:, at : at + model] for at in range(0, piece.shape[1], model)]

    pieces = [piece_of(mlp_out), piece_of(positions)]
    for weight in (attn_in, attn_out, mlp_in):
        pieces += blocks_of(piece_of(weight))
    ends = [0]
    for piece in pieces:
        ends.append(ends[-1] + piece.shape[0])
    packed = lax.all_gather(jnp.concatenate(pieces), ("dp", "seq"))

    def unpacked(begin, count):
        parts = [packed[:, ends[at] : ends[at + 1]].reshape(-1, model) for at in range(begin, begin + count)]
        return parts[0] if count == 1 else jnp.concatenate(parts, axis=1)

    w_down = unpacked(0, 1)
    pos_all = unpacked(1, 1)
    w_in = unpacked(2, 3)
    w_out = unpacked(5, 1)
    w_up = unpacked(6, hidden // model)

    all_rows = deliver(clean_ids, ("seq",), 1)
    row_ids = lax.dynamic_index_in_dim(all_rows, row_at, 1, keepdims=False).reshape(length)
    row = dp_at * rows + row_at
    row_length = lax.dynamic_index_in_dim(lengths, row, 0, keepdims=False)
    row_masked = lax.dynamic_index_in_dim(masked, row, 0, keepdims=False)
    picks = lax.dynamic_slice_in_dim(row_masked, share * n_pick, n_pick, 0)
    slot = jnp.arange(length, dtype=i32)
    is_masked = jnp.any(slot[:, None] == row_masked[None, :], axis=1)
    noisy = jnp.where(is_masked, vocab - 1, row_ids)
    targets = jnp.sum(jnp.where(picks[:, None] == slot[None, :], row_ids[None, :], 0), axis=1)
    valid_all = ((masked >= 1) & (masked < lengths[:, None])).astype(f32)
    masked_count = jnp.sum(valid_all)

    owner = noisy // vocab_part
    within = noisy - owner * vocab_part
    owner_half = owner * 2 + (within >= half).astype(i32)
    within_half = jnp.where(within >= half, within - half, within)
    same = noisy[:, None] == noisy[None, :]
    leader = jnp.min(jnp.where(same, slot[None, :], length), axis=1)
    leads = leader == slot
    before = (slot[None, :] < slot[:, None]) & leads[None, :]
    rank = jnp.sum((before & (owner[:, None] == owner[None, :])).astype(i32), axis=1)
    rank_half = jnp.sum((before & (owner_half[:, None] == owner_half[None, :])).astype(i32), axis=1)
    lead_of = leader[:, None] == slot[None, :]
    place = jnp.sum(jnp.where(lead_of, rank[None, :], 0), axis=1)
    place_half = jnp.sum(jnp.where(lead_of, rank_half[None, :], 0), axis=1)

    def asked(owners, ranks, names, count, size, turn):
        spot = jnp.where(ranks // size == turn, owners * size + lax.rem(ranks, size), -1)
        spots = jnp.arange(count * size, dtype=i32)
        listed = leads[None, :] & (spots[:, None] == spot[None, :])
        return spot, jnp.sum(jnp.where(listed, names[None, :], 0), axis=1)

    spot, ask = asked(owner, place, within, n_dp, FETCH, 0)
    spot_half, ask_half = asked(owner_half, place_half, within_half, 2 * n_dp, GIVE, 0)
    turns = jnp.stack([jnp.max(place) // FETCH + 1, jnp.max(place_half) // GIVE + 1])
    pieces = [as_rows(piece) for piece in (ask, ask_half, targets, turns)]
    ends = [0]
    for piece in pieces:
        ends.append(ends[-1] + piece.shape[0])
    told = deliver(jnp.concatenate(pieces), ("dp", "seq"), 2)

    def heard(index, size):
        return told[:, ends[index] : ends[index + 1]].reshape(n_dp * n_seq, -1)[:, :size]

    turns = jnp.max(heard(3, 2), axis=0)
    asks = lax.dynamic_index_in_dim(heard(0, n_dp * FETCH).reshape(n_dp, n_seq, n_dp, FETCH), seq_at, 1, False)
    asks = lax.dynamic_index_in_dim(asks, dp_at, 1, False)
    half_at = dp_at * 2 + core
    asks_half = lax.dynamic_index_in_dim(heard(1, 2 * n_dp * GIVE).reshape(-1, 2 * n_dp, GIVE), half_at, 1, False)
    all_targets = lax.dynamic_index_in_dim(heard(2, n_pick).reshape(n_dp, n_seq, n_pick), seq_at, 1, False)

    def one_hot(spots, count):
        return (spots[:, None] == jnp.arange(count, dtype=i32)[None, :]).astype(bf16)

    found = jnp.take(table, asks, axis=0).astype(bf16)
    fetched = deliver(found, ("dp",), 3, lambda place: place[0]).reshape(n_dp * FETCH, model)
    embedded = jnp.dot(one_hot(spot, n_dp * FETCH), fetched, preferred_element_type=f32)

    def fetch_more(state):
        turn, total = state
        next_spot, next_ask = asked(owner, place, within, n_dp, FETCH, turn)
        wanted = lax.all_to_all(next_ask.reshape(n_dp, FETCH), "dp", 0, 0)
        sent = jnp.take(table, wanted, axis=0).astype(bf16)
        got = lax.all_to_all(sent, "dp", 0, 0).reshape(n_dp * FETCH, model)
        return turn + 1, total + jnp.dot(one_hot(next_spot, n_dp * FETCH), got, preferred_element_type=f32)

    _, embedded = lax.while_loop(lambda state: state[0] < turns[0], fetch_more, (jnp.int32(1), embedded))

    start = embedded + pos_all.astype(f32)
    attn_normed, norm_one_back = jax.vjp(layer_norm, start, vectors[0], vectors[1])
    attn_low = attn_normed.astype(bf16)
    in_bias = jnp.concatenate([vectors[6], jnp.zeros_like(vectors[6]), vectors[7]])
    qkv = (jnp.dot(attn_low, w_in, preferred_element_type=f32) + in_bias).astype(bf16)
    chosen = one_hot(picks - 1, length)
    query = jnp.dot(chosen, qkv[:, :model], preferred_element_type=f32).astype(bf16)
    start_picked = jnp.dot(chosen.astype(f32), start, precision=lax.Precision.HIGHEST)
    q_heads = query.reshape(n_pick, H, head_dim)
    k_heads = qkv[:, model : 2 * model].reshape(length, H, head_dim)
    v_heads = qkv[:, 2 * model :].reshape(length, H, head_dim)
    key_keep = (slot < row_length)[None, None, :]
    raw = jnp.einsum("shd,khd->hsk", q_heads, k_heads, preferred_element_type=f32) * 0.125
    scores = jnp.where(key_keep, raw, mask_fill)
    log_total = jax.nn.logsumexp(scores, axis=-1, keepdims=True)
    probs = jnp.exp(scores - log_total)
    probs_low = probs.astype(bf16)
    mixed = jnp.einsum("hsk,khd->shd", probs_low, v_heads, preferred_element_type=f32)
    mixed = mixed.reshape(n_pick, model).astype(bf16)
    after_attn = start_picked + jnp.dot(mixed, w_out, preferred_element_type=f32) + vectors[8]
    mlp_normed, norm_two_back = jax.vjp(layer_norm, after_attn, vectors[2], vectors[3])
    mlp_low = mlp_normed.astype(bf16)
    up_pre = jnp.dot(mlp_low, w_up, preferred_element_type=f32) + vectors[10:14].reshape(-1)
    activated, gelu_back = jax.vjp(gelu_fn, up_pre)
    act_low = activated.astype(bf16)
    final_in = after_attn + jnp.dot(act_low, w_down, preferred_element_type=f32) + vectors[9]
    final_normed, norm_end_back = jax.vjp(layer_norm, final_in, vectors[4], vectors[5])
    sources = final_normed.astype(bf16)

    table_low = table.astype(bf16)
    heads = deliver(sources, ("dp",), 9).reshape(n_dp * n_pick, model)
    logits = jnp.einsum("nd,vd->nv", heads, table_low, preferred_element_type=f32)
    flat_targets = all_targets.reshape(-1) - dp_at * vocab_part
    rows_here = valid_all.reshape(n_dp, rows, sharers, n_pick)
    rows_here = lax.dynamic_index_in_dim(rows_here, row_at, 1, False)
    flat_valid = lax.dynamic_index_in_dim(rows_here, share, 1, False).reshape(-1)
    hit_mask = flat_targets[:, None] == jnp.arange(vocab_part, dtype=i32)[None, :]
    part_max = jnp.max(logits, axis=1)
    part_sum = jnp.sum(jnp.exp(logits - part_max[:, None]), axis=1)
    part_hit = jnp.sum(jnp.where(hit_mask, logits, 0.0), axis=1)
    stats = jnp.stack([part_max, part_sum, part_hit]).reshape(3, -1, 128)
    stats = deliver(stats, ("dp",), 5).reshape(n_dp, 3, -1)
    top = jnp.max(stats[:, 0], axis=0)
    summed = jnp.sum(stats[:, 1] * jnp.exp(stats[:, 0] - top[None]), axis=0)
    log_norm = top + jnp.log(summed)
    loss_group = jnp.sum(flat_valid * (log_norm - jnp.sum(stats[:, 2], axis=0)))
    logit_grad = (
        (flat_valid / masked_count)[:, None]
        * (jnp.exp(logits - log_norm[:, None]) - hit_mask.astype(f32))
    ).astype(bf16)
    table_grad = jnp.einsum("nv,nd->vd", logit_grad, heads, preferred_element_type=f32)
    table_grad = jnp.pad(table_grad, ((0, 2 * half - vocab_part), (0, 0)))
    half_own = lax.dynamic_slice_in_dim(table_grad, core * half, half, 0)
    half_other = lax.dynamic_slice_in_dim(table_grad, (1 - core) * half, half, 0).astype(bf16)
    logit_grad, half_other = lax.optimization_barrier((logit_grad, half_other))
    half_low = (half_own + from_peer(half_other, "seq", 1, 2, 1).astype(f32)).astype(bf16)
    heads_grad = jnp.dot(logit_grad, table_low, preferred_element_type=f32).astype(bf16)
    heads_grad, half_low = lax.optimization_barrier((heads_grad, half_low))
    if n_x == 2:
        half_across = from_peer(half_low, "seq", 2, 2, 1)
    else:
        groups = [list(range(at, n_seq, 2)) for at in range(2)]
        half_low = jnp.sum(lax.all_gather(half_low, "seq", axis_index_groups=groups).astype(f32), axis=0)
        half_across = jnp.zeros_like(half_low)
    final_grad = heads_grad.reshape(n_dp, n_pick, model)
    final_own = lax.dynamic_index_in_dim(final_grad, dp_at, 0, False).astype(f32)
    for step in range(1, n_dp):
        block = lax.dynamic_index_in_dim(final_grad, lax.rem(dp_at + step, n_dp), 0, False)
        final_own = final_own + from_peer(block, "dp", 1, n_dp, step).astype(f32)
    final_grad = final_own

    final_in_grad, gain_end, shift_end = norm_end_back(final_grad)
    down_grad = final_in_grad.astype(bf16)
    w_down_grad = jnp.einsum("sf,sd->fd", act_low, down_grad, preferred_element_type=f32)
    down_bias = jnp.sum(down_grad.astype(f32), axis=0)
    act_grad = jnp.einsum("sd,fd->sf", down_grad, w_down, preferred_element_type=f32)
    up_grad = gelu_back(act_grad)[0].astype(bf16)
    up_bias = jnp.sum(up_grad.astype(f32), axis=0)
    w_up_grad = jnp.einsum("sd,sf->df", mlp_low, up_grad, preferred_element_type=f32)
    mlp_grad = jnp.einsum("sf,df->sd", up_grad, w_up, preferred_element_type=f32)
    attn_res_grad, gain_two, shift_two = norm_two_back(mlp_grad)
    after_grad = final_in_grad + attn_res_grad
    out_grad = after_grad.astype(bf16)
    out_bias = jnp.sum(out_grad.astype(f32), axis=0)
    w_out_grad = jnp.einsum("se,sd->ed", mixed, out_grad, preferred_element_type=f32)
    mixed_grad = jnp.einsum("sd,ed->se", out_grad, w_out, preferred_element_type=f32).astype(bf16)
    mixed_grad = mixed_grad.reshape(n_pick, H, head_dim)
    prob_grad = jnp.einsum("shd,khd->hsk", mixed_grad, v_heads, preferred_element_type=f32)
    correction = jnp.sum(prob_grad * probs, axis=-1, keepdims=True)
    score_grad = (probs * (prob_grad - correction)).astype(bf16)
    query_grad = jnp.einsum("hsk,khd->shd", score_grad, k_heads, preferred_element_type=f32) * 0.125
    key_grad = jnp.einsum("hsk,shd->khd", score_grad, q_heads, preferred_element_type=f32) * 0.125
    value_grad = jnp.einsum("hsk,shd->khd", probs_low, mixed_grad, preferred_element_type=f32)
    query_grad = query_grad.reshape(n_pick, model).astype(bf16)
    query_full = jnp.einsum("st,sd->td", chosen, query_grad, preferred_element_type=f32).astype(bf16)
    qkv_grad = jnp.concatenate(
        [
            query_full,
            key_grad.reshape(length, model).astype(bf16),
            value_grad.reshape(length, model).astype(bf16),
        ],
        axis=-1,
    )
    qkv_bias = jnp.sum(qkv_grad.astype(f32), axis=0)
    w_in_grad = jnp.einsum("sd,se->de", attn_low, qkv_grad, preferred_element_type=f32)
    normed_grad = jnp.einsum("se,de->sd", qkv_grad, w_in, preferred_element_type=f32)
    start_extra, gain_one, shift_one = norm_one_back(normed_grad)
    after_full = jnp.einsum(
        "st,sd->td", chosen.astype(f32), after_grad, precision=lax.Precision.HIGHEST
    )
    start_grad = after_full + start_extra
    start_grad_low = start_grad.astype(bf16)

    def given(spots):
        summed_ids = jnp.einsum(
            "ts,td->sd", one_hot(spots, 2 * n_dp * GIVE), start_grad_low, preferred_element_type=f32
        )
        return summed_ids.astype(bf16).reshape(2 * n_dp, GIVE, model)

    vec_grad = jnp.concatenate(
        [
            jnp.stack(
                [
                    gain_one,
                    shift_one,
                    gain_two,
                    shift_two,
                    gain_end,
                    shift_end,
                    qkv_bias[:model],
                    qkv_bias[2 * model :],
                    out_bias,
                    down_bias,
                ]
            ),
            up_bias.reshape(-1, model),
            jnp.full((1, model), loss_group),
            jnp.zeros((1, model), f32),
        ],
        axis=0,
    )

    def columns(grad):
        return [part.astype(bf16).reshape(n_dp, -1, model) for part in blocks_of(grad)]

    layer_parts = [w_down_grad, start_grad, w_in_grad, w_out_grad, w_up_grad]
    whole = jnp.concatenate([part for grad in layer_parts for part in columns(grad)], axis=1)
    chunks = 4
    layer_sum, came, vec_total = settle(
        whole.reshape(n_dp, 2, n_x, chunks, -1, model), given(spot_half), vec_grad, n_x, n_y, n_z, 7
    )
    def give_more(state):
        turn, total, _ = state
        next_spot, next_ask = asked(owner_half, place_half, within_half, 2 * n_dp, GIVE, turn)
        names = lax.all_gather(next_ask.reshape(2 * n_dp, GIVE), ("dp", "seq"))
        names = lax.dynamic_index_in_dim(names, half_at, 1, False).reshape(1, -1)
        sent = given(next_spot).reshape(n_dp, 1, 2, GIVE, model)
        sent = jnp.broadcast_to(sent, (n_dp, n_x, 2, GIVE, model)).reshape(-1, GIVE, model)
        got = lax.all_to_all(sent, ("dp", "seq"), 0, 0).reshape(-1, model)
        total, squares = close_half(total, jnp.zeros_like(total), names, got, tile)
        return turn + 1, total, jnp.sum(squares)

    names = asks_half.reshape(1, -1)
    values = came.reshape(-1, model)
    half_own, squares_own = close_half(half_low, half_across, names, values, tile)
    half_square = jnp.sum(squares_own)

    _, half_own, half_square = lax.while_loop(
        lambda state: state[0] < turns[1], give_more, (jnp.int32(1), half_own, half_square)
    )
    layer_sum = layer_sum.reshape(-1, model).astype(f32)
    layer_square = jnp.sum(layer_sum * layer_sum)
    loss_sum = vec_total[14, 0] / n_dp
    vec_total = vec_total[:14]

    def side_by_side(rows_of, count):
        return jnp.concatenate(jnp.split(rows_of, count, axis=0), axis=1)

    ends = [0]
    for grad in layer_parts:
        ends.append(ends[-1] + grad.shape[0] * grad.shape[1] // (model * n_dp))
    g_down, g_pos, g_in, g_out, g_up = [layer_sum[begin:end] for begin, end in zip(ends, ends[1:])]
    g_in = side_by_side(g_in, 3)
    g_up = side_by_side(g_up, hidden // model)
    half_other = from_peer(half_own, "seq", 1, 2, 1)
    said = jnp.full((8, 128), half_square / n_x + layer_square / n_seq)
    square_total = jnp.sum(deliver(said, ("dp", "seq"), 8)[:, 0, 0])
    grad_norm = jnp.sqrt(square_total + jnp.sum(vec_total * vec_total))
    factor = clip_at / jnp.maximum(grad_norm, clip_at)
    weights = (attn_in, attn_out, mlp_in, mlp_out, table, positions, vectors)
    all_grads = (g_in, g_out, g_up, g_down, None, g_pos, vec_total)
    firsts = (
        first_attn_in,
        first_attn_out,
        first_mlp_in,
        first_mlp_out,
        first_table,
        first_positions,
        first_vectors,
    )
    seconds = (
        second_attn_in,
        second_attn_out,
        second_mlp_in,
        second_mlp_out,
        second_table,
        second_positions,
        second_vectors,
    )
    news, moments, squares = ([], [], [])
    for index in range(7):
        rate, decay = (1.0, 0.0) if index == 6 else (0.1, 0.1)
        if index == 4:
            new_w, new_m, new_v = adam_table(
                core, factor, table, first_table, second_table, half_own, half_other, tile
            )
        else:
            new_w, new_m, new_v = adam_update(
                weights[index], all_grads[index] * factor, firsts[index], seconds[index], rate, decay
            )
        news.append(new_w)
        moments.append(new_m)
        squares.append(new_v)
    return (*news, *moments, *squares, loss_sum, masked_count, grad_norm)


def solution(mesh):
    part = P("dp", None)
    six = (part,) * 6 + (P(),)
    return jax.shard_map(
        on_device,
        mesh=mesh,
        in_specs=(P("dp", "seq"), P(), P()) + six * 3,
        out_specs=six * 3 + (P(), P(), P()),
        check_vma=False,
    )
```

```python
import math

import jax
import jax.numpy as jnp
from jax import lax
from jax.experimental import pallas as pl
from jax.experimental.pallas import tpu as pltpu
from jax.sharding import PartitionSpec as P

H = 12
STEP = 10
FETCH = 96
GIVE = 64

mask_fill = -1000000000.0
clip_at = 0.002
beta_one = 0.9
beta_two = 0.999
adam_eps = 1e-08

f32 = jnp.float32
bf16 = jnp.bfloat16
i32 = jnp.int32
HBM = pl.BlockSpec(memory_space=pl.ANY)
VMEM = pl.BlockSpec(memory_space=pltpu.VMEM)
MESH = pl.DeviceIdType.MESH


def deliver(x, axes, call_id, block_of=None):
    sizes = [lax.axis_size(axis) for axis in axes]
    count = math.prod(sizes)
    block = x.shape if block_of is None else x.shape[1:]

    def body(x_ref, o_ref, sent, came, own):
        here = [lax.axis_index(axis) for axis in axes]

        def flat(place):
            index = place[0]
            for size, along in zip(sizes[1:], place[1:]):
                index = index * size + along
            return index

        def peer(step):
            place = []
            for size, at in zip(reversed(sizes), reversed(here)):
                place.append(lax.rem(at + lax.rem(step, size), size))
                step = step // size
            return place[::-1]

        def source(place):
            return x_ref if block_of is None else x_ref.at[block_of(place)]

        mine = flat(here)

        def copy(step):
            place = peer(step)
            return pltpu.make_async_remote_copy(
                source(place),
                o_ref.at[mine],
                sent.at[step],
                came.at[step],
                device_id=dict(zip(axes, place)),
                device_id_type=MESH,
            )

        barrier = pltpu.get_barrier_semaphore()

        @pl.loop(1, count)
        def _(step):
            pl.semaphore_signal(
                barrier, inc=1, device_id=dict(zip(axes, peer(step))), device_id_type=MESH
            )

        local = pltpu.make_async_copy(source(here), o_ref.at[mine], own)
        local.start()
        pl.semaphore_wait(barrier, count - 1)

        @pl.loop(1, count)
        def _(step):
            copy(step).start()

        local.wait()

        @pl.loop(1, count)
        def _(step):
            copy(step).wait()

    return pl.pallas_call(
        body,
        out_shape=jax.ShapeDtypeStruct((count,) + block, x.dtype),
        in_specs=[HBM],
        out_specs=HBM,
        scratch_shapes=[
            pltpu.SemaphoreType.DMA((count,)),
            pltpu.SemaphoreType.DMA((count,)),
            pltpu.SemaphoreType.DMA,
        ],
        compiler_params=pltpu.CompilerParams(collective_id=call_id, has_side_effects=True),
    )(x)


def from_peer(x, axis, span, size, step):
    pairs = []
    for at in range(lax.axis_size(axis)):
        digit = at // span % size
        pairs.append((at, at + ((digit + step) % size - digit) * span))
    return lax.ppermute(x, axis, pairs)


def group_sum(x, dim, axis, span):
    size = x.shape[dim]
    at = lax.rem(lax.axis_index(axis) // span, size)
    total = lax.dynamic_index_in_dim(x, at, dim, False).astype(f32)
    for step in range(1, size):
        block = lax.dynamic_index_in_dim(x, lax.rem(at + step, size), dim, False)
        total = total + from_peer(block, axis, span, size, step).astype(f32)
    return total.astype(bf16)


def group_join(x, dim, axis, span, size):
    at = lax.rem(lax.axis_index(axis) // span, size)
    parts = [x] + [from_peer(x, axis, span, size, size - step) for step in range(1, size)]
    if size == 2:
        first = jnp.where(at == 0, parts[0], parts[1])
        second = jnp.where(at == 0, parts[1], parts[0])
        return jnp.stack([first, second], axis=dim)
    turned = jnp.stack(parts + parts, axis=dim)
    return lax.dynamic_slice_in_dim(turned, size - at, size, dim)


def settle(grads, given, vector, n_x, n_y, n_z, call_id):
    n_dp, _, _, chunks, height, width = grads.shape
    n_seq = 2 * n_x
    count = n_dp * n_seq
    near = n_dp * 2
    n_most = max(n_x, n_y)
    blocks = n_x * n_y * n_z

    def body(g_ref, e_ref, v_ref, o_ref, came_ref, vec_ref, *scratch):
        own, got, first, second, third = scratch[:5]
        v_core, v_x, v_y, v_z = scratch[5:9]
        core_out, core_in, core_own = scratch[9:12]
        one_out, one_in, two_out, two_in, three_out, three_in = scratch[12:18]
        last_own, e_out, e_in, far_out, far_in, v_out, v_in, side_own = scratch[18:]
        dp_at, seq_at = lax.axis_index("dp"), lax.axis_index("seq")
        x_at, c_at = seq_at // 2, lax.rem(seq_at, 2)
        z_at, y_at = dp_at // n_y, lax.rem(dp_at, n_y)
        partner = {"seq": x_at * 2 + 1 - c_at}

        def send(source, target, out_sem, in_sem, device):
            copy = pltpu.make_async_remote_copy(
                source, target, out_sem, in_sem, device_id=device, device_id_type=MESH
            )
            copy.start()
            return copy

        barrier = pltpu.get_barrier_semaphore()

        @pl.loop(1, count)
        def _(step):
            seq_to = lax.rem(seq_at + lax.rem(step, n_seq), n_seq)
            peer = {"dp": lax.rem(dp_at + step // n_seq, n_dp), "seq": seq_to}
            pl.semaphore_signal(barrier, inc=1, device_id=peer, device_id_type=MESH)

        def x_first(chunk):
            return chunk % 2 == 0

        def order(chunk):
            return (n_x, x_at, n_y, y_at) if x_first(chunk) else (n_y, y_at, n_x, x_at)

        def places(chunk, block):
            z, y, x = block // (n_y * n_x), lax.rem(block // n_x, n_y), lax.rem(block, n_x)
            at = (x * n_y + y) * n_z + z if x_first(chunk) else (y * n_x + x) * n_z + z
            return z * n_y + y, x, at

        for chunk in range(chunks):

            @pl.loop(0, blocks)
            def _(block):
                owner, x, at = places(chunk, block)
                source = g_ref.at[owner, c_at, x, chunk]
                pltpu.make_async_copy(source, own.at[chunk, at], core_own.at[chunk]).start()

        v_core[c_at] = v_ref[...]
        mine = came_ref.at[dp_at * n_seq + seq_at]
        side = pltpu.make_async_copy(e_ref.at[dp_at * 2 + c_at], mine, side_own)
        side.start()
        pl.semaphore_wait(barrier, count - 1)
        for chunk in range(chunks):

            @pl.loop(0, blocks)
            def _(block):
                owner, x, at = places(chunk, block)
                source = g_ref.at[owner, 1 - c_at, x, chunk]
                send(source, got.at[chunk, at], core_out.at[chunk], core_in.at[chunk], partner)

        v_turn = [
            (v_core, c_at, 2, lambda to: {"seq": x_at * 2 + to}),
            (v_x, x_at, n_x, lambda to: {"seq": to * 2 + c_at}),
            (v_y, y_at, n_y, lambda to: {"dp": z_at * n_y + to}),
            (v_z, z_at, n_z, lambda to: {"dp": to * n_y + y_at}),
        ]

        def vector_out(turn):
            buffer, at, size, device = v_turn[turn]
            return [
                send(
                    buffer.at[at],
                    buffer.at[at],
                    v_out.at[turn, step - 1],
                    v_in.at[turn, step - 1],
                    device(lax.rem(at + step, size)),
                )
                for step in range(1, size)
            ]

        def vector_sum(turn, copies):
            buffer, _, size, _ = v_turn[turn]
            for copy in copies:
                copy.wait()
            total = buffer[0]
            for place in range(1, size):
                total = total + buffer[place]
            return total

        v_copies = vector_out(0)

        def near_copy(step):
            owner = lax.rem(dp_at + step // 2, n_dp)
            core = lax.rem(c_at + lax.rem(step, 2), 2)
            return pltpu.make_async_remote_copy(
                e_ref.at[owner * 2 + core],
                mine,
                e_out.at[step],
                e_in.at[step],
                device_id={"dp": owner, "seq": x_at * 2 + core},
                device_id_type=MESH,
            )

        def far_copy(step, turn):
            origin = lax.rem(dp_at + n_dp - step // 2, n_dp)
            core = lax.rem(c_at + lax.rem(step, 2), 2)
            block = came_ref.at[origin * n_seq + x_at * 2 + core]
            to = lax.rem(x_at + turn, n_x) * 2 + c_at
            return pltpu.make_async_remote_copy(
                block,
                block,
                far_out.at[step, turn - 1],
                far_in.at[step, turn - 1],
                device_id={"seq": to},
                device_id_type=MESH,
            )

        @pl.loop(1, near)
        def _(step):
            near_copy(step).start()

        kept = {}
        for chunk in range(chunks):
            n_first, at_first, n_second, at_second = order(chunk)
            span = n_second * n_z
            whole = own.at[chunk]
            pltpu.make_async_copy(whole, whole, core_own.at[chunk]).wait()
            pltpu.make_async_remote_copy(
                whole, whole, core_out.at[chunk], core_in.at[chunk], device_id=partner, device_id_type=MESH
            ).wait()

            @pl.loop(0, blocks)
            def _(block):
                total = own[chunk, block].astype(f32) + got[chunk, block].astype(f32)
                own[chunk, block] = total.astype(bf16)

            for step in range(1, n_first):
                to = lax.rem(at_first + step, n_first)
                if x_first(chunk):
                    device = {"seq": to * 2 + c_at}
                else:
                    device = {"dp": z_at * n_y + to}
                copy = send(
                    own.at[chunk, pl.ds(to * span, span)],
                    first.at[chunk, step - 1, pl.ds(0, span)],
                    one_out.at[chunk, step - 1],
                    one_in.at[chunk, step - 1],
                    device,
                )
                kept[1, chunk, step] = copy
        v_x[x_at] = vector_sum(0, v_copies)
        v_copies = vector_out(1)
        side.wait()
        for turn in range(1, n_x):
            far_copy(0, turn).start()
        for chunk in range(chunks):
            n_first, at_first, n_second, at_second = order(chunk)
            span = n_second * n_z
            for step in range(1, n_first):
                kept[1, chunk, step].wait_recv()
            base = at_first * span

            @pl.loop(0, span)
            def _(block):
                total = own[chunk, base + block].astype(f32)
                for step in range(1, n_first):
                    total = total + first[chunk, step - 1, block].astype(f32)
                own[chunk, base + block] = total.astype(bf16)

            for step in range(1, n_second):
                to = lax.rem(at_second + step, n_second)
                if x_first(chunk):
                    device = {"dp": z_at * n_y + to}
                else:
                    device = {"seq": to * 2 + c_at}
                kept[2, chunk, step] = send(
                    own.at[chunk, pl.ds(base + to * n_z, n_z)],
                    second.at[chunk, step - 1],
                    two_out.at[chunk, step - 1],
                    two_in.at[chunk, step - 1],
                    device,
                )
            if chunk == 0:
                v_y[y_at] = vector_sum(1, v_copies)
                v_copies = vector_out(2)

                @pl.loop(1, near)
                def _(step):
                    near_copy(step).wait()
                    for turn in range(1, n_x):
                        far_copy(step, turn).start()

        v_z[z_at] = vector_sum(2, v_copies)
        v_copies = vector_out(3)
        for chunk in range(chunks):
            n_first, at_first, n_second, at_second = order(chunk)
            for step in range(1, n_second):
                kept[2, chunk, step].wait_recv()
            base = (at_first * n_second + at_second) * n_z

            @pl.loop(0, n_z)
            def _(block):
                total = own[chunk, base + block].astype(f32)
                for step in range(1, n_second):
                    total = total + second[chunk, step - 1, block].astype(f32)
                own[chunk, base + block] = total.astype(bf16)

            for step in range(1, n_z):
                to = lax.rem(z_at + step, n_z)
                kept[3, chunk, step] = send(
                    own.at[chunk, base + to],
                    third.at[chunk, step - 1],
                    three_out.at[chunk, step - 1],
                    three_in.at[chunk, step - 1],
                    {"dp": to * n_y + y_at},
                )
        vec_ref[...] = vector_sum(3, v_copies)
        for chunk in range(chunks):
            n_first, at_first, n_second, at_second = order(chunk)
            for step in range(1, n_z):
                kept[3, chunk, step].wait_recv()
            here = (at_first * n_second + at_second) * n_z + z_at
            total = own[chunk, here].astype(f32)
            for step in range(1, n_z):
                total = total + third[chunk, step - 1].astype(f32)
            own[chunk, here] = total.astype(bf16)
            copy = pltpu.make_async_copy(own.at[chunk, here], o_ref.at[chunk], last_own.at[chunk])
            copy.start()
            kept[0, chunk] = copy

        @pl.loop(0, near)
        def _(step):
            for turn in range(1, n_x):
                far_copy(step, turn).wait()

        for chunk in range(chunks):
            kept[0, chunk].wait()
        for key, copy in kept.items():
            if key[0] > 0:
                copy.wait_send()

    def dma(*shape):
        return pltpu.SemaphoreType.DMA(shape)

    most = n_most * n_z
    return pl.pallas_call(
        body,
        out_shape=(
            jax.ShapeDtypeStruct((chunks, height, width), bf16),
            jax.ShapeDtypeStruct((count,) + given.shape[1:], given.dtype),
            jax.ShapeDtypeStruct(vector.shape, vector.dtype),
        ),
        in_specs=[HBM, HBM, VMEM],
        out_specs=(HBM, HBM, VMEM),
        scratch_shapes=[
            pltpu.VMEM((chunks, blocks, height, width), bf16),
            pltpu.VMEM((chunks, blocks, height, width), bf16),
            pltpu.VMEM((chunks, n_most - 1, most, height, width), bf16),
            pltpu.VMEM((chunks, n_most - 1, n_z, height, width), bf16),
            pltpu.VMEM((chunks, n_z - 1, height, width), bf16),
            pltpu.VMEM((2,) + vector.shape, f32),
            pltpu.VMEM((n_x,) + vector.shape, f32),
            pltpu.VMEM((n_y,) + vector.shape, f32),
            pltpu.VMEM((n_z,) + vector.shape, f32),
            dma(chunks),
            dma(chunks),
            dma(chunks),
            dma(chunks, n_most - 1),
            dma(chunks, n_most - 1),
            dma(chunks, n_most - 1),
            dma(chunks, n_most - 1),
            dma(chunks, n_z - 1),
            dma(chunks, n_z - 1),
            dma(chunks),
            dma(near),
            dma(near),
            dma(near, n_x - 1),
            dma(near, n_x - 1),
            dma(4, max(n_most, n_z) - 1),
            dma(4, max(n_most, n_z) - 1),
            pltpu.SemaphoreType.DMA,
        ],
        compiler_params=pltpu.CompilerParams(
            collective_id=call_id, has_side_effects=True, vmem_limit_bytes=48 << 20
        ),
    )(grads, given, vector)


def read_heads(source, table_low, targets, vocab_part, chunk, n_y, n_z, call_id):
    n_pick, width = source.shape
    size = table_low.shape[0]
    n_dp = n_y * n_z
    chunks = size // chunk

    def body(s_ref, t_ref, target_ref, e_ref, h_ref, m_ref, stat_ref, e_buf, h_buf, t_buf, told, came, *sems):
        z_out, z_in, y_out, y_in, stat_out, stat_in, e_sem, load_sem, h_sem = sems
        dp_at = lax.axis_index("dp")
        z_at, y_at = dp_at // n_y, lax.rem(dp_at, n_y)
        load = pltpu.make_async_copy(t_ref, t_buf, load_sem)
        load.start()
        h_buf[dp_at] = s_ref[...]
        barrier = pltpu.get_barrier_semaphore()

        @pl.loop(1, n_dp)
        def _(step):
            to = lax.rem(dp_at + step, n_dp)
            pl.semaphore_signal(barrier, inc=1, device_id={"dp": to}, device_id_type=MESH)

        pl.semaphore_wait(barrier, n_dp - 1)

        def z_copy(step):
            mine = h_buf.at[dp_at]
            to = lax.rem(z_at + step, n_z) * n_y + y_at
            return pltpu.make_async_remote_copy(
                mine, mine, z_out.at[step], z_in.at[step], device_id={"dp": to}, device_id_type=MESH
            )

        def y_copy(turn, step):
            block = h_buf.at[lax.rem(z_at + n_z - turn, n_z) * n_y + y_at]
            to = z_at * n_y + lax.rem(y_at + step, n_y)
            return pltpu.make_async_remote_copy(
                block,
                block,
                y_out.at[turn, step],
                y_in.at[turn, step],
                device_id={"dp": to},
                device_id_type=MESH,
            )

        for step in range(1, n_y):
            y_copy(0, step).start()
        for step in range(1, n_z):
            z_copy(step).start()
        load.wait()

        def logits(rows, index):
            part = t_buf[index * chunk : (index + 1) * chunk]
            return lax.dot_general(part, rows, (((1,), (1,)), ((), ())), preferred_element_type=f32)

        @pl.loop(0, n_dp)
        def _(turn):
            z_turn, y_turn = turn // n_y, lax.rem(turn, n_y)

            @pl.when((y_turn == 0) & (z_turn > 0))
            def _():
                z_copy(z_turn).wait_recv()
                for step in range(1, n_y):
                    y_copy(z_turn, step).start()

            @pl.when(y_turn > 0)
            def _():
                y_copy(z_turn, y_turn).wait_recv()

            origin = lax.rem(z_at + n_z - z_turn, n_z) * n_y + lax.rem(y_at + n_y - y_turn, n_y)
            rows = h_buf[origin]
            target = target_ref[origin]
            row = lax.broadcasted_iota(i32, (chunk // 8, 8, n_pick), 0) * 8
            row = row + lax.broadcasted_iota(i32, (chunk // 8, 8, n_pick), 1)
            top = summed = hit = None
            ahead = logits(rows, 0)
            for index in range(chunks):
                now = ahead.reshape(chunk // 8, 8, n_pick)
                if index + 1 < chunks:
                    ahead = logits(rows, index + 1)
                first = index * chunk
                if first + chunk > vocab_part:
                    now = jnp.where(row < vocab_part - first, now, -jnp.inf)
                chunk_top = jnp.max(now, axis=0)
                new_top = chunk_top if top is None else jnp.maximum(top, chunk_top)
                grown = jnp.exp(now - new_top[None])
                chunk_sum = jnp.sum(grown, axis=0)
                chunk_hit = jnp.sum(jnp.where(row == (target - first)[None], now, 0.0), axis=0)
                if top is None:
                    summed, hit = chunk_sum, chunk_hit
                else:
                    summed = summed * jnp.exp(top - new_top) + chunk_sum
                    hit = hit + chunk_hit
                top = new_top
                e_buf[origin, first : first + chunk] = grown.reshape(chunk, n_pick).astype(bf16)
                m_ref[origin, index] = top
            best = jnp.max(top, axis=0, keepdims=True)
            told[origin] = jnp.zeros((8, n_pick), f32)
            told[origin, 0:1] = best
            told[origin, 1:2] = jnp.sum(summed * jnp.exp(top - best), axis=0, keepdims=True)
            told[origin, 2:3] = jnp.sum(hit, axis=0, keepdims=True)
            pltpu.make_async_copy(e_buf.at[origin], e_ref.at[origin], e_sem.at[origin]).start()

        def stat_copy(step):
            to = lax.rem(dp_at + step, n_dp)
            return pltpu.make_async_remote_copy(
                told,
                came.at[dp_at],
                stat_out.at[step],
                stat_in.at[step],
                device_id={"dp": to},
                device_id_type=MESH,
            )

        @pl.loop(1, n_dp)
        def _(step):
            stat_copy(step).start()

        came[dp_at] = told[...]
        keep = pltpu.make_async_copy(h_buf, h_ref, h_sem)
        keep.start()
        for step in range(1, n_z):
            z_copy(step).wait_send()
        for turn in range(n_z):
            for step in range(1, n_y):
                y_copy(turn, step).wait_send()

        @pl.loop(0, n_dp)
        def _(origin):
            pltpu.make_async_copy(e_buf.at[origin], e_ref.at[origin], e_sem.at[origin]).wait()

        @pl.loop(1, n_dp)
        def _(step):
            stat_copy(step).wait()

        keep.wait()
        stat_ref[...] = came[...]

    def dma(*shape):
        return pltpu.SemaphoreType.DMA(shape)

    return pl.pallas_call(
        body,
        out_shape=(
            jax.ShapeDtypeStruct((n_dp, size, n_pick), bf16),
            jax.ShapeDtypeStruct((n_dp, n_pick, width), bf16),
            jax.ShapeDtypeStruct((n_dp, chunks, 8, n_pick), f32),
            jax.ShapeDtypeStruct((n_dp, n_dp, 8, n_pick), f32),
        ),
        in_specs=[VMEM, HBM, VMEM],
        out_specs=(HBM, HBM, VMEM, VMEM),
        scratch_shapes=[
            pltpu.VMEM((n_dp, size, n_pick), bf16),
            pltpu.VMEM((n_dp, n_pick, width), bf16),
            pltpu.VMEM((size, width), bf16),
            pltpu.VMEM((n_dp, 8, n_pick), f32),
            pltpu.VMEM((n_dp, n_dp, 8, n_pick), f32),
            dma(n_z),
            dma(n_z),
            dma(n_z, n_y),
            dma(n_z, n_y),
            dma(n_dp),
            dma(n_dp),
            dma(n_dp),
            pltpu.SemaphoreType.DMA,
            pltpu.SemaphoreType.DMA,
        ],
        compiler_params=pltpu.CompilerParams(
            collective_id=call_id, has_side_effects=True, vmem_limit_bytes=56 << 20
        ),
    )(source, table_low, targets)


def write_heads(grown, heads, turned, tops, stats, targets, weights, chunk, call_id):
    n_dp, size, n_pick = grown.shape
    width = heads.shape[2]
    chunks = size // chunk
    turns = chunks // 2

    def body(e_ref, h_ref, t_ref, m_ref, stat_ref, target_ref, w_ref, d_ref, half_ref, log_ref, *scratch):
        buf, t_buf, df_buf, out_buf, got, res = scratch[:6]
        e_sem, t_sem, df_out, df_in, df_own, pair_out, pair_in, res_sem = scratch[6:]
        dp_at, seq_at = lax.axis_index("dp"), lax.axis_index("seq")
        core = lax.rem(seq_at, 2)
        partner = {"seq": seq_at + 1 - 2 * core}
        load = pltpu.make_async_copy(t_ref, t_buf, t_sem)

        def e_copy(turn):
            origin = lax.rem(dp_at + 1 + turn, n_dp)
            return pltpu.make_async_copy(e_ref.at[origin], buf.at[origin], e_sem.at[turn])

        e_copy(0).start()
        load.start()

        @pl.loop(1, n_dp)
        def _(turn):
            e_copy(turn).start()

        barrier = pltpu.get_barrier_semaphore()

        @pl.loop(1, n_dp)
        def _(step):
            to = lax.rem(dp_at + step, n_dp)
            pl.semaphore_signal(barrier, inc=1, device_id={"dp": to}, device_id_type=MESH)

        pl.semaphore_signal(barrier, inc=1, device_id=partner, device_id_type=MESH)

        @pl.loop(0, n_dp)
        def _(origin):
            top = stat_ref[0, origin, 0:1]
            for sender in range(1, n_dp):
                top = jnp.maximum(top, stat_ref[sender, origin, 0:1])
            total = jnp.zeros((1, n_pick), f32)
            hit = jnp.zeros((1, n_pick), f32)
            for sender in range(n_dp):
                total = total + stat_ref[sender, origin, 1:2] * jnp.exp(stat_ref[sender, origin, 0:1] - top)
                hit = hit + stat_ref[sender, origin, 2:3]
            log_ref[0, origin] = top + jnp.log(total)
            log_ref[1, origin] = hit

        load.wait()
        pl.semaphore_wait(barrier, n_dp)

        def df_copy(turn):
            to = lax.rem(dp_at + 1 + turn, n_dp)
            return pltpu.make_async_remote_copy(
                df_buf.at[to],
                d_ref.at[dp_at],
                df_out.at[turn],
                df_in.at[turn],
                device_id={"dp": to},
                device_id_type=MESH,
            )

        @pl.loop(0, n_dp)
        def _(turn):
            origin = lax.rem(dp_at + 1 + turn, n_dp)
            e_copy(turn).wait()
            log_total = log_ref[0, origin]
            weight = w_ref[origin]
            target = target_ref[origin]
            row = lax.broadcasted_iota(i32, (chunk // 8, 8, n_pick), 0) * 8
            row = row + lax.broadcasted_iota(i32, (chunk // 8, 8, n_pick), 1)

            def gradient(index):
                rows = pl.ds(index * chunk, chunk)
                scale = jnp.exp(m_ref[origin, index] - log_total) * weight
                part = buf[origin, rows].astype(f32).reshape(chunk // 8, 8, n_pick) * scale[None]
                at_target = row == (target - index * chunk)[None]
                part = part - jnp.where(at_target, weight[None], 0.0)
                part = part.reshape(chunk, n_pick).astype(bf16)
                buf[origin, rows] = part
                return part

            total = None
            ahead = gradient(0)
            for index in range(chunks):
                now = ahead
                if index + 1 < chunks:
                    ahead = gradient(index + 1)
                columns = t_buf[:, index * chunk : (index + 1) * chunk]
                part = jnp.dot(columns, now, preferred_element_type=f32)
                total = part if total is None else total + part
            df_buf[origin] = total.astype(bf16)

            @pl.when(turn < n_dp - 1)
            def _():
                df_copy(turn).start()

        local = pltpu.make_async_copy(df_buf.at[dp_at], d_ref.at[dp_at], df_own)
        local.start()

        def table_part(index):
            first = pl.multiple_of(index * chunk, chunk)
            part = jnp.concatenate([buf[origin, pl.ds(first, chunk)] for origin in range(n_dp)], axis=1)
            return jnp.dot(part, h_ref[...], preferred_element_type=f32)

        def pair_copy(turn):
            return pltpu.make_async_remote_copy(
                out_buf.at[turn],
                got.at[turn],
                pair_out.at[turn],
                pair_in.at[turn],
                device_id=partner,
                device_id_type=MESH,
            )

        @pl.loop(0, turns)
        def _(turn):
            out_buf[turn] = table_part((1 - core) * turns + turn).astype(bf16)
            pair_copy(turn).start()

        def res_copy(turn):
            return pltpu.make_async_copy(res.at[turn], half_ref.at[turn], res_sem.at[turn])

        @pl.loop(0, turns)
        def _(turn):
            total = table_part(core * turns + turn)
            pair_copy(turn).wait()
            res[turn] = (total + got[turn].astype(f32)).astype(bf16)
            res_copy(turn).start()

        @pl.loop(0, turns)
        def _(turn):
            res_copy(turn).wait()

        local.wait()

        @pl.loop(0, n_dp - 1)
        def _(turn):
            df_copy(turn).wait()

    def dma(*shape):
        return pltpu.SemaphoreType.DMA(shape)

    return pl.pallas_call(
        body,
        out_shape=(
            jax.ShapeDtypeStruct((n_dp, width, n_pick), bf16),
            jax.ShapeDtypeStruct((turns, chunk, width), bf16),
            jax.ShapeDtypeStruct((2, n_dp, 1, n_pick), f32),
        ),
        in_specs=[HBM, VMEM, HBM, VMEM, VMEM, VMEM, VMEM],
        out_specs=(HBM, HBM, VMEM),
        scratch_shapes=[
            pltpu.VMEM((n_dp, size, n_pick), bf16),
            pltpu.VMEM((width, size), bf16),
            pltpu.VMEM((n_dp, width, n_pick), bf16),
            pltpu.VMEM((turns, chunk, width), bf16),
            pltpu.VMEM((turns, chunk, width), bf16),
            pltpu.VMEM((turns, chunk, width), bf16),
            dma(n_dp),
            pltpu.SemaphoreType.DMA,
            dma(n_dp),
            dma(n_dp),
            pltpu.SemaphoreType.DMA,
            dma(turns),
            dma(turns),
            dma(turns),
        ],
        compiler_params=pltpu.CompilerParams(
            collective_id=call_id, has_side_effects=True, vmem_limit_bytes=62 << 20
        ),
    )(grown, heads.reshape(n_dp * n_pick, width), turned, tops, stats, targets, weights)


def staged(work, ins, small, outs, temps, limit, buffers_of=(), pieces=None, eager=2):
    n_in, n_small, n_out = len(ins), len(small), len(outs)
    packed, places = ((), {}) if pieces is None else ((pieces[0],), pieces[1])

    def body(*refs):
        packed_refs, refs = refs[: len(packed)], refs[len(packed) :]
        in_refs, small_refs, refs = refs[:n_in], refs[n_in : n_in + n_small], refs[n_in + n_small :]
        out_refs, in_bufs, refs = refs[:n_out], refs[n_out : n_out + n_in], refs[n_out + n_in :]
        out_bufs, (in_sem, out_sem), temp_refs = refs[:n_out], refs[n_out : n_out + 2], refs[n_out + 2 :]
        loads = {}
        names = list(ins)

        def start(at):
            name = names[at]
            loads[name] = pltpu.make_async_copy(in_refs[at], in_bufs[at], in_sem.at[at])
            if name not in places:
                loads[name].start()
                return
            loads[name] = pltpu.make_async_copy(in_bufs[at], in_bufs[at], in_sem.at[at])
            for source, target in places[name]:
                pltpu.make_async_copy(
                    packed_refs[0].at[source], in_bufs[at].at[target], in_sem.at[at]
                ).start()

        for at in range(eager):
            start(at)
        buffers = dict(zip(ins, in_bufs))
        pending, sent = list(ins), []

        def get(name):
            if name in pending:
                pending.remove(name)
                loads[name].wait()
                if name == names[eager - 1]:
                    for at in range(eager, n_in):
                        start(at)
            return buffers[name]

        def put(name, begin=0, count=None):
            at = list(outs).index(name)
            source, target = out_bufs[at], out_refs[at]
            if count is not None:
                source, target = source.at[:, pl.ds(0, count)], target.at[:, pl.ds(begin, count)]
            copy = pltpu.make_async_copy(source, target, out_sem.at[len(sent)])
            copy.start()
            sent.append(copy)
            return copy

        def done(copy):
            copy.wait()
            sent[sent.index(copy)] = None

        work(get, dict(zip(small, small_refs)), dict(zip(outs, out_bufs)), (put, done), temp_refs)
        for name in list(pending):
            get(name)
        for copy in sent:
            if copy is not None:
                copy.wait()

    def scratch(value):
        return pltpu.VMEM(value.shape, value.dtype)

    def refs_of(name, value):
        return jnp.zeros((8, 128), value.dtype) if name in places else value

    return pl.pallas_call(
        body,
        out_shape=tuple(outs.values()),
        in_specs=[HBM] * (len(packed) + n_in) + [VMEM] * n_small,
        out_specs=(HBM,) * n_out,
        scratch_shapes=[scratch(value) for value in ins.values()]
        + [scratch(dict(buffers_of).get(name, value)) for name, value in outs.items()]
        + [pltpu.SemaphoreType.DMA((n_in,)), pltpu.SemaphoreType.DMA((n_out + 2,))]
        + temps,
        compiler_params=pltpu.CompilerParams(vmem_limit_bytes=limit << 20),
        cost_estimate=pl.CostEstimate(flops=0, bytes_accessed=0, transcendentals=0),
    )(*packed, *[refs_of(name, value) for name, value in ins.items()], *small.values())


def dot(left, right, left_dim=1, right_dim=0):
    return lax.dot_general(
        left, right, (((left_dim,), (right_dim,)), ((), ())), preferred_element_type=f32
    )


def norm_parts(x):
    centre = x - jnp.mean(x, axis=-1, keepdims=True)
    scale = lax.rsqrt(jnp.mean(centre * centre, axis=-1, keepdims=True) + 1e-05)
    return centre * scale, scale


def norm_back(x, gain, grad):
    unit, scale = norm_parts(x)
    d_gain = jnp.sum(grad * unit, axis=0, keepdims=True)
    d_shift = jnp.sum(grad, axis=0, keepdims=True)
    inner = grad * gain
    pull = jnp.mean(inner, axis=-1, keepdims=True)
    pull = pull + unit * jnp.mean(inner * unit, axis=-1, keepdims=True)
    return scale * (inner - pull), d_gain, d_shift


def iota(shape, dim):
    return lax.broadcasted_iota(i32, shape, dim)


def flat(ref, columns=slice(None)):
    value = ref[..., columns]
    return value.reshape(-1, value.shape[-1])


def row_block(ref, block, size):
    first = block * size
    if len(ref.shape) == 2:
        return ref[first : first + size]
    _, inner, rows, _ = ref.shape
    if inner * rows <= size:
        per = inner * rows
        return flat(ref[first // per : (first + size) // per])
    owner, first = divmod(first, inner * rows)
    return flat(ref[owner, first // rows : (first + size) // rows])


def split_three(x):
    high = x.astype(bf16)
    rest = x - high.astype(f32)
    middle = rest.astype(bf16)
    return high, middle, (rest - middle.astype(f32)).astype(bf16)


def layer_forward(embedded, pos, w_in, w_out, w_up, w_down, vectors, picks, row_length, pieces):
    length, model = embedded.shape
    n_pick = picks.shape[0]
    lanes = 128
    groups = model // lanes
    head_dim = model // H
    per = lanes // head_dim

    def work(get, small, out, moves, temps):
        put, _ = moves
        vec = small["vectors"]
        v_turned, o_turned = temps
        emb, pos_rows = get("emb"), get("pos")
        start = emb[...].astype(f32) + flat(pos_rows).astype(f32)
        unit, _ = norm_parts(start)
        out["a"][...] = (unit * vec[0:1] + vec[1:2]).astype(bf16)
        put("a")
        chosen = jnp.where(small["pick_col"][...] - 1 == iota((n_pick, length), 1), 1.0, 0.0).astype(bf16)
        start_picked = dot(chosen, emb[...]) + dot(chosen, flat(pos_rows))
        w = get("w_in")
        out["k"][...] = dot(out["a"][...], flat(w, slice(model, 2 * model))).astype(bf16)
        put("k")
        out["v"][...] = (dot(out["a"][...], flat(w, slice(2 * model, 3 * model))) + vec[7:8]).astype(bf16)
        put("v")
        a_picked = dot(chosen, out["a"][...]).astype(bf16)
        out["q"][...] = (dot(a_picked, flat(w, slice(0, model))) + vec[6:7]).astype(bf16)
        put("q")
        keep = iota((length, n_pick), 0) < small["length"][0, 0]

        @pl.loop(0, groups)
        def _(group):
            place = pl.ds(pl.multiple_of(group * lanes, lanes), lanes)
            v_turned[...] = out["v"][:, place].T
            q_pair, k_pair = out["q"][:, place], out["k"][:, place]
            mixed = None
            for j in range(per):
                q_head = jnp.where(iota((n_pick, lanes), 1) // head_dim == j, q_pair, jnp.zeros_like(q_pair))
                score = jnp.where(keep, dot(k_pair, q_head, 1, 1) * 0.125, mask_fill)
                top = jnp.max(score, axis=0, keepdims=True)
                grown = jnp.exp(score - top)
                total = jnp.sum(grown, axis=0, keepdims=True)
                out["lse"][group * per + j] = top + jnp.log(total)
                probs = (grown * (1.0 / total)).astype(bf16)
                part = dot(v_turned[...], probs)
                mixed = part if mixed is None else jnp.where(iota((lanes, n_pick), 0) // head_dim == j, part, mixed)
            o_turned[pl.ds(pl.multiple_of(group * lanes, lanes), lanes)] = mixed

        out["o"][...] = o_turned[...].T.astype(bf16)
        put("lse")
        put("o")
        x1 = start_picked + dot(out["o"][...], flat(get("w_out"))) + vec[8:9]
        out["x1"][...] = x1
        put("x1")
        unit, _ = norm_parts(x1)
        out["m"][...] = (unit * vec[2:3] + vec[3:4]).astype(bf16)
        put("m")
        up, down = get("w_up"), get("w_down")
        x2 = x1 + vec[9:10]
        for block in range(up.shape[-1] // model):
            place = slice(block * model, (block + 1) * model)
            u1 = dot(out["m"][...], flat(up, place)) + vec[10 + block : 11 + block]
            x2 = x2 + dot(gelu_fn(u1).astype(bf16), row_block(down, block, model))
        out["x2"][...] = x2
        put("x2")
        unit, _ = norm_parts(x2)
        out["f"][...] = (unit * vec[4:5] + vec[5:6]).astype(bf16)
        put("f")

    def shape(rows, dtype):
        return jax.ShapeDtypeStruct((rows, model), dtype)

    outs = {
        "a": shape(length, bf16),
        "k": shape(length, bf16),
        "v": shape(length, bf16),
        "q": shape(n_pick, bf16),
        "lse": jax.ShapeDtypeStruct((H, 1, n_pick), f32),
        "o": shape(n_pick, bf16),
        "x1": shape(n_pick, f32),
        "m": shape(n_pick, bf16),
        "x2": shape(n_pick, f32),
        "f": shape(n_pick, bf16),
    }
    values = staged(
        work,
        {"emb": embedded, "pos": pos, "w_in": w_in, "w_out": w_out, "w_up": w_up, "w_down": w_down},
        {"vectors": vectors, "pick_col": picks[:, None], "length": row_length.reshape(1, 1)},
        outs,
        [pltpu.VMEM((lanes, length), bf16), pltpu.VMEM((model, n_pick), f32)],
        60,
        pieces=pieces,
    )
    return dict(zip(outs, values))


def layer_backward(
    final_grad, kept, embedded, pos, weights, vectors, picks, spots, row_length, loss, n_dp, pieces
):
    length, model = embedded.shape
    n_pick = picks.shape[0]
    lanes = 128
    groups = model // lanes
    head_dim = model // H
    per = lanes // head_dim
    w_in, w_out, w_up, w_down = weights
    hidden = w_up.shape[-1]
    thick, long, n_place = model // n_dp, hidden // n_dp, spots[1]
    wide = hidden // model
    first_rows = 2 * long
    last_rows = 4 * thick + length // n_dp

    def work(get, small, out, moves, temps):
        put, done = moves
        vec, d_vec = small["vectors"], out["vec"]
        dqkv, dq, d_mixed = temps
        whole = out["whole"]

        def rows_of(first, count, values):
            values = values.astype(bf16)
            for owner in range(n_dp):
                whole[owner, first : first + count] = values[owner * count : (owner + 1) * count]

        x2, dfin = get("x2"), get("dfin")
        dx2, d_vec[4:5], d_vec[5:6] = norm_back(x2[...], vec[4:5], dfin[...])
        dy2 = dx2.astype(bf16)
        d_vec[9:10] = jnp.sum(dy2.astype(f32), axis=0, keepdims=True)
        m, up, down = get("m"), get("w_up"), get("w_down")
        m_turned = m[...].T
        dm = None
        for block in range(wide):
            place = slice(block * model, (block + 1) * model)
            u1 = dot(m[...], flat(up, place)) + vec[10 + block : 11 + block]
            act, gelu_back = jax.vjp(gelu_fn, u1)
            part = dot(act.astype(bf16).T, dy2).astype(bf16)
            run = min(long, model)
            for at in range(0, model, run):
                owner, row = divmod(block * model + at, long)
                whole[owner, row : row + run] = part[at : at + run]
            du1 = gelu_back(dot(dy2, row_block(down, block, model), 1, 1))[0].astype(bf16)
            d_vec[10 + block : 11 + block] = jnp.sum(du1.astype(f32), axis=0, keepdims=True)
            rows_of(long + block * thick, thick, dot(m_turned, du1))
            part = dot(du1, flat(up, place), 1, 1)
            dm = part if dm is None else dm + part
        first_out = put("whole", 0, first_rows)
        dx1, d_vec[2:3], d_vec[3:4] = norm_back(get("x1")[...], vec[2:3], dm)
        dx1 = dx2 + dx1
        dy1 = dx1.astype(bf16)
        d_vec[8:9] = jnp.sum(dy1.astype(f32), axis=0, keepdims=True)
        done(first_out)
        rows_of(0, thick, dot(get("o")[...].T, dy1))
        d_mixed[...] = dot(dy1, flat(get("w_out")), 1, 1).astype(bf16)
        keep = iota((length, n_pick), 0) < small["length"][0, 0]
        q, k, v, lse = get("q"), get("k"), get("v"), small["lse"]

        @pl.loop(0, groups)
        def _(group):
            def place(part):
                return pl.ds(pl.multiple_of(part * model + group * lanes, lanes), lanes)

            q_pair, k_pair, v_pair, d_pair = q[:, place(0)], k[:, place(0)], v[:, place(0)], d_mixed[:, place(0)]
            k_turned = k_pair.T
            sums = None
            for j in range(per):
                lane = iota((n_pick, lanes), 1) // head_dim == j
                q_head = jnp.where(lane, q_pair, jnp.zeros_like(q_pair))
                d_head = jnp.where(lane, d_pair, jnp.zeros_like(d_pair))
                score = jnp.where(keep, dot(k_pair, q_head, 1, 1) * 0.125, mask_fill)
                probs = jnp.exp(score - lse[group * per + j])
                dp = dot(v_pair, d_head, 1, 1)
                ds = (probs * (dp - jnp.sum(dp * probs, axis=0, keepdims=True))).astype(bf16)
                parts = (dot(k_turned, ds), dot(ds, q_pair), dot(probs.astype(bf16), d_pair))
                if sums is None:
                    sums = parts
                else:
                    rows = iota((lanes, n_pick), 0) // head_dim == j
                    columns = iota((length, lanes), 1) // head_dim == j
                    sums = (
                        jnp.where(rows, parts[0], sums[0]),
                        jnp.where(columns, parts[1], sums[1]),
                        jnp.where(columns, parts[2], sums[2]),
                    )
            dq[:, place(0)] = (sums[0] * 0.125).T.astype(bf16)
            dqkv[:, place(1)] = (sums[1] * 0.125).astype(bf16)
            dqkv[:, place(2)] = sums[2].astype(bf16)

        chosen = jnp.where(small["pick_row"][...] - 1 == iota((length, n_pick), 0), 1.0, 0.0).astype(bf16)
        dqkv[:, :model] = dot(chosen, dq[...]).astype(bf16)
        d_vec[6:7] = jnp.sum(dq[...].astype(f32), axis=0, keepdims=True)
        d_vec[7:8] = jnp.sum(dqkv[:, 2 * model :].astype(f32), axis=0, keepdims=True)
        a_turned = get("a")[...].T
        for part in range(3):
            rows_of((1 + part) * thick, thick, dot(a_turned, dqkv[:, part * model : (part + 1) * model]))
        da = dot(dqkv[...], flat(get("w_in")), 1, 1)
        start = get("emb")[...].astype(f32) + flat(get("pos")).astype(f32)
        dx0, d_vec[0:1], d_vec[1:2] = norm_back(start, vec[0:1], da)
        for part in split_three(dx1):
            dx0 = dx0 + dot(chosen, part)
        rows_of(4 * thick, length // n_dp, dx0)
        put("whole", first_rows, last_rows)
        d_vec[14:15] = small["loss"][...]
        d_vec[15:16] = jnp.zeros((1, model), f32)
        put("vec")
        out["low"][...] = dx0.astype(bf16)
        put("low")
        step = min(n_place, 512)
        for first in range(0, n_place, step):
            where = jnp.where(small["spots"][...] == iota((step, length), 0) + first, 1.0, 0.0).astype(bf16)
            out["given"][first : first + step] = dot(where, out["low"][...]).astype(bf16)
        put("given")

    outs = {
        "whole": jax.ShapeDtypeStruct((n_dp, first_rows + last_rows, model), bf16),
        "vec": jax.ShapeDtypeStruct((16, model), f32),
        "low": jax.ShapeDtypeStruct((length, model), bf16),
        "given": jax.ShapeDtypeStruct((n_place, model), bf16),
    }
    ins = {
        "x2": kept["x2"],
        "dfin": final_grad,
        "m": kept["m"],
        "w_up": w_up,
        "w_down": w_down,
        "x1": kept["x1"],
        "o": kept["o"],
        "w_out": w_out,
        "q": kept["q"],
        "k": kept["k"],
        "v": kept["v"],
        "a": kept["a"],
        "w_in": w_in,
        "emb": embedded,
        "pos": pos,
    }
    small = {
        "vectors": vectors,
        "lse": kept["lse"],
        "pick_row": picks[None, :],
        "spots": spots[0][None, :],
        "length": row_length.reshape(1, 1),
        "loss": jnp.full((1, model), loss),
    }
    temps = [
        pltpu.VMEM((length, 3 * model), bf16),
        pltpu.VMEM((n_pick, model), bf16),
        pltpu.VMEM((n_pick, model), bf16),
    ]
    buffer = jax.ShapeDtypeStruct((n_dp, max(first_rows, last_rows), model), bf16)
    return staged(work, ins, small, outs, temps, 62, {"whole": buffer}, pieces, 5)


def table_forms(table, size, chunk):
    count, width = table.shape

    def body(t_ref, low_ref, turned_ref):
        row = iota((chunk, width), 0) + pl.program_id(0) * chunk
        value = jnp.where(row < count, t_ref[...], 0.0)
        low_ref[...] = value.astype(bf16)
        turned_ref[...] = value.T.astype(bf16)

    return pl.pallas_call(
        body,
        grid=(size // chunk,),
        in_specs=[pl.BlockSpec((chunk, width), lambda step: (step, 0))],
        out_specs=(
            pl.BlockSpec((chunk, width), lambda step: (step, 0)),
            pl.BlockSpec((width, chunk), lambda step: (0, step)),
        ),
        out_shape=(
            jax.ShapeDtypeStruct((size, width), bf16),
            jax.ShapeDtypeStruct((width, size), bf16),
        ),
        compiler_params=pltpu.CompilerParams(vmem_limit_bytes=32 << 20),
    )(table)


def close_half(own, other, names, values, layer, tile):
    half, width = own.shape
    count = min(names.shape[1], 2048)
    parts = names.shape[1] // count

    def body(own_ref, other_ref, names_ref, values_ref, layer_ref, o_ref, square_ref, total):
        step, part = pl.program_id(0), pl.program_id(1)

        @pl.when(part == 0)
        def _():
            total[...] = own_ref[...].astype(f32) + other_ref[...].astype(f32)

        row = iota((tile, count), 0) + step * tile
        where = jnp.where(row == names_ref[...], 1.0, 0.0).astype(bf16)
        total[...] += jnp.dot(where, values_ref[...], preferred_element_type=f32)

        @pl.when((step == 0) & (part == 0))
        def _():
            layer_part = layer_ref[...].astype(f32)
            square_ref[...] = jnp.sum(layer_part * layer_part, axis=0, keepdims=True)

        @pl.when(part == parts - 1)
        def _():
            o_ref[...] = total[...].astype(bf16)
            square_ref[...] += jnp.sum(total[...] * total[...], axis=0, keepdims=True)

    rows = pl.BlockSpec((tile, width), lambda step, part: (step, 0))
    return pl.pallas_call(
        body,
        grid=(half // tile, parts),
        in_specs=[
            rows,
            rows,
            pl.BlockSpec((1, count), lambda step, part: (0, part)),
            pl.BlockSpec((count, width), lambda step, part: (part, 0)),
            pl.BlockSpec(layer.shape, lambda step, part: (0, 0)),
        ],
        out_specs=(rows, pl.BlockSpec((1, width), lambda step, part: (0, 0))),
        out_shape=(jax.ShapeDtypeStruct((half, width), bf16), jax.ShapeDtypeStruct((1, width), f32)),
        scratch_shapes=[pltpu.VMEM((tile, width), f32)],
        compiler_params=pltpu.CompilerParams(vmem_limit_bytes=48 << 20),
        cost_estimate=pl.CostEstimate(
            flops=2 * half * names.shape[1] * width, bytes_accessed=8 * half * width, transcendentals=0
        ),
    )(own, other, names, values, layer)


def adam_table(at, factor, weights, mine, other, tile, half, n_x, steps, done):
    size, width = weights[0].shape
    per_half, per_part = half // tile, half // n_x // tile
    turns = len(steps) * per_part
    first_step = steps[0]

    def body(at_ref, factor_ref, w_ref, m_ref, v_ref, mine_ref, other_ref, *refs):
        from_mine = pl.program_id(0) < turns
        grad = jnp.where(from_mine, mine_ref[...], other_ref[...]).astype(f32) * factor_ref[0]
        new_w, new_m, new_v, token = refs[-4:]
        token[...] = jnp.zeros_like(token)
        new_w[...], new_m[...], new_v[...] = adam_update(
            w_ref[...], grad, m_ref[...], v_ref[...], 0.1, 0.1
        )

    def row_at(step, at_ref, factor_ref):
        core = lax.rem(at_ref[0] + step // turns, 2)
        turn = lax.rem(step, turns)
        x = lax.rem(at_ref[1] + n_x - (first_step + turn // per_part), n_x)
        return (core * per_half + x * per_part + lax.rem(turn, per_part), 0)

    def mine_at(step, at_ref, factor_ref):
        return (jnp.minimum(step, turns - 1), 0)

    def other_at(step, at_ref, factor_ref):
        return (jnp.maximum(step - turns, 0), 0)

    rows = pl.BlockSpec((tile, width), row_at)
    done = () if done is None else done
    return pl.pallas_call(
        body,
        grid_spec=pltpu.PrefetchScalarGridSpec(
            num_scalar_prefetch=2,
            grid=(2 * turns,),
            in_specs=[rows, rows, rows, pl.BlockSpec((tile, width), mine_at), pl.BlockSpec((tile, width), other_at)]
            + [HBM] * len(done),
            out_specs=(rows, rows, rows, pl.BlockSpec((8, 128), lambda *_: (0, 0))),
        ),
        out_shape=(jax.ShapeDtypeStruct((size, width), f32),) * 3 + (jax.ShapeDtypeStruct((8, 128), f32),),
        input_output_aliases={7 + index: index for index in range(len(done))},
        compiler_params=pltpu.CompilerParams(vmem_limit_bytes=56 << 20),
        cost_estimate=pl.CostEstimate(
            flops=40 * turns * tile * width, bytes_accessed=52 * turns * tile * width, transcendentals=0
        ),
    )(at, factor.reshape(1), *weights, mine, other, *done)


def layer_norm(x, gain, shift):
    centre = x - jnp.mean(x, axis=-1, keepdims=True)
    var = jnp.mean(centre * centre, axis=-1, keepdims=True)
    return centre * lax.rsqrt(var + 1e-05) * gain + shift


def gelu_fn(x):
    return jax.nn.gelu(x, approximate=True)


def adam_update(weight, grad, first, second, rate, decay):
    first_new = beta_one * first + (1.0 - beta_one) * grad
    second_new = beta_two * second + (1.0 - beta_two) * grad * grad
    mhat = first_new / (1.0 - beta_one**STEP)
    vhat = second_new / (1.0 - beta_two**STEP)
    return (
        weight - rate * (mhat / (jnp.sqrt(vhat) + adam_eps) + decay * weight),
        first_new,
        second_new,
    )


def as_rows(flat):
    return jnp.pad(flat, (0, -flat.size % 1024)).reshape(-1, 128)


def on_device(
    clean_ids,
    lengths,
    masked,
    attn_in,
    attn_out,
    mlp_in,
    mlp_out,
    table,
    positions,
    vectors,
    first_attn_in,
    first_attn_out,
    first_mlp_in,
    first_mlp_out,
    first_table,
    first_positions,
    first_vectors,
    second_attn_in,
    second_attn_out,
    second_mlp_in,
    second_mlp_out,
    second_table,
    second_positions,
    second_vectors,
):
    rows, slots = clean_ids.shape
    n_dp = lax.axis_size("dp")
    n_seq = lax.axis_size("seq")
    dp_at = lax.axis_index("dp")
    seq_at = lax.axis_index("seq")
    core = lax.rem(seq_at, 2)
    length = slots * n_seq
    vocab_part, model = table.shape
    vocab = vocab_part * n_dp
    head_dim = model // H
    sharers = max(1, n_seq // rows)
    n_pick = masked.shape[1] // sharers
    row_at = seq_at // sharers
    share = lax.rem(seq_at, sharers)
    half = -(-vocab_part // 256) * 128
    tile = 128 * max(count for count in range(1, 8) if half % (128 * count) == 0)
    n_x = n_seq // 2
    n_y = 1 << (n_dp.bit_length() - 1) // 2
    n_z = n_dp // n_y

    def piece_of(weight):
        piece = weight.shape[0] // n_seq
        return lax.dynamic_slice_in_dim(weight, seq_at * piece, piece, 0).astype(bf16)

    thick = attn_in.shape[0]
    hidden = mlp_in.shape[1]
    blocks = 4
    split = n_seq // blocks
    thin = thick // split

    def block_of(weights):
        wide = [weight[:, at : at + model] for weight in weights for at in range(0, weight.shape[1], model)]
        wide = jnp.stack(wide).reshape(n_seq, thin, model)
        return lax.dynamic_index_in_dim(wide, seq_at, 0, False).astype(bf16)

    given_rows = [block_of((attn_in, attn_out)), block_of((mlp_in,)), piece_of(mlp_out), piece_of(positions)]
    ends = [0]
    for piece in given_rows:
        ends.append(ends[-1] + piece.shape[0])
    long, some = ends[3] - ends[2], ends[4] - ends[3]
    packed = lax.all_gather(jnp.concatenate(given_rows), ("dp", "seq")).reshape(n_dp, n_seq, -1, model)
    if thin % 16 == 0 and some % 16 == 0 and split == 1:

        def rows_at(part):
            return pl.ds(ends[part], ends[part + 1] - ends[part])

        def blocks_at(part, blocks):
            return [
                ((slice(None), block, rows_at(part)), (slice(None), slice(None), pl.ds(at * model, model)))
                for at, block in enumerate(blocks)
            ]

        def all_at(part):
            return [((slice(None), slice(None), rows_at(part)), (slice(None),))]

        weight_pieces = (
            packed,
            {
                "pos": all_at(3),
                "w_in": blocks_at(0, range(3)),
                "w_out": blocks_at(0, [3]),
                "w_up": blocks_at(1, range(4)),
                "w_down": all_at(2),
            },
        )

        def shape(*dims):
            return jax.ShapeDtypeStruct(dims, bf16)

        pos_all, w_in, w_out = shape(n_dp, n_seq, some, model), shape(n_dp, thick, 3 * model), shape(n_dp, thick, model)
        w_up, w_down = shape(n_dp, thick, hidden), shape(n_dp, n_seq, long, model)
    else:
        weight_pieces = None

        def columns_of(part, block):
            got = packed[:, block * split : (block + 1) * split, ends[part] : ends[part + 1]]
            return got.reshape(-1, model)

        w_in = jnp.concatenate([columns_of(0, block) for block in range(3)], axis=1)
        w_out = columns_of(0, 3)
        w_up = jnp.concatenate([columns_of(1, block) for block in range(4)], axis=1)
        w_down = packed[:, :, ends[2] : ends[3]].reshape(hidden, model)
        pos_all = packed[:, :, ends[3] :].reshape(length, model)

    all_rows = deliver(clean_ids, ("seq",), 1)
    row_ids = lax.dynamic_index_in_dim(all_rows, row_at, 1, keepdims=False).reshape(length)
    row = dp_at * rows + row_at
    row_length = lax.dynamic_index_in_dim(lengths, row, 0, keepdims=False)
    row_masked = lax.dynamic_index_in_dim(masked, row, 0, keepdims=False)
    picks = lax.dynamic_slice_in_dim(row_masked, share * n_pick, n_pick, 0)
    slot = jnp.arange(length, dtype=i32)
    is_masked = jnp.any(slot[:, None] == row_masked[None, :], axis=1)
    noisy = jnp.where(is_masked, vocab - 1, row_ids)
    targets = jnp.sum(jnp.where(picks[:, None] == slot[None, :], row_ids[None, :], 0), axis=1)
    valid_all = ((masked >= 1) & (masked < lengths[:, None])).astype(f32)
    masked_count = jnp.sum(valid_all)

    owner = noisy // vocab_part
    within = noisy - owner * vocab_part
    owner_half = owner * 2 + (within >= half).astype(i32)
    within_half = jnp.where(within >= half, within - half, within)
    same = noisy[:, None] == noisy[None, :]
    leader = jnp.min(jnp.where(same, slot[None, :], length), axis=1)
    leads = leader == slot
    before = (slot[None, :] < slot[:, None]) & leads[None, :]
    rank = jnp.sum((before & (owner[:, None] == owner[None, :])).astype(i32), axis=1)
    rank_half = jnp.sum((before & (owner_half[:, None] == owner_half[None, :])).astype(i32), axis=1)
    lead_of = leader[:, None] == slot[None, :]
    place = jnp.sum(jnp.where(lead_of, rank[None, :], 0), axis=1)
    place_half = jnp.sum(jnp.where(lead_of, rank_half[None, :], 0), axis=1)

    def asked(owners, ranks, names, count, size, turn):
        spot = jnp.where(ranks // size == turn, owners * size + lax.rem(ranks, size), -1)
        spots = jnp.arange(count * size, dtype=i32)
        listed = leads[None, :] & (spots[:, None] == spot[None, :])
        return spot, jnp.sum(jnp.where(listed, names[None, :], 0), axis=1)

    spot, ask = asked(owner, place, within, n_dp, FETCH, 0)
    spot_half, ask_half = asked(owner_half, place_half, within_half, 2 * n_dp, GIVE, 0)
    turns = jnp.stack([jnp.max(place) // FETCH + 1, jnp.max(place_half) // GIVE + 1])
    pieces = [as_rows(piece) for piece in (ask, ask_half, targets, turns)]
    ends = [0]
    for piece in pieces:
        ends.append(ends[-1] + piece.shape[0])
    told = deliver(jnp.concatenate(pieces), ("dp", "seq"), 2)

    def heard(index, size):
        return told[:, ends[index] : ends[index + 1]].reshape(n_dp * n_seq, -1)[:, :size]

    turns = jnp.max(heard(3, 2), axis=0)
    asks = lax.dynamic_index_in_dim(heard(0, n_dp * FETCH).reshape(n_dp, n_seq, n_dp, FETCH), seq_at, 1, False)
    asks = lax.dynamic_index_in_dim(asks, dp_at, 1, False)
    half_at = dp_at * 2 + core
    asks_half = lax.dynamic_index_in_dim(heard(1, 2 * n_dp * GIVE).reshape(-1, 2 * n_dp, GIVE), half_at, 1, False)
    all_targets = lax.dynamic_index_in_dim(heard(2, n_pick).reshape(n_dp, n_seq, n_pick), seq_at, 1, False)

    def one_hot(spots, count):
        return (spots[:, None] == jnp.arange(count, dtype=i32)[None, :]).astype(bf16)

    table_low, table_turned = table_forms(table, 2 * half, tile)
    found = jnp.take(table_low, asks, axis=0)
    fetched = deliver(found, ("dp",), 3, lambda place: place[0]).reshape(n_dp * FETCH, model)
    embedded = jnp.dot(one_hot(spot, n_dp * FETCH), fetched, preferred_element_type=f32)

    def fetch_more(state):
        turn, total = state
        next_spot, next_ask = asked(owner, place, within, n_dp, FETCH, turn)
        wanted = lax.all_to_all(next_ask.reshape(n_dp, FETCH), "dp", 0, 0)
        sent = jnp.take(table_low, wanted, axis=0)
        got = lax.all_to_all(sent, "dp", 0, 0).reshape(n_dp * FETCH, model)
        return turn + 1, total + jnp.dot(one_hot(next_spot, n_dp * FETCH), got, preferred_element_type=f32)

    _, embedded = lax.while_loop(lambda state: state[0] < turns[0], fetch_more, (jnp.int32(1), embedded))

    embedded = embedded.astype(bf16)
    kept = layer_forward(
        embedded, pos_all, w_in, w_out, w_up, w_down, vectors, picks, row_length, weight_pieces
    )
    sources = kept["f"]

    flat_targets = (all_targets - dp_at * vocab_part).reshape(n_dp, 1, n_pick)
    flat_targets = jnp.where(flat_targets < vocab_part, flat_targets, -1)
    rows_here = valid_all.reshape(n_dp, rows, sharers, n_pick)
    rows_here = lax.dynamic_index_in_dim(rows_here, row_at, 1, False)
    flat_valid = lax.dynamic_index_in_dim(rows_here, share, 1, False).reshape(n_dp, 1, n_pick)
    grown, heads, tops, stats = read_heads(
        sources, table_low, flat_targets, vocab_part, tile, n_y, n_z, 9
    )
    final_grad, half_low, logs = write_heads(
        grown, heads, table_turned, tops, stats, flat_targets, flat_valid / masked_count, tile, 5
    )
    loss_group = jnp.sum(flat_valid * (logs[0] - logs[1]))
    final_grad = jnp.sum(final_grad.astype(f32), axis=0).T
    half_low = half_low.reshape(half, model)
    part = half // n_x
    slab = 16 * max(count for count in range(1, 26) if part % (16 * count) == 0)
    x_at = seq_at // 2

    def part_of(step):
        return lax.dynamic_slice_in_dim(half_low, lax.rem(x_at + step, n_x) * part, part, 0)

    part_came = [from_peer(part_of(step), "seq", 2, n_x, step) for step in range(1, n_x)]
    if n_x > 2:
        part_came = [sum(came.astype(f32) for came in part_came).astype(bf16)]

    whole, vec_grad, start_grad_low, first_given = layer_backward(
        final_grad,
        kept,
        embedded,
        pos_all,
        (w_in, w_out, w_up, w_down),
        vectors,
        picks,
        (spot_half, 2 * n_dp * GIVE),
        row_length,
        loss_group,
        n_dp,
        weight_pieces,
    )

    def given(spots):
        summed_ids = jnp.einsum(
            "ts,td->sd", one_hot(spots, 2 * n_dp * GIVE), start_grad_low, preferred_element_type=f32
        )
        return summed_ids.astype(bf16).reshape(2 * n_dp, GIVE, model)

    chunks = 4
    layer_piece, came, vec_total = settle(
        whole.reshape(n_dp, 2, n_x, chunks, -1, model),
        first_given.reshape(2 * n_dp, GIVE, model),
        vec_grad,
        n_x,
        n_y,
        n_z,
        7,
    )
    layer_piece = layer_piece.reshape(-1, model)

    def give_more(state):
        turn, total, _ = state
        next_spot, next_ask = asked(owner_half, place_half, within_half, 2 * n_dp, GIVE, turn)
        names = lax.all_gather(next_ask.reshape(2 * n_dp, GIVE), ("dp", "seq"))
        names = lax.dynamic_index_in_dim(names, half_at, 1, False).reshape(1, -1) - x_at * part
        sent = given(next_spot).reshape(n_dp, 1, 2, GIVE, model)
        sent = jnp.broadcast_to(sent, (n_dp, n_x, 2, GIVE, model)).reshape(-1, GIVE, model)
        got = lax.all_to_all(sent, ("dp", "seq"), 0, 0).reshape(-1, model)
        total, squares = close_half(
            total, jnp.zeros_like(total), names, got, layer_piece, slab
        )
        return turn + 1, total, jnp.sum(squares)

    names = asks_half.reshape(1, -1) - x_at * part
    values = came.reshape(-1, model)
    part_own, squares_own = close_half(
        part_of(0), part_came[0], names, values, layer_piece, slab
    )
    _, part_own, part_square = lax.while_loop(
        lambda state: state[0] < turns[1], give_more, (jnp.int32(1), part_own, jnp.sum(squares_own))
    )
    layer_sum = group_join(layer_piece, 0, "seq", 2, n_x).reshape(-1, model)
    layer_sum = group_join(layer_sum, 0, "seq", 1, 2).reshape(-1, model).astype(f32)
    loss_sum = vec_total[14, 0] / n_dp
    vec_total = vec_total[:14]

    def side_by_side(rows_of, count):
        return jnp.concatenate(jnp.split(rows_of, count, axis=0), axis=1)

    ends = [0]
    for count in (mlp_out.shape[0], hidden // model * thick, thick, 3 * thick, positions.shape[0]):
        ends.append(ends[-1] + count)
    g_down, g_up, g_out, g_in, g_pos = [layer_sum[begin:end] for begin, end in zip(ends, ends[1:])]
    g_in = side_by_side(g_in, 3)
    g_up = side_by_side(g_up, hidden // model)
    said = jnp.full((8, 128), part_square)
    square_total = jnp.sum(deliver(said, ("dp", "seq"), 8)[:, 0, 0])
    part_own, square_total = lax.optimization_barrier((part_own, square_total))
    far_own = [from_peer(part_own, "seq", 2, n_x, step) for step in range(1, n_x)]
    far_own = far_own[0] if n_x == 2 else jnp.concatenate(far_own)
    part_pair = from_peer(part_own, "seq", 1, 2, 1)
    grad_norm = jnp.sqrt(square_total + jnp.sum(vec_total * vec_total))
    factor = clip_at / jnp.maximum(grad_norm, clip_at)
    weights = (attn_in, attn_out, mlp_in, mlp_out, table, positions, vectors)
    all_grads = (g_in, g_out, g_up, g_down, None, g_pos, vec_total)
    firsts = (
        first_attn_in,
        first_attn_out,
        first_mlp_in,
        first_mlp_out,
        first_table,
        first_positions,
        first_vectors,
    )
    seconds = (
        second_attn_in,
        second_attn_out,
        second_mlp_in,
        second_mlp_out,
        second_table,
        second_positions,
        second_vectors,
    )
    news, moments, squares = ([], [], [])
    for index in range(7):
        rate, decay = (1.0, 0.0) if index == 6 else (0.1, 0.1)
        if index == 4:
            state = (table, first_table, second_table)
            at = jnp.stack([core, x_at])
            *near, token = adam_table(at, factor, state, part_own, part_pair, slab, half, n_x, (0,), None)
            far_own = far_own + token[0, 0].astype(bf16)
            far_pair = from_peer(far_own, "seq", 1, 2, 1)
            far_steps = tuple(range(1, n_x))
            new_w, new_m, new_v, _ = adam_table(
                at, factor, state, far_own, far_pair, slab, half, n_x, far_steps, near
            )
        else:
            new_w, new_m, new_v = adam_update(
                weights[index], all_grads[index] * factor, firsts[index], seconds[index], rate, decay
            )
        news.append(new_w)
        moments.append(new_m)
        squares.append(new_v)
    return (*news, *moments, *squares, loss_sum, masked_count, grad_norm)


def solution(mesh):
    part = P("dp", None)
    six = (part,) * 6 + (P(),)
    return jax.shard_map(
        on_device,
        mesh=mesh,
        in_specs=(P("dp", "seq"), P(), P()) + six * 3,
        out_specs=six * 3 + (P(), P(), P()),
        check_vma=False,
    )
```

```python
import math

import jax
import jax.numpy as jnp
from jax import lax
from jax.experimental import pallas as pl
from jax.experimental.pallas import tpu as pltpu
from jax.sharding import PartitionSpec as P

H = 12
STEP = 10
FETCH = 96
GIVE = 64

mask_fill = -1000000000.0
clip_at = 0.002
beta_one = 0.9
beta_two = 0.999
adam_eps = 1e-08

f32 = jnp.float32
bf16 = jnp.bfloat16
i32 = jnp.int32
HBM = pl.BlockSpec(memory_space=pl.ANY)
VMEM = pl.BlockSpec(memory_space=pltpu.VMEM)
MESH = pl.DeviceIdType.MESH


def deliver(x, axes, call_id, block_of=None):
    sizes = [lax.axis_size(axis) for axis in axes]
    count = math.prod(sizes)
    block = x.shape if block_of is None else x.shape[1:]

    def body(x_ref, o_ref, sent, came, own):
        here = [lax.axis_index(axis) for axis in axes]

        def flat(place):
            index = place[0]
            for size, along in zip(sizes[1:], place[1:]):
                index = index * size + along
            return index

        def peer(step):
            place = []
            for size, at in zip(reversed(sizes), reversed(here)):
                place.append(lax.rem(at + lax.rem(step, size), size))
                step = step // size
            return place[::-1]

        def source(place):
            return x_ref if block_of is None else x_ref.at[block_of(place)]

        mine = flat(here)

        def copy(step):
            place = peer(step)
            return pltpu.make_async_remote_copy(
                source(place),
                o_ref.at[mine],
                sent.at[step],
                came.at[step],
                device_id=dict(zip(axes, place)),
                device_id_type=MESH,
            )

        barrier = pltpu.get_barrier_semaphore()

        @pl.loop(1, count)
        def _(step):
            pl.semaphore_signal(
                barrier, inc=1, device_id=dict(zip(axes, peer(step))), device_id_type=MESH
            )

        local = pltpu.make_async_copy(source(here), o_ref.at[mine], own)
        local.start()
        pl.semaphore_wait(barrier, count - 1)

        @pl.loop(1, count)
        def _(step):
            copy(step).start()

        local.wait()

        @pl.loop(1, count)
        def _(step):
            copy(step).wait()

    return pl.pallas_call(
        body,
        out_shape=jax.ShapeDtypeStruct((count,) + block, x.dtype),
        in_specs=[HBM],
        out_specs=HBM,
        scratch_shapes=[
            pltpu.SemaphoreType.DMA((count,)),
            pltpu.SemaphoreType.DMA((count,)),
            pltpu.SemaphoreType.DMA,
        ],
        compiler_params=pltpu.CompilerParams(collective_id=call_id, has_side_effects=True),
    )(x)


def from_peer(x, axis, span, size, step):
    pairs = []
    for at in range(lax.axis_size(axis)):
        digit = at // span % size
        pairs.append((at, at + ((digit + step) % size - digit) * span))
    return lax.ppermute(x, axis, pairs)


def group_sum(x, dim, axis, span):
    size = x.shape[dim]
    at = lax.rem(lax.axis_index(axis) // span, size)
    total = lax.dynamic_index_in_dim(x, at, dim, False).astype(f32)
    for step in range(1, size):
        block = lax.dynamic_index_in_dim(x, lax.rem(at + step, size), dim, False)
        total = total + from_peer(block, axis, span, size, step).astype(f32)
    return total.astype(bf16)


def group_join(x, dim, axis, span, size):
    at = lax.rem(lax.axis_index(axis) // span, size)
    parts = [x] + [from_peer(x, axis, span, size, size - step) for step in range(1, size)]
    if size == 2:
        first = jnp.where(at == 0, parts[0], parts[1])
        second = jnp.where(at == 0, parts[1], parts[0])
        return jnp.stack([first, second], axis=dim)
    turned = jnp.stack(parts + parts, axis=dim)
    return lax.dynamic_slice_in_dim(turned, size - at, size, dim)


def settle(grads, given, vector, n_x, n_y, n_z, call_id):
    n_dp, _, _, chunks, height, width = grads.shape
    n_seq = 2 * n_x
    count = n_dp * n_seq
    near = n_dp * 2
    n_most = max(n_x, n_y)
    blocks = n_x * n_y * n_z

    def body(g_ref, e_ref, v_ref, o_ref, came_ref, vec_ref, *scratch):
        own, got, first, second, third = scratch[:5]
        v_core, v_x, v_y, v_z = scratch[5:9]
        core_out, core_in, core_own = scratch[9:12]
        one_out, one_in, two_out, two_in, three_out, three_in = scratch[12:18]
        x_out, x_in, pair_out, pair_in, last_own = scratch[18:23]
        e_out, e_in, far_out, far_in, v_out, v_in, side_own = scratch[23:]
        dp_at, seq_at = lax.axis_index("dp"), lax.axis_index("seq")
        x_at, c_at = seq_at // 2, lax.rem(seq_at, 2)
        z_at, y_at = dp_at // n_y, lax.rem(dp_at, n_y)
        partner = {"seq": x_at * 2 + 1 - c_at}

        def send(source, target, out_sem, in_sem, device):
            copy = pltpu.make_async_remote_copy(
                source, target, out_sem, in_sem, device_id=device, device_id_type=MESH
            )
            copy.start()
            return copy

        barrier = pltpu.get_barrier_semaphore()

        @pl.loop(1, count)
        def _(step):
            seq_to = lax.rem(seq_at + lax.rem(step, n_seq), n_seq)
            peer = {"dp": lax.rem(dp_at + step // n_seq, n_dp), "seq": seq_to}
            pl.semaphore_signal(barrier, inc=1, device_id=peer, device_id_type=MESH)

        def x_first(chunk):
            return chunk % 2 == 1

        def order(chunk):
            return (n_x, x_at, n_y, y_at) if x_first(chunk) else (n_y, y_at, n_x, x_at)

        def places(chunk, block):
            z, y, x = block // (n_y * n_x), lax.rem(block // n_x, n_y), lax.rem(block, n_x)
            at = (x * n_y + y) * n_z + z if x_first(chunk) else (y * n_x + x) * n_z + z
            return z * n_y + y, x, at

        for chunk in range(chunks):

            @pl.loop(0, blocks)
            def _(block):
                owner, x, at = places(chunk, block)
                source = g_ref.at[owner, c_at, x, chunk]
                pltpu.make_async_copy(source, own.at[chunk, at], core_own.at[chunk]).start()

        v_core[c_at] = v_ref[...]
        mine = came_ref.at[dp_at * n_seq + seq_at]
        side = pltpu.make_async_copy(e_ref.at[dp_at * 2 + c_at], mine, side_own)
        side.start()
        pl.semaphore_wait(barrier, count - 1)
        for chunk in range(chunks):

            @pl.loop(0, blocks)
            def _(block):
                owner, x, at = places(chunk, block)
                source = g_ref.at[owner, 1 - c_at, x, chunk]
                send(source, got.at[chunk, at], core_out.at[chunk], core_in.at[chunk], partner)

        v_turn = [
            (v_core, c_at, 2, lambda to: {"seq": x_at * 2 + to}),
            (v_x, x_at, n_x, lambda to: {"seq": to * 2 + c_at}),
            (v_y, y_at, n_y, lambda to: {"dp": z_at * n_y + to}),
            (v_z, z_at, n_z, lambda to: {"dp": to * n_y + y_at}),
        ]

        def vector_out(turn):
            buffer, at, size, device = v_turn[turn]
            return [
                send(
                    buffer.at[at],
                    buffer.at[at],
                    v_out.at[turn, step - 1],
                    v_in.at[turn, step - 1],
                    device(lax.rem(at + step, size)),
                )
                for step in range(1, size)
            ]

        def vector_sum(turn, copies):
            buffer, _, size, _ = v_turn[turn]
            for copy in copies:
                copy.wait()
            total = buffer[0]
            for place in range(1, size):
                total = total + buffer[place]
            return total

        v_copies = vector_out(0)

        def near_copy(step):
            owner = lax.rem(dp_at + step // 2, n_dp)
            core = lax.rem(c_at + lax.rem(step, 2), 2)
            return pltpu.make_async_remote_copy(
                e_ref.at[owner * 2 + core],
                mine,
                e_out.at[step],
                e_in.at[step],
                device_id={"dp": owner, "seq": x_at * 2 + core},
                device_id_type=MESH,
            )

        def far_copy(step, turn):
            origin = lax.rem(dp_at + n_dp - step // 2, n_dp)
            core = lax.rem(c_at + lax.rem(step, 2), 2)
            block = came_ref.at[origin * n_seq + x_at * 2 + core]
            to = lax.rem(x_at + turn, n_x) * 2 + c_at
            return pltpu.make_async_remote_copy(
                block,
                block,
                far_out.at[step, turn - 1],
                far_in.at[step, turn - 1],
                device_id={"seq": to},
                device_id_type=MESH,
            )

        @pl.loop(1, near)
        def _(step):
            near_copy(step).start()

        kept = {}
        for chunk in range(chunks):
            n_first, at_first, n_second, at_second = order(chunk)
            span = n_second * n_z
            whole = own.at[chunk]
            pltpu.make_async_copy(whole, whole, core_own.at[chunk]).wait()
            pltpu.make_async_remote_copy(
                whole, whole, core_out.at[chunk], core_in.at[chunk], device_id=partner, device_id_type=MESH
            ).wait()

            @pl.loop(0, blocks)
            def _(block):
                total = own[chunk, block].astype(f32) + got[chunk, block].astype(f32)
                own[chunk, block] = total.astype(bf16)

            for step in range(1, n_first):
                to = lax.rem(at_first + step, n_first)
                if x_first(chunk):
                    device = {"seq": to * 2 + c_at}
                else:
                    device = {"dp": z_at * n_y + to}
                copy = send(
                    own.at[chunk, pl.ds(to * span, span)],
                    first.at[chunk, step - 1, pl.ds(0, span)],
                    one_out.at[chunk, step - 1],
                    one_in.at[chunk, step - 1],
                    device,
                )
                kept[1, chunk, step] = copy
        v_x[x_at] = vector_sum(0, v_copies)
        v_copies = vector_out(1)
        side.wait()
        for turn in range(1, n_x):
            far_copy(0, turn).start()
        for chunk in range(chunks):
            n_first, at_first, n_second, at_second = order(chunk)
            span = n_second * n_z
            for step in range(1, n_first):
                kept[1, chunk, step].wait_recv()
            base = at_first * span

            @pl.loop(0, span)
            def _(block):
                total = own[chunk, base + block].astype(f32)
                for step in range(1, n_first):
                    total = total + first[chunk, step - 1, block].astype(f32)
                own[chunk, base + block] = total.astype(bf16)

            for step in range(1, n_second):
                to = lax.rem(at_second + step, n_second)
                if x_first(chunk):
                    device = {"dp": z_at * n_y + to}
                else:
                    device = {"seq": to * 2 + c_at}
                kept[2, chunk, step] = send(
                    own.at[chunk, pl.ds(base + to * n_z, n_z)],
                    second.at[chunk, step - 1],
                    two_out.at[chunk, step - 1],
                    two_in.at[chunk, step - 1],
                    device,
                )
            if chunk == 0:
                v_y[y_at] = vector_sum(1, v_copies)
                v_copies = vector_out(2)

                @pl.loop(1, near)
                def _(step):
                    near_copy(step).wait()
                    for turn in range(1, n_x):
                        far_copy(step, turn).start()

        v_z[z_at] = vector_sum(2, v_copies)
        v_copies = vector_out(3)
        for chunk in range(chunks):
            n_first, at_first, n_second, at_second = order(chunk)
            for step in range(1, n_second):
                kept[2, chunk, step].wait_recv()
            base = (at_first * n_second + at_second) * n_z

            @pl.loop(0, n_z)
            def _(block):
                total = own[chunk, base + block].astype(f32)
                for step in range(1, n_second):
                    total = total + second[chunk, step - 1, block].astype(f32)
                own[chunk, base + block] = total.astype(bf16)

            for step in range(1, n_z):
                to = lax.rem(z_at + step, n_z)
                kept[3, chunk, step] = send(
                    own.at[chunk, base + to],
                    third.at[chunk, step - 1],
                    three_out.at[chunk, step - 1],
                    three_in.at[chunk, step - 1],
                    {"dp": to * n_y + y_at},
                )
        vec_ref[...] = vector_sum(3, v_copies)
        for chunk in range(chunks):
            n_first, at_first, n_second, at_second = order(chunk)
            for step in range(1, n_z):
                kept[3, chunk, step].wait_recv()
            here = (at_first * n_second + at_second) * n_z + z_at
            total = own[chunk, here].astype(f32)
            for step in range(1, n_z):
                total = total + third[chunk, step - 1].astype(f32)
            own[chunk, here] = total.astype(bf16)
            result = o_ref.at[c_at, x_at, chunk]
            copy = pltpu.make_async_copy(own.at[chunk, here], result, last_own.at[chunk])
            copy.start()
            kept[0, chunk] = copy
            for step in range(1, n_x):
                to = lax.rem(x_at + step, n_x)
                kept[4, chunk, step] = send(
                    own.at[chunk, here],
                    result,
                    x_out.at[chunk, step - 1],
                    x_in.at[chunk, step - 1],
                    {"seq": to * 2 + c_at},
                )
            kept[5, chunk, 0] = send(
                own.at[chunk, here], result, pair_out.at[chunk, 0], pair_in.at[chunk, 0], partner
            )
        for chunk in range(chunks):
            for step in range(1, n_x):
                kept[4, chunk, step].wait_recv()
                origin = lax.rem(x_at + n_x - step, n_x)
                piece = o_ref.at[c_at, origin, chunk]
                kept[5, chunk, step] = send(
                    piece, piece, pair_out.at[chunk, step], pair_in.at[chunk, step], partner
                )

        @pl.loop(0, near)
        def _(step):
            for turn in range(1, n_x):
                far_copy(step, turn).wait()

        for chunk in range(chunks):
            kept[0, chunk].wait()
            for step in range(n_x):
                kept[5, chunk, step].wait()
        for key, copy in kept.items():
            if 1 <= key[0] <= 4:
                copy.wait_send()

    def dma(*shape):
        return pltpu.SemaphoreType.DMA(shape)

    most = n_most * n_z
    return pl.pallas_call(
        body,
        out_shape=(
            jax.ShapeDtypeStruct((2, n_x, chunks, height, width), bf16),
            jax.ShapeDtypeStruct((count,) + given.shape[1:], given.dtype),
            jax.ShapeDtypeStruct(vector.shape, vector.dtype),
        ),
        in_specs=[HBM, HBM, VMEM],
        out_specs=(HBM, HBM, VMEM),
        scratch_shapes=[
            pltpu.VMEM((chunks, blocks, height, width), bf16),
            pltpu.VMEM((chunks, blocks, height, width), bf16),
            pltpu.VMEM((chunks, n_most - 1, most, height, width), bf16),
            pltpu.VMEM((chunks, n_most - 1, n_z, height, width), bf16),
            pltpu.VMEM((chunks, n_z - 1, height, width), bf16),
            pltpu.VMEM((2,) + vector.shape, f32),
            pltpu.VMEM((n_x,) + vector.shape, f32),
            pltpu.VMEM((n_y,) + vector.shape, f32),
            pltpu.VMEM((n_z,) + vector.shape, f32),
            dma(chunks),
            dma(chunks),
            dma(chunks),
            dma(chunks, n_most - 1),
            dma(chunks, n_most - 1),
            dma(chunks, n_most - 1),
            dma(chunks, n_most - 1),
            dma(chunks, n_z - 1),
            dma(chunks, n_z - 1),
            dma(chunks, n_x - 1),
            dma(chunks, n_x - 1),
            dma(chunks, n_x),
            dma(chunks, n_x),
            dma(chunks),
            dma(near),
            dma(near),
            dma(near, n_x - 1),
            dma(near, n_x - 1),
            dma(4, max(n_most, n_z) - 1),
            dma(4, max(n_most, n_z) - 1),
            pltpu.SemaphoreType.DMA,
        ],
        compiler_params=pltpu.CompilerParams(
            collective_id=call_id, has_side_effects=True, vmem_limit_bytes=48 << 20
        ),
    )(grads, given, vector)


def read_heads(source, table_low, targets, vocab_part, chunk, n_y, n_z, call_id):
    n_pick, width = source.shape
    size = table_low.shape[0]
    n_dp = n_y * n_z
    chunks = size // chunk

    def body(s_ref, t_ref, target_ref, e_ref, h_ref, m_ref, stat_ref, e_buf, h_buf, t_buf, told, came, *sems):
        z_out, z_in, y_out, y_in, stat_out, stat_in, e_sem, load_sem, h_sem = sems
        dp_at = lax.axis_index("dp")
        z_at, y_at = dp_at // n_y, lax.rem(dp_at, n_y)
        load = pltpu.make_async_copy(t_ref, t_buf, load_sem)
        load.start()
        h_buf[dp_at] = s_ref[...]
        barrier = pltpu.get_barrier_semaphore()

        @pl.loop(1, n_dp)
        def _(step):
            to = lax.rem(dp_at + step, n_dp)
            pl.semaphore_signal(barrier, inc=1, device_id={"dp": to}, device_id_type=MESH)

        pl.semaphore_wait(barrier, n_dp - 1)

        def z_copy(step):
            mine = h_buf.at[dp_at]
            to = lax.rem(z_at + step, n_z) * n_y + y_at
            return pltpu.make_async_remote_copy(
                mine, mine, z_out.at[step], z_in.at[step], device_id={"dp": to}, device_id_type=MESH
            )

        def y_copy(turn, step):
            block = h_buf.at[lax.rem(z_at + n_z - turn, n_z) * n_y + y_at]
            to = z_at * n_y + lax.rem(y_at + step, n_y)
            return pltpu.make_async_remote_copy(
                block,
                block,
                y_out.at[turn, step],
                y_in.at[turn, step],
                device_id={"dp": to},
                device_id_type=MESH,
            )

        for step in range(1, n_y):
            y_copy(0, step).start()
        for step in range(1, n_z):
            z_copy(step).start()
        load.wait()

        def logits(rows, index):
            part = t_buf[index * chunk : (index + 1) * chunk]
            return lax.dot_general(part, rows, (((1,), (1,)), ((), ())), preferred_element_type=f32)

        @pl.loop(0, n_dp)
        def _(turn):
            z_turn, y_turn = turn // n_y, lax.rem(turn, n_y)

            @pl.when((y_turn == 0) & (z_turn > 0))
            def _():
                z_copy(z_turn).wait_recv()
                for step in range(1, n_y):
                    y_copy(z_turn, step).start()

            @pl.when(y_turn > 0)
            def _():
                y_copy(z_turn, y_turn).wait_recv()

            origin = lax.rem(z_at + n_z - z_turn, n_z) * n_y + lax.rem(y_at + n_y - y_turn, n_y)
            rows = h_buf[origin]
            target = target_ref[origin]
            row = lax.broadcasted_iota(i32, (chunk // 8, 8, n_pick), 0) * 8
            row = row + lax.broadcasted_iota(i32, (chunk // 8, 8, n_pick), 1)
            top = summed = hit = None
            ahead = logits(rows, 0)
            for index in range(chunks):
                now = ahead.reshape(chunk // 8, 8, n_pick)
                if index + 1 < chunks:
                    ahead = logits(rows, index + 1)
                first = index * chunk
                if first + chunk > vocab_part:
                    now = jnp.where(row < vocab_part - first, now, -jnp.inf)
                chunk_top = jnp.max(now, axis=0)
                new_top = chunk_top if top is None else jnp.maximum(top, chunk_top)
                grown = jnp.exp(now - new_top[None])
                chunk_sum = jnp.sum(grown, axis=0)
                chunk_hit = jnp.sum(jnp.where(row == (target - first)[None], now, 0.0), axis=0)
                if top is None:
                    summed, hit = chunk_sum, chunk_hit
                else:
                    summed = summed * jnp.exp(top - new_top) + chunk_sum
                    hit = hit + chunk_hit
                top = new_top
                e_buf[origin, first : first + chunk] = grown.reshape(chunk, n_pick).astype(bf16)
                m_ref[origin, index] = top
            best = jnp.max(top, axis=0, keepdims=True)
            told[origin] = jnp.zeros((8, n_pick), f32)
            told[origin, 0:1] = best
            told[origin, 1:2] = jnp.sum(summed * jnp.exp(top - best), axis=0, keepdims=True)
            told[origin, 2:3] = jnp.sum(hit, axis=0, keepdims=True)
            pltpu.make_async_copy(e_buf.at[origin], e_ref.at[origin], e_sem.at[origin]).start()

        def stat_copy(step):
            to = lax.rem(dp_at + step, n_dp)
            return pltpu.make_async_remote_copy(
                told,
                came.at[dp_at],
                stat_out.at[step],
                stat_in.at[step],
                device_id={"dp": to},
                device_id_type=MESH,
            )

        @pl.loop(1, n_dp)
        def _(step):
            stat_copy(step).start()

        came[dp_at] = told[...]
        keep = pltpu.make_async_copy(h_buf, h_ref, h_sem)
        keep.start()
        for step in range(1, n_z):
            z_copy(step).wait_send()
        for turn in range(n_z):
            for step in range(1, n_y):
                y_copy(turn, step).wait_send()

        @pl.loop(0, n_dp)
        def _(origin):
            pltpu.make_async_copy(e_buf.at[origin], e_ref.at[origin], e_sem.at[origin]).wait()

        @pl.loop(1, n_dp)
        def _(step):
            stat_copy(step).wait()

        keep.wait()
        stat_ref[...] = came[...]

    def dma(*shape):
        return pltpu.SemaphoreType.DMA(shape)

    return pl.pallas_call(
        body,
        out_shape=(
            jax.ShapeDtypeStruct((n_dp, size, n_pick), bf16),
            jax.ShapeDtypeStruct((n_dp, n_pick, width), bf16),
            jax.ShapeDtypeStruct((n_dp, chunks, 8, n_pick), f32),
            jax.ShapeDtypeStruct((n_dp, n_dp, 8, n_pick), f32),
        ),
        in_specs=[VMEM, HBM, VMEM],
        out_specs=(HBM, HBM, VMEM, VMEM),
        scratch_shapes=[
            pltpu.VMEM((n_dp, size, n_pick), bf16),
            pltpu.VMEM((n_dp, n_pick, width), bf16),
            pltpu.VMEM((size, width), bf16),
            pltpu.VMEM((n_dp, 8, n_pick), f32),
            pltpu.VMEM((n_dp, n_dp, 8, n_pick), f32),
            dma(n_z),
            dma(n_z),
            dma(n_z, n_y),
            dma(n_z, n_y),
            dma(n_dp),
            dma(n_dp),
            dma(n_dp),
            pltpu.SemaphoreType.DMA,
            pltpu.SemaphoreType.DMA,
        ],
        compiler_params=pltpu.CompilerParams(
            collective_id=call_id, has_side_effects=True, vmem_limit_bytes=56 << 20
        ),
    )(source, table_low, targets)


def write_heads(grown, heads, turned, tops, stats, targets, weights, chunk, n_x, call_id):
    n_dp, size, n_pick = grown.shape
    width = heads.shape[2]
    chunks = size // chunk
    turns = chunks // 2
    part = size // 2 // n_x
    block = math.gcd(chunk, part)

    def body(e_ref, h_ref, t_ref, m_ref, stat_ref, target_ref, w_ref, d_ref, log_ref, *refs):
        part_refs, scratch = refs[:n_x], refs[n_x:]
        buf, t_buf, df_buf, out_buf, got, res = scratch[:6]
        e_sem, t_sem, df_out, df_in, df_own, pair_out, pair_in, res_sem = scratch[6:]
        dp_at, seq_at = lax.axis_index("dp"), lax.axis_index("seq")
        core = lax.rem(seq_at, 2)
        partner = {"seq": seq_at + 1 - 2 * core}
        load = pltpu.make_async_copy(t_ref, t_buf, t_sem)

        def e_copy(turn):
            origin = lax.rem(dp_at + 1 + turn, n_dp)
            return pltpu.make_async_copy(e_ref.at[origin], buf.at[origin], e_sem.at[turn])

        e_copy(0).start()
        load.start()

        @pl.loop(1, n_dp)
        def _(turn):
            e_copy(turn).start()

        barrier = pltpu.get_barrier_semaphore()

        @pl.loop(1, n_dp)
        def _(step):
            to = lax.rem(dp_at + step, n_dp)
            pl.semaphore_signal(barrier, inc=1, device_id={"dp": to}, device_id_type=MESH)

        pl.semaphore_signal(barrier, inc=1, device_id=partner, device_id_type=MESH)

        @pl.loop(0, n_dp)
        def _(origin):
            top = stat_ref[0, origin, 0:1]
            for sender in range(1, n_dp):
                top = jnp.maximum(top, stat_ref[sender, origin, 0:1])
            total = jnp.zeros((1, n_pick), f32)
            hit = jnp.zeros((1, n_pick), f32)
            for sender in range(n_dp):
                total = total + stat_ref[sender, origin, 1:2] * jnp.exp(stat_ref[sender, origin, 0:1] - top)
                hit = hit + stat_ref[sender, origin, 2:3]
            log_ref[0, origin] = top + jnp.log(total)
            log_ref[1, origin] = hit

        load.wait()
        pl.semaphore_wait(barrier, n_dp)

        def df_copy(turn):
            to = lax.rem(dp_at + 1 + turn, n_dp)
            return pltpu.make_async_remote_copy(
                df_buf.at[to],
                d_ref.at[dp_at],
                df_out.at[turn],
                df_in.at[turn],
                device_id={"dp": to},
                device_id_type=MESH,
            )

        @pl.loop(0, n_dp)
        def _(turn):
            origin = lax.rem(dp_at + 1 + turn, n_dp)
            e_copy(turn).wait()
            log_total = log_ref[0, origin]
            weight = w_ref[origin]
            target = target_ref[origin]
            row = lax.broadcasted_iota(i32, (chunk // 8, 8, n_pick), 0) * 8
            row = row + lax.broadcasted_iota(i32, (chunk // 8, 8, n_pick), 1)

            def gradient(index):
                rows = pl.ds(index * chunk, chunk)
                scale = jnp.exp(m_ref[origin, index] - log_total) * weight
                part = buf[origin, rows].astype(f32).reshape(chunk // 8, 8, n_pick) * scale[None]
                at_target = row == (target - index * chunk)[None]
                part = part - jnp.where(at_target, weight[None], 0.0)
                part = part.reshape(chunk, n_pick).astype(bf16)
                buf[origin, rows] = part
                return part

            total = None
            ahead = gradient(0)
            for index in range(chunks):
                now = ahead
                if index + 1 < chunks:
                    ahead = gradient(index + 1)
                columns = t_buf[:, index * chunk : (index + 1) * chunk]
                part = jnp.dot(columns, now, preferred_element_type=f32)
                total = part if total is None else total + part
            df_buf[origin] = total.astype(bf16)

            @pl.when(turn < n_dp - 1)
            def _():
                df_copy(turn).start()

        local = pltpu.make_async_copy(df_buf.at[dp_at], d_ref.at[dp_at], df_own)
        local.start()

        def table_part(index):
            first = pl.multiple_of(index * chunk, chunk)
            part = jnp.concatenate([buf[origin, pl.ds(first, chunk)] for origin in range(n_dp)], axis=1)
            return jnp.dot(part, h_ref[...], preferred_element_type=f32)

        def pair_copy(turn):
            return pltpu.make_async_remote_copy(
                out_buf.at[turn],
                got.at[turn],
                pair_out.at[turn],
                pair_in.at[turn],
                device_id=partner,
                device_id_type=MESH,
            )

        @pl.loop(0, turns)
        def _(turn):
            out_buf[turn] = table_part((1 - core) * turns + turn).astype(bf16)
            pair_copy(turn).start()

        def res_out(turn):
            for index in range(chunk // block):
                at = turn * (chunk // block) + index
                rows = pl.ds(pl.multiple_of(lax.rem(at, part // block) * block, block), block)
                slot = lax.rem(at // (part // block) + n_x - seq_at // 2, n_x)
                for place in range(n_x):

                    @pl.when(slot == place)
                    def _():
                        pltpu.make_async_copy(
                            res.at[turn, pl.ds(index * block, block)], part_refs[place].at[rows], res_sem.at[turn]
                        ).start()

        @pl.loop(0, turns)
        def _(turn):
            total = table_part(core * turns + turn)
            pair_copy(turn).wait()
            res[turn] = (total + got[turn].astype(f32)).astype(bf16)
            res_out(turn)

        @pl.loop(0, turns)
        def _(turn):
            pltpu.make_async_copy(res.at[turn], res.at[turn], res_sem.at[turn]).wait()

        local.wait()

        @pl.loop(0, n_dp - 1)
        def _(turn):
            df_copy(turn).wait()

    def dma(*shape):
        return pltpu.SemaphoreType.DMA(shape)

    return pl.pallas_call(
        body,
        out_shape=(
            jax.ShapeDtypeStruct((n_dp, width, n_pick), bf16),
            jax.ShapeDtypeStruct((2, n_dp, 1, n_pick), f32),
        )
        + (jax.ShapeDtypeStruct((part, width), bf16),) * n_x,
        in_specs=[HBM, VMEM, HBM, VMEM, VMEM, VMEM, VMEM],
        out_specs=(HBM, VMEM) + (HBM,) * n_x,
        scratch_shapes=[
            pltpu.VMEM((n_dp, size, n_pick), bf16),
            pltpu.VMEM((width, size), bf16),
            pltpu.VMEM((n_dp, width, n_pick), bf16),
            pltpu.VMEM((turns, chunk, width), bf16),
            pltpu.VMEM((turns, chunk, width), bf16),
            pltpu.VMEM((turns, chunk, width), bf16),
            dma(n_dp),
            pltpu.SemaphoreType.DMA,
            dma(n_dp),
            dma(n_dp),
            pltpu.SemaphoreType.DMA,
            dma(turns),
            dma(turns),
            dma(turns),
        ],
        compiler_params=pltpu.CompilerParams(
            collective_id=call_id, has_side_effects=True, vmem_limit_bytes=62 << 20
        ),
    )(grown, heads.reshape(n_dp * n_pick, width), turned, tops, stats, targets, weights)


def staged(work, ins, small, outs, temps, limit, buffers_of=(), pieces=None, eager=2):
    n_in, n_small, n_out = len(ins), len(small), len(outs)
    packed, places = ((), {}) if pieces is None else ((pieces[0],), pieces[1])

    def body(*refs):
        packed_refs, refs = refs[: len(packed)], refs[len(packed) :]
        in_refs, small_refs, refs = refs[:n_in], refs[n_in : n_in + n_small], refs[n_in + n_small :]
        out_refs, in_bufs, refs = refs[:n_out], refs[n_out : n_out + n_in], refs[n_out + n_in :]
        out_bufs, (in_sem, out_sem), temp_refs = refs[:n_out], refs[n_out : n_out + 2], refs[n_out + 2 :]
        loads = {}
        names = list(ins)

        def start(at):
            name = names[at]
            loads[name] = pltpu.make_async_copy(in_refs[at], in_bufs[at], in_sem.at[at])
            if name not in places:
                loads[name].start()
                return
            loads[name] = pltpu.make_async_copy(in_bufs[at], in_bufs[at], in_sem.at[at])
            for source, target in places[name]:
                pltpu.make_async_copy(
                    packed_refs[0].at[source], in_bufs[at].at[target], in_sem.at[at]
                ).start()

        for at in range(eager):
            start(at)
        buffers = dict(zip(ins, in_bufs))
        pending, sent = list(ins), []

        def get(name):
            if name in pending:
                pending.remove(name)
                loads[name].wait()
                if name == names[eager - 1]:
                    for at in range(eager, n_in):
                        start(at)
            return buffers[name]

        def put(name, begin=0, count=None):
            at = list(outs).index(name)
            source, target = out_bufs[at], out_refs[at]
            if count is not None:
                source, target = source.at[:, pl.ds(0, count)], target.at[:, pl.ds(begin, count)]
            copy = pltpu.make_async_copy(source, target, out_sem.at[len(sent)])
            copy.start()
            sent.append(copy)
            return copy

        def done(copy):
            copy.wait()
            sent[sent.index(copy)] = None

        work(get, dict(zip(small, small_refs)), dict(zip(outs, out_bufs)), (put, done), temp_refs)
        for name in list(pending):
            get(name)
        for copy in sent:
            if copy is not None:
                copy.wait()

    def scratch(value):
        return pltpu.VMEM(value.shape, value.dtype)

    def refs_of(name, value):
        return jnp.zeros((8, 128), value.dtype) if name in places else value

    return pl.pallas_call(
        body,
        out_shape=tuple(outs.values()),
        in_specs=[HBM] * (len(packed) + n_in) + [VMEM] * n_small,
        out_specs=(HBM,) * n_out,
        scratch_shapes=[scratch(value) for value in ins.values()]
        + [scratch(dict(buffers_of).get(name, value)) for name, value in outs.items()]
        + [pltpu.SemaphoreType.DMA((n_in,)), pltpu.SemaphoreType.DMA((n_out + 2,))]
        + temps,
        compiler_params=pltpu.CompilerParams(vmem_limit_bytes=limit << 20),
        cost_estimate=pl.CostEstimate(flops=0, bytes_accessed=0, transcendentals=0),
    )(*packed, *[refs_of(name, value) for name, value in ins.items()], *small.values())


def dot(left, right, left_dim=1, right_dim=0):
    return lax.dot_general(
        left, right, (((left_dim,), (right_dim,)), ((), ())), preferred_element_type=f32
    )


def norm_parts(x):
    centre = x - jnp.mean(x, axis=-1, keepdims=True)
    scale = lax.rsqrt(jnp.mean(centre * centre, axis=-1, keepdims=True) + 1e-05)
    return centre * scale, scale


def norm_back(x, gain, grad):
    unit, scale = norm_parts(x)
    d_gain = jnp.sum(grad * unit, axis=0, keepdims=True)
    d_shift = jnp.sum(grad, axis=0, keepdims=True)
    inner = grad * gain
    pull = jnp.mean(inner, axis=-1, keepdims=True)
    pull = pull + unit * jnp.mean(inner * unit, axis=-1, keepdims=True)
    return scale * (inner - pull), d_gain, d_shift


def iota(shape, dim):
    return lax.broadcasted_iota(i32, shape, dim)


def flat(ref, columns=slice(None)):
    value = ref[..., columns]
    return value.reshape(-1, value.shape[-1])


def row_block(ref, block, size):
    first = block * size
    if len(ref.shape) == 2:
        return ref[first : first + size]
    _, inner, rows, _ = ref.shape
    if inner * rows <= size:
        per = inner * rows
        return flat(ref[first // per : (first + size) // per])
    owner, first = divmod(first, inner * rows)
    return flat(ref[owner, first // rows : (first + size) // rows])


def split_three(x):
    high = x.astype(bf16)
    rest = x - high.astype(f32)
    middle = rest.astype(bf16)
    return high, middle, (rest - middle.astype(f32)).astype(bf16)


def layer_forward(embedded, pos, w_in, w_out, w_up, w_down, vectors, picks, row_length, pieces):
    length, model = embedded.shape
    n_pick = picks.shape[0]
    lanes = 128
    groups = model // lanes
    head_dim = model // H
    per = lanes // head_dim

    def work(get, small, out, moves, temps):
        put, _ = moves
        vec = small["vectors"]
        v_turned, o_turned = temps
        emb, pos_rows = get("emb"), get("pos")
        start = emb[...].astype(f32) + flat(pos_rows).astype(f32)
        unit, _ = norm_parts(start)
        out["a"][...] = (unit * vec[0:1] + vec[1:2]).astype(bf16)
        put("a")
        chosen = jnp.where(small["pick_col"][...] - 1 == iota((n_pick, length), 1), 1.0, 0.0).astype(bf16)
        start_picked = dot(chosen, emb[...]) + dot(chosen, flat(pos_rows))
        w = get("w_in")
        out["k"][...] = dot(out["a"][...], flat(w, slice(model, 2 * model))).astype(bf16)
        put("k")
        out["v"][...] = (dot(out["a"][...], flat(w, slice(2 * model, 3 * model))) + vec[7:8]).astype(bf16)
        put("v")
        a_picked = dot(chosen, out["a"][...]).astype(bf16)
        out["q"][...] = (dot(a_picked, flat(w, slice(0, model))) + vec[6:7]).astype(bf16)
        put("q")
        keep = iota((length, n_pick), 0) < small["length"][0, 0]

        @pl.loop(0, groups)
        def _(group):
            place = pl.ds(pl.multiple_of(group * lanes, lanes), lanes)
            v_turned[...] = out["v"][:, place].T
            q_pair, k_pair = out["q"][:, place], out["k"][:, place]
            mixed = None
            for j in range(per):
                q_head = jnp.where(iota((n_pick, lanes), 1) // head_dim == j, q_pair, jnp.zeros_like(q_pair))
                score = jnp.where(keep, dot(k_pair, q_head, 1, 1) * 0.125, mask_fill)
                top = jnp.max(score, axis=0, keepdims=True)
                grown = jnp.exp(score - top)
                total = jnp.sum(grown, axis=0, keepdims=True)
                out["lse"][group * per + j] = top + jnp.log(total)
                probs = (grown * (1.0 / total)).astype(bf16)
                part = dot(v_turned[...], probs)
                mixed = part if mixed is None else jnp.where(iota((lanes, n_pick), 0) // head_dim == j, part, mixed)
            o_turned[pl.ds(pl.multiple_of(group * lanes, lanes), lanes)] = mixed

        out["o"][...] = o_turned[...].T.astype(bf16)
        put("lse")
        put("o")
        x1 = start_picked + dot(out["o"][...], flat(get("w_out"))) + vec[8:9]
        out["x1"][...] = x1
        put("x1")
        unit, _ = norm_parts(x1)
        out["m"][...] = (unit * vec[2:3] + vec[3:4]).astype(bf16)
        put("m")
        up, down = get("w_up"), get("w_down")
        x2 = x1 + vec[9:10]
        for block in range(up.shape[-1] // model):
            place = slice(block * model, (block + 1) * model)
            u1 = dot(out["m"][...], flat(up, place)) + vec[10 + block : 11 + block]
            x2 = x2 + dot(gelu_fn(u1).astype(bf16), row_block(down, block, model))
        out["x2"][...] = x2
        put("x2")
        unit, _ = norm_parts(x2)
        out["f"][...] = (unit * vec[4:5] + vec[5:6]).astype(bf16)
        put("f")

    def shape(rows, dtype):
        return jax.ShapeDtypeStruct((rows, model), dtype)

    outs = {
        "a": shape(length, bf16),
        "k": shape(length, bf16),
        "v": shape(length, bf16),
        "q": shape(n_pick, bf16),
        "lse": jax.ShapeDtypeStruct((H, 1, n_pick), f32),
        "o": shape(n_pick, bf16),
        "x1": shape(n_pick, f32),
        "m": shape(n_pick, bf16),
        "x2": shape(n_pick, f32),
        "f": shape(n_pick, bf16),
    }
    values = staged(
        work,
        {"emb": embedded, "pos": pos, "w_in": w_in, "w_out": w_out, "w_up": w_up, "w_down": w_down},
        {"vectors": vectors, "pick_col": picks[:, None], "length": row_length.reshape(1, 1)},
        outs,
        [pltpu.VMEM((lanes, length), bf16), pltpu.VMEM((model, n_pick), f32)],
        60,
        pieces=pieces,
    )
    return dict(zip(outs, values))


def layer_backward(
    final_grad, kept, embedded, pos, weights, vectors, picks, spots, row_length, loss, n_dp, pieces
):
    length, model = embedded.shape
    n_pick = picks.shape[0]
    lanes = 128
    groups = model // lanes
    head_dim = model // H
    per = lanes // head_dim
    w_in, w_out, w_up, w_down = weights
    hidden = w_up.shape[-1]
    thick, long, n_place = model // n_dp, hidden // n_dp, spots[1]
    wide = hidden // model
    first_rows = 2 * long
    last_rows = 4 * thick + length // n_dp

    def work(get, small, out, moves, temps):
        put, done = moves
        vec, d_vec = small["vectors"], out["vec"]
        dqkv, dq, d_mixed = temps
        whole = out["whole"]

        def rows_of(first, count, values):
            values = values.astype(bf16)
            for owner in range(n_dp):
                whole[owner, first : first + count] = values[owner * count : (owner + 1) * count]

        x2, dfin = get("x2"), get("dfin")
        dx2, d_vec[4:5], d_vec[5:6] = norm_back(x2[...], vec[4:5], dfin[...])
        dy2 = dx2.astype(bf16)
        d_vec[9:10] = jnp.sum(dy2.astype(f32), axis=0, keepdims=True)
        m, up, down = get("m"), get("w_up"), get("w_down")
        m_turned = m[...].T
        dm = None
        for block in range(wide):
            place = slice(block * model, (block + 1) * model)
            u1 = dot(m[...], flat(up, place)) + vec[10 + block : 11 + block]
            act, gelu_back = jax.vjp(gelu_fn, u1)
            part = dot(act.astype(bf16).T, dy2).astype(bf16)
            run = min(long, model)
            for at in range(0, model, run):
                owner, row = divmod(block * model + at, long)
                whole[owner, row : row + run] = part[at : at + run]
            du1 = gelu_back(dot(dy2, row_block(down, block, model), 1, 1))[0].astype(bf16)
            d_vec[10 + block : 11 + block] = jnp.sum(du1.astype(f32), axis=0, keepdims=True)
            rows_of(long + block * thick, thick, dot(m_turned, du1))
            part = dot(du1, flat(up, place), 1, 1)
            dm = part if dm is None else dm + part
        first_out = put("whole", 0, first_rows)
        dx1, d_vec[2:3], d_vec[3:4] = norm_back(get("x1")[...], vec[2:3], dm)
        dx1 = dx2 + dx1
        dy1 = dx1.astype(bf16)
        d_vec[8:9] = jnp.sum(dy1.astype(f32), axis=0, keepdims=True)
        done(first_out)
        rows_of(0, thick, dot(get("o")[...].T, dy1))
        d_mixed[...] = dot(dy1, flat(get("w_out")), 1, 1).astype(bf16)
        keep = iota((length, n_pick), 0) < small["length"][0, 0]
        q, k, v, lse = get("q"), get("k"), get("v"), small["lse"]

        @pl.loop(0, groups)
        def _(group):
            def place(part):
                return pl.ds(pl.multiple_of(part * model + group * lanes, lanes), lanes)

            q_pair, k_pair, v_pair, d_pair = q[:, place(0)], k[:, place(0)], v[:, place(0)], d_mixed[:, place(0)]
            k_turned = k_pair.T
            sums = None
            for j in range(per):
                lane = iota((n_pick, lanes), 1) // head_dim == j
                q_head = jnp.where(lane, q_pair, jnp.zeros_like(q_pair))
                d_head = jnp.where(lane, d_pair, jnp.zeros_like(d_pair))
                score = jnp.where(keep, dot(k_pair, q_head, 1, 1) * 0.125, mask_fill)
                probs = jnp.exp(score - lse[group * per + j])
                dp = dot(v_pair, d_head, 1, 1)
                ds = (probs * (dp - jnp.sum(dp * probs, axis=0, keepdims=True))).astype(bf16)
                parts = (dot(k_turned, ds), dot(ds, q_pair), dot(probs.astype(bf16), d_pair))
                if sums is None:
                    sums = parts
                else:
                    rows = iota((lanes, n_pick), 0) // head_dim == j
                    columns = iota((length, lanes), 1) // head_dim == j
                    sums = (
                        jnp.where(rows, parts[0], sums[0]),
                        jnp.where(columns, parts[1], sums[1]),
                        jnp.where(columns, parts[2], sums[2]),
                    )
            dq[:, place(0)] = (sums[0] * 0.125).T.astype(bf16)
            dqkv[:, place(1)] = (sums[1] * 0.125).astype(bf16)
            dqkv[:, place(2)] = sums[2].astype(bf16)

        chosen = jnp.where(small["pick_row"][...] - 1 == iota((length, n_pick), 0), 1.0, 0.0).astype(bf16)
        dqkv[:, :model] = dot(chosen, dq[...]).astype(bf16)
        d_vec[6:7] = jnp.sum(dq[...].astype(f32), axis=0, keepdims=True)
        d_vec[7:8] = jnp.sum(dqkv[:, 2 * model :].astype(f32), axis=0, keepdims=True)
        a_turned = get("a")[...].T
        for part in range(3):
            rows_of((1 + part) * thick, thick, dot(a_turned, dqkv[:, part * model : (part + 1) * model]))
        da = dot(dqkv[...], flat(get("w_in")), 1, 1)
        start = get("emb")[...].astype(f32) + flat(get("pos")).astype(f32)
        dx0, d_vec[0:1], d_vec[1:2] = norm_back(start, vec[0:1], da)
        for part in split_three(dx1):
            dx0 = dx0 + dot(chosen, part)
        rows_of(4 * thick, length // n_dp, dx0)
        put("whole", first_rows, last_rows)
        d_vec[14:15] = small["loss"][...]
        d_vec[15:16] = jnp.zeros((1, model), f32)
        put("vec")
        out["low"][...] = dx0.astype(bf16)
        put("low")
        step = min(n_place, 512)
        for first in range(0, n_place, step):
            where = jnp.where(small["spots"][...] == iota((step, length), 0) + first, 1.0, 0.0).astype(bf16)
            out["given"][first : first + step] = dot(where, out["low"][...]).astype(bf16)
        put("given")

    outs = {
        "whole": jax.ShapeDtypeStruct((n_dp, first_rows + last_rows, model), bf16),
        "vec": jax.ShapeDtypeStruct((16, model), f32),
        "low": jax.ShapeDtypeStruct((length, model), bf16),
        "given": jax.ShapeDtypeStruct((n_place, model), bf16),
    }
    ins = {
        "x2": kept["x2"],
        "dfin": final_grad,
        "m": kept["m"],
        "w_up": w_up,
        "w_down": w_down,
        "x1": kept["x1"],
        "o": kept["o"],
        "w_out": w_out,
        "q": kept["q"],
        "k": kept["k"],
        "v": kept["v"],
        "a": kept["a"],
        "w_in": w_in,
        "emb": embedded,
        "pos": pos,
    }
    small = {
        "vectors": vectors,
        "lse": kept["lse"],
        "pick_row": picks[None, :],
        "spots": spots[0][None, :],
        "length": row_length.reshape(1, 1),
        "loss": jnp.full((1, model), loss),
    }
    temps = [
        pltpu.VMEM((length, 3 * model), bf16),
        pltpu.VMEM((n_pick, model), bf16),
        pltpu.VMEM((n_pick, model), bf16),
    ]
    buffer = jax.ShapeDtypeStruct((n_dp, max(first_rows, last_rows), model), bf16)
    return staged(work, ins, small, outs, temps, 62, {"whole": buffer}, pieces, 5)


def table_forms(table, size, chunk):
    count, width = table.shape

    def body(t_ref, low_ref, turned_ref):
        row = iota((chunk, width), 0) + pl.program_id(0) * chunk
        value = jnp.where(row < count, t_ref[...], 0.0)
        low_ref[...] = value.astype(bf16)
        turned_ref[...] = value.T.astype(bf16)

    return pl.pallas_call(
        body,
        grid=(size // chunk,),
        in_specs=[pl.BlockSpec((chunk, width), lambda step: (step, 0))],
        out_specs=(
            pl.BlockSpec((chunk, width), lambda step: (step, 0)),
            pl.BlockSpec((width, chunk), lambda step: (0, step)),
        ),
        out_shape=(
            jax.ShapeDtypeStruct((size, width), bf16),
            jax.ShapeDtypeStruct((width, size), bf16),
        ),
        compiler_params=pltpu.CompilerParams(vmem_limit_bytes=32 << 20),
    )(table)


def close_half(own, other, names, values, layer, share, tile):
    half, width = own.shape
    count = min(names.shape[1], 2048)
    parts = names.shape[1] // count

    def body(own_ref, other_ref, names_ref, values_ref, layer_ref, o_ref, square_ref, total):
        step, part = pl.program_id(0), pl.program_id(1)

        @pl.when(part == 0)
        def _():
            total[...] = own_ref[...].astype(f32) + other_ref[...].astype(f32)

        row = iota((tile, count), 0) + step * tile
        where = jnp.where(row == names_ref[...], 1.0, 0.0).astype(bf16)
        total[...] += jnp.dot(where, values_ref[...], preferred_element_type=f32)

        @pl.when((step == 0) & (part == 0))
        def _():
            layer_part = layer_ref[...].astype(f32)
            square_ref[...] = jnp.sum(layer_part * layer_part, axis=0, keepdims=True) * share

        @pl.when(part == parts - 1)
        def _():
            o_ref[...] = total[...].astype(bf16)
            square_ref[...] += jnp.sum(total[...] * total[...], axis=0, keepdims=True)

    rows = pl.BlockSpec((tile, width), lambda step, part: (step, 0))
    return pl.pallas_call(
        body,
        grid=(half // tile, parts),
        in_specs=[
            rows,
            rows,
            pl.BlockSpec((1, count), lambda step, part: (0, part)),
            pl.BlockSpec((count, width), lambda step, part: (part, 0)),
            pl.BlockSpec(layer.shape, lambda step, part: (0, 0)),
        ],
        out_specs=(rows, pl.BlockSpec((1, width), lambda step, part: (0, 0))),
        out_shape=(jax.ShapeDtypeStruct((half, width), bf16), jax.ShapeDtypeStruct((1, width), f32)),
        scratch_shapes=[pltpu.VMEM((tile, width), f32)],
        compiler_params=pltpu.CompilerParams(vmem_limit_bytes=48 << 20),
        cost_estimate=pl.CostEstimate(flops=0, bytes_accessed=0, transcendentals=0),
    )(own, other, names, values, layer)


def adam_table(at, squares, vector, weights, mine, other, tile, half, n_x, steps, done):
    size, width = weights[0].shape
    per_half, per_part = half // tile, half // n_x // tile
    turns = len(steps) * per_part
    first_step = steps[0]

    def body(at_ref, square_ref, vec_ref, w_ref, m_ref, v_ref, mine_ref, other_ref, *refs):
        new_w, new_m, new_v, token, factor = refs[-5:]

        @pl.when(pl.program_id(0) == 0)
        def _():
            squares = jnp.sum(square_ref[...], axis=0)[0:1, 0:1]
            row = jnp.sum(vec_ref[...] * vec_ref[...], axis=0, keepdims=True)
            norm = jnp.sqrt(squares + jnp.sum(row, axis=1, keepdims=True))
            factor[...] = jnp.broadcast_to(clip_at / jnp.maximum(norm, clip_at), factor.shape)
            token[...] = jnp.zeros_like(token)

        from_mine = pl.program_id(0) < turns
        grad = jnp.where(from_mine, mine_ref[...], other_ref[...]).astype(f32) * factor[0:1, 0:1]
        new_w[...], new_m[...], new_v[...] = adam_update(
            w_ref[...], grad, m_ref[...], v_ref[...], 0.1, 0.1
        )

    def row_at(step, at_ref):
        core = lax.rem(at_ref[0] + step // turns, 2)
        turn = lax.rem(step, turns)
        x = lax.rem(at_ref[1] + n_x - (first_step + turn // per_part), n_x)
        return (core * per_half + x * per_part + lax.rem(turn, per_part), 0)

    def mine_at(step, at_ref):
        return (jnp.minimum(step, turns - 1), 0)

    def other_at(step, at_ref):
        return (jnp.maximum(step - turns, 0), 0)

    rows = pl.BlockSpec((tile, width), row_at)
    done = () if done is None else done
    return pl.pallas_call(
        body,
        grid_spec=pltpu.PrefetchScalarGridSpec(
            num_scalar_prefetch=1,
            grid=(2 * turns,),
            in_specs=[VMEM, VMEM, rows, rows, rows, pl.BlockSpec((tile, width), mine_at), pl.BlockSpec((tile, width), other_at)]
            + [HBM] * len(done),
            out_specs=(rows, rows, rows, pl.BlockSpec((8, 128), lambda *_: (0, 0))),
            scratch_shapes=[pltpu.VMEM((8, 128), f32)],
        ),
        out_shape=(jax.ShapeDtypeStruct((size, width), f32),) * 3 + (jax.ShapeDtypeStruct((8, 128), f32),),
        input_output_aliases={8 + index: index for index in range(len(done))},
        compiler_params=pltpu.CompilerParams(vmem_limit_bytes=56 << 20),
        cost_estimate=pl.CostEstimate(flops=0, bytes_accessed=0, transcendentals=0),
    )(at, squares, vector, *weights, mine, other, *done)


def update_layer(factor, grads, weights, firsts, seconds):
    steps = 4 if all(weight.shape[0] % 32 == 0 for weight in weights) else 1
    count = len(weights)

    def body(factor_ref, *refs):
        grad_refs, refs = refs[:count], refs[count:]
        ins, outs, token = refs[: 3 * count], refs[3 * count : 6 * count], refs[6 * count]
        token[...] = jnp.zeros_like(token)
        for index, grad in enumerate(grad_refs):
            for block in range(grad.shape[0]):
                columns = slice(block * grad.shape[2], (block + 1) * grad.shape[2])
                w, m, v = (ins[index + kind * count][:, columns] for kind in range(3))
                new = adam_update(w, grad[block] * factor_ref[0:1, 0:1], m, v, 0.1, 0.1)
                for kind in range(3):
                    outs[index + kind * count][:, columns] = new[kind]

    def rows(value):
        return pl.BlockSpec((value.shape[0] // steps, value.shape[1]), lambda step: (step, 0))

    def blocks(value):
        return pl.BlockSpec((value.shape[0], value.shape[1] // steps, value.shape[2]), lambda step: (0, step, 0))

    states = (*weights, *firsts, *seconds)
    *news, token = pl.pallas_call(
        body,
        grid=(steps,),
        in_specs=[VMEM] + [blocks(grad) for grad in grads] + [rows(value) for value in states],
        out_specs=tuple(rows(value) for value in states) + (pl.BlockSpec((8, 128), lambda step: (0, 0)),),
        out_shape=tuple(jax.ShapeDtypeStruct(value.shape, f32) for value in states)
        + (jax.ShapeDtypeStruct((8, 128), f32),),
        compiler_params=pltpu.CompilerParams(vmem_limit_bytes=56 << 20),
        cost_estimate=pl.CostEstimate(flops=0, bytes_accessed=0, transcendentals=0),
    )(factor, *grads, *states)
    return [news[index::count] for index in range(count)], token


def layer_norm(x, gain, shift):
    centre = x - jnp.mean(x, axis=-1, keepdims=True)
    var = jnp.mean(centre * centre, axis=-1, keepdims=True)
    return centre * lax.rsqrt(var + 1e-05) * gain + shift


def gelu_fn(x):
    return jax.nn.gelu(x, approximate=True)


def adam_update(weight, grad, first, second, rate, decay):
    first_new = beta_one * first + (1.0 - beta_one) * grad
    second_new = beta_two * second + (1.0 - beta_two) * grad * grad
    mhat = first_new / (1.0 - beta_one**STEP)
    vhat = second_new / (1.0 - beta_two**STEP)
    return (
        weight - rate * (mhat / (jnp.sqrt(vhat) + adam_eps) + decay * weight),
        first_new,
        second_new,
    )


def as_rows(flat):
    return jnp.pad(flat, (0, -flat.size % 1024)).reshape(-1, 128)


def on_device(
    clean_ids,
    lengths,
    masked,
    attn_in,
    attn_out,
    mlp_in,
    mlp_out,
    table,
    positions,
    vectors,
    first_attn_in,
    first_attn_out,
    first_mlp_in,
    first_mlp_out,
    first_table,
    first_positions,
    first_vectors,
    second_attn_in,
    second_attn_out,
    second_mlp_in,
    second_mlp_out,
    second_table,
    second_positions,
    second_vectors,
):
    rows, slots = clean_ids.shape
    n_dp = lax.axis_size("dp")
    n_seq = lax.axis_size("seq")
    dp_at = lax.axis_index("dp")
    seq_at = lax.axis_index("seq")
    core = lax.rem(seq_at, 2)
    length = slots * n_seq
    vocab_part, model = table.shape
    vocab = vocab_part * n_dp
    head_dim = model // H
    sharers = max(1, n_seq // rows)
    n_pick = masked.shape[1] // sharers
    row_at = seq_at // sharers
    share = lax.rem(seq_at, sharers)
    half = -(-vocab_part // 256) * 128
    tile = 128 * max(count for count in range(1, 8) if half % (128 * count) == 0)
    n_x = n_seq // 2
    n_y = 1 << (n_dp.bit_length() - 1) // 2
    n_z = n_dp // n_y

    def piece_of(weight):
        piece = weight.shape[0] // n_seq
        return lax.dynamic_slice_in_dim(weight, seq_at * piece, piece, 0).astype(bf16)

    thick = attn_in.shape[0]
    hidden = mlp_in.shape[1]
    blocks = 4
    split = n_seq // blocks
    thin = thick // split

    def block_of(weights):
        wide = [weight[:, at : at + model] for weight in weights for at in range(0, weight.shape[1], model)]
        wide = jnp.stack(wide).reshape(n_seq, thin, model)
        return lax.dynamic_index_in_dim(wide, seq_at, 0, False).astype(bf16)

    given_rows = [block_of((attn_in, attn_out)), block_of((mlp_in,)), piece_of(mlp_out), piece_of(positions)]
    ends = [0]
    for piece in given_rows:
        ends.append(ends[-1] + piece.shape[0])
    long, some = ends[3] - ends[2], ends[4] - ends[3]
    packed = lax.all_gather(jnp.concatenate(given_rows), ("dp", "seq")).reshape(n_dp, n_seq, -1, model)
    if thin % 16 == 0 and some % 16 == 0 and split == 1:

        def rows_at(part):
            return pl.ds(ends[part], ends[part + 1] - ends[part])

        def blocks_at(part, blocks):
            return [
                ((slice(None), block, rows_at(part)), (slice(None), slice(None), pl.ds(at * model, model)))
                for at, block in enumerate(blocks)
            ]

        def all_at(part):
            return [((slice(None), slice(None), rows_at(part)), (slice(None),))]

        weight_pieces = (
            packed,
            {
                "pos": all_at(3),
                "w_in": blocks_at(0, range(3)),
                "w_out": blocks_at(0, [3]),
                "w_up": blocks_at(1, range(4)),
                "w_down": all_at(2),
            },
        )

        def shape(*dims):
            return jax.ShapeDtypeStruct(dims, bf16)

        pos_all, w_in, w_out = shape(n_dp, n_seq, some, model), shape(n_dp, thick, 3 * model), shape(n_dp, thick, model)
        w_up, w_down = shape(n_dp, thick, hidden), shape(n_dp, n_seq, long, model)
    else:
        weight_pieces = None

        def columns_of(part, block):
            got = packed[:, block * split : (block + 1) * split, ends[part] : ends[part + 1]]
            return got.reshape(-1, model)

        w_in = jnp.concatenate([columns_of(0, block) for block in range(3)], axis=1)
        w_out = columns_of(0, 3)
        w_up = jnp.concatenate([columns_of(1, block) for block in range(4)], axis=1)
        w_down = packed[:, :, ends[2] : ends[3]].reshape(hidden, model)
        pos_all = packed[:, :, ends[3] :].reshape(length, model)

    all_rows = deliver(clean_ids, ("seq",), 1)
    row_ids = lax.dynamic_index_in_dim(all_rows, row_at, 1, keepdims=False).reshape(length)
    row = dp_at * rows + row_at
    row_length = lax.dynamic_index_in_dim(lengths, row, 0, keepdims=False)
    row_masked = lax.dynamic_index_in_dim(masked, row, 0, keepdims=False)
    picks = lax.dynamic_slice_in_dim(row_masked, share * n_pick, n_pick, 0)
    slot = jnp.arange(length, dtype=i32)
    is_masked = jnp.any(slot[:, None] == row_masked[None, :], axis=1)
    noisy = jnp.where(is_masked, vocab - 1, row_ids)
    targets = jnp.sum(jnp.where(picks[:, None] == slot[None, :], row_ids[None, :], 0), axis=1)
    valid_all = ((masked >= 1) & (masked < lengths[:, None])).astype(f32)
    masked_count = jnp.sum(valid_all)

    owner = noisy // vocab_part
    within = noisy - owner * vocab_part
    owner_half = owner * 2 + (within >= half).astype(i32)
    within_half = jnp.where(within >= half, within - half, within)
    same = noisy[:, None] == noisy[None, :]
    leader = jnp.min(jnp.where(same, slot[None, :], length), axis=1)
    leads = leader == slot
    before = (slot[None, :] < slot[:, None]) & leads[None, :]
    rank = jnp.sum((before & (owner[:, None] == owner[None, :])).astype(i32), axis=1)
    rank_half = jnp.sum((before & (owner_half[:, None] == owner_half[None, :])).astype(i32), axis=1)
    lead_of = leader[:, None] == slot[None, :]
    place = jnp.sum(jnp.where(lead_of, rank[None, :], 0), axis=1)
    place_half = jnp.sum(jnp.where(lead_of, rank_half[None, :], 0), axis=1)

    def asked(owners, ranks, names, count, size, turn):
        spot = jnp.where(ranks // size == turn, owners * size + lax.rem(ranks, size), -1)
        spots = jnp.arange(count * size, dtype=i32)
        listed = leads[None, :] & (spots[:, None] == spot[None, :])
        return spot, jnp.sum(jnp.where(listed, names[None, :], 0), axis=1)

    spot, ask = asked(owner, place, within, n_dp, FETCH, 0)
    spot_half, ask_half = asked(owner_half, place_half, within_half, 2 * n_dp, GIVE, 0)
    turns = jnp.stack([jnp.max(place) // FETCH + 1, jnp.max(place_half) // GIVE + 1])
    pieces = [as_rows(piece) for piece in (ask, ask_half, targets, turns)]
    ends = [0]
    for piece in pieces:
        ends.append(ends[-1] + piece.shape[0])
    told = deliver(jnp.concatenate(pieces), ("dp", "seq"), 2)

    def heard(index, size):
        return told[:, ends[index] : ends[index + 1]].reshape(n_dp * n_seq, -1)[:, :size]

    turns = jnp.max(heard(3, 2), axis=0)
    asks = lax.dynamic_index_in_dim(heard(0, n_dp * FETCH).reshape(n_dp, n_seq, n_dp, FETCH), seq_at, 1, False)
    asks = lax.dynamic_index_in_dim(asks, dp_at, 1, False)
    half_at = dp_at * 2 + core
    asks_half = lax.dynamic_index_in_dim(heard(1, 2 * n_dp * GIVE).reshape(-1, 2 * n_dp, GIVE), half_at, 1, False)
    all_targets = lax.dynamic_index_in_dim(heard(2, n_pick).reshape(n_dp, n_seq, n_pick), seq_at, 1, False)

    def one_hot(spots, count):
        return (spots[:, None] == jnp.arange(count, dtype=i32)[None, :]).astype(bf16)

    table_low, table_turned = table_forms(table, 2 * half, tile)
    found = jnp.take(table_low, asks, axis=0)
    fetched = deliver(found, ("dp",), 3, lambda place: place[0]).reshape(n_dp * FETCH, model)
    embedded = jnp.dot(one_hot(spot, n_dp * FETCH), fetched, preferred_element_type=f32)

    def fetch_more(state):
        turn, total = state
        next_spot, next_ask = asked(owner, place, within, n_dp, FETCH, turn)
        wanted = lax.all_to_all(next_ask.reshape(n_dp, FETCH), "dp", 0, 0)
        sent = jnp.take(table_low, wanted, axis=0)
        got = lax.all_to_all(sent, "dp", 0, 0).reshape(n_dp * FETCH, model)
        return turn + 1, total + jnp.dot(one_hot(next_spot, n_dp * FETCH), got, preferred_element_type=f32)

    _, embedded = lax.while_loop(lambda state: state[0] < turns[0], fetch_more, (jnp.int32(1), embedded))

    embedded = embedded.astype(bf16)
    kept = layer_forward(
        embedded, pos_all, w_in, w_out, w_up, w_down, vectors, picks, row_length, weight_pieces
    )
    sources = kept["f"]

    flat_targets = (all_targets - dp_at * vocab_part).reshape(n_dp, 1, n_pick)
    flat_targets = jnp.where(flat_targets < vocab_part, flat_targets, -1)
    rows_here = valid_all.reshape(n_dp, rows, sharers, n_pick)
    rows_here = lax.dynamic_index_in_dim(rows_here, row_at, 1, False)
    flat_valid = lax.dynamic_index_in_dim(rows_here, share, 1, False).reshape(n_dp, 1, n_pick)
    grown, heads, tops, stats = read_heads(
        sources, table_low, flat_targets, vocab_part, tile, n_y, n_z, 9
    )
    final_grad, logs, *half_parts = write_heads(
        grown, heads, table_turned, tops, stats, flat_targets, flat_valid / masked_count, tile, n_x, 5
    )
    loss_group = jnp.sum(flat_valid * (logs[0] - logs[1]))
    final_grad = jnp.sum(final_grad.astype(f32), axis=0).T
    part = half // n_x
    slab = 16 * max(count for count in range(1, 26) if part % (16 * count) == 0)
    x_at = seq_at // 2

    part_came = [from_peer(half_parts[step], "seq", 2, n_x, step) for step in range(1, n_x)]
    if n_x > 2:
        part_came = [sum(came.astype(f32) for came in part_came).astype(bf16)]

    whole, vec_grad, start_grad_low, first_given = layer_backward(
        final_grad,
        kept,
        embedded,
        pos_all,
        (w_in, w_out, w_up, w_down),
        vectors,
        picks,
        (spot_half, 2 * n_dp * GIVE),
        row_length,
        loss_group,
        n_dp,
        weight_pieces,
    )

    def given(spots):
        summed_ids = jnp.einsum(
            "ts,td->sd", one_hot(spots, 2 * n_dp * GIVE), start_grad_low, preferred_element_type=f32
        )
        return summed_ids.astype(bf16).reshape(2 * n_dp, GIVE, model)

    chunks = 5
    layer_sum, came, vec_total = settle(
        whole.reshape(n_dp, 2, n_x, chunks, -1, model),
        first_given.reshape(2 * n_dp, GIVE, model),
        vec_grad,
        n_x,
        n_y,
        n_z,
        7,
    )
    layer_sum = layer_sum.reshape(-1, model)

    def give_more(state):
        turn, total, _ = state
        next_spot, next_ask = asked(owner_half, place_half, within_half, 2 * n_dp, GIVE, turn)
        names = lax.all_gather(next_ask.reshape(2 * n_dp, GIVE), ("dp", "seq"))
        names = lax.dynamic_index_in_dim(names, half_at, 1, False).reshape(1, -1) - x_at * part
        sent = given(next_spot).reshape(n_dp, 1, 2, GIVE, model)
        sent = jnp.broadcast_to(sent, (n_dp, n_x, 2, GIVE, model)).reshape(-1, GIVE, model)
        got = lax.all_to_all(sent, ("dp", "seq"), 0, 0).reshape(-1, model)
        total, squares = close_half(
            total, jnp.zeros_like(total), names, got, layer_sum, 1.0 / n_seq, slab
        )
        return turn + 1, total, jnp.sum(squares)

    names = asks_half.reshape(1, -1) - x_at * part
    values = came.reshape(-1, model)
    part_own, squares_own = close_half(
        half_parts[0], part_came[0], names, values, layer_sum, 1.0 / n_seq, slab
    )
    _, part_own, part_square = lax.while_loop(
        lambda state: state[0] < turns[1], give_more, (jnp.int32(1), part_own, jnp.sum(squares_own))
    )
    loss_sum = vec_total[14, 0] / n_dp
    vec_total = vec_total[:14]

    said = jnp.where(jnp.arange(8)[:, None] == 0, part_square, jnp.zeros((8, 128), f32))
    told_squares = deliver(said, ("seq",), 8)
    zero = told_squares[0, 1, 0].astype(bf16)
    far_out = part_own + zero
    far_own = [from_peer(far_out, "seq", 2, n_x, step) for step in range(1, n_x)]
    far_own = far_own[0] if n_x == 2 else jnp.concatenate(far_own)
    part_pair = from_peer(part_own, "seq", 1, 2, 1)
    told_squares = deliver(jnp.sum(told_squares, axis=0), ("dp",), 4)
    square_total = jnp.sum(told_squares[:, 0, 0])
    grad_norm = jnp.sqrt(square_total + jnp.sum(vec_total * vec_total))
    factor = clip_at / jnp.maximum(grad_norm, clip_at)
    state = (table, first_table, second_table)
    at = jnp.stack([core, x_at])
    *near, token = adam_table(
        at, told_squares, vec_total, state, part_own, part_pair, slab, half, n_x, (0,), None
    )
    layer_sum = layer_sum.astype(f32)
    ends = [0]
    for count in (mlp_out.shape[0], hidden // model * thick, thick, 3 * thick, positions.shape[0]):
        ends.append(ends[-1] + count)
    g_down, g_up, g_out, g_in, g_pos = [layer_sum[begin:end] for begin, end in zip(ends, ends[1:])]
    layer_grads = (
        g_in.reshape(3, thick, model),
        g_out[None],
        g_up.reshape(-1, thick, model),
        g_down[None],
        g_pos[None],
    )
    updates, layer_token = update_layer(
        (factor + token[0, 0]).reshape(1, 1),
        layer_grads,
        (attn_in, attn_out, mlp_in, mlp_out, positions),
        (first_attn_in, first_attn_out, first_mlp_in, first_mlp_out, first_positions),
        (second_attn_in, second_attn_out, second_mlp_in, second_mlp_out, second_positions),
    )
    results = dict(zip((0, 1, 2, 3, 5), updates))
    results[6] = adam_update(vectors, vec_total * factor, first_vectors, second_vectors, 1.0, 0.0)
    far_own = far_own + (token[0, 0] + layer_token[0, 0]).astype(bf16)
    far_pair = from_peer(far_own, "seq", 1, 2, 1)
    far_steps = tuple(range(1, n_x))
    *results[4], _ = adam_table(
        at, told_squares, vec_total, state, far_own, far_pair, slab, half, n_x, far_steps, near
    )
    news, moments, squares = zip(*(results[index] for index in range(7)))
    return (*news, *moments, *squares, loss_sum, masked_count, grad_norm)


def solution(mesh):
    part = P("dp", None)
    six = (part,) * 6 + (P(),)
    return jax.shard_map(
        on_device,
        mesh=mesh,
        in_specs=(P("dp", "seq"), P(), P()) + six * 3,
        out_specs=six * 3 + (P(), P(), P()),
        check_vma=False,
    )
```

```python
import math

import jax
import jax.numpy as jnp
from jax import lax
from jax.experimental import pallas as pl
from jax.experimental.pallas import tpu as pltpu
from jax.sharding import PartitionSpec as P

H = 12
STEP = 10
FETCH = 96
GIVE = 64

mask_fill = -1000000000.0
clip_at = 0.002
beta_one = 0.9
beta_two = 0.999
adam_eps = 1e-08

f32 = jnp.float32
bf16 = jnp.bfloat16
i32 = jnp.int32
HBM = pl.BlockSpec(memory_space=pl.ANY)
VMEM = pl.BlockSpec(memory_space=pltpu.VMEM)
MESH = pl.DeviceIdType.MESH


def deliver(x, axes, call_id, block_of=None):
    sizes = [lax.axis_size(axis) for axis in axes]
    count = math.prod(sizes)
    block = x.shape if block_of is None else x.shape[1:]

    def body(x_ref, o_ref, sent, came, own):
        here = [lax.axis_index(axis) for axis in axes]

        def flat(place):
            index = place[0]
            for size, along in zip(sizes[1:], place[1:]):
                index = index * size + along
            return index

        def peer(step):
            place = []
            for size, at in zip(reversed(sizes), reversed(here)):
                place.append(lax.rem(at + lax.rem(step, size), size))
                step = step // size
            return place[::-1]

        def source(place):
            return x_ref if block_of is None else x_ref.at[block_of(place)]

        mine = flat(here)

        def copy(step):
            place = peer(step)
            return pltpu.make_async_remote_copy(
                source(place),
                o_ref.at[mine],
                sent.at[step],
                came.at[step],
                device_id=dict(zip(axes, place)),
                device_id_type=MESH,
            )

        barrier = pltpu.get_barrier_semaphore()

        @pl.loop(1, count)
        def _(step):
            pl.semaphore_signal(
                barrier, inc=1, device_id=dict(zip(axes, peer(step))), device_id_type=MESH
            )

        local = pltpu.make_async_copy(source(here), o_ref.at[mine], own)
        local.start()
        pl.semaphore_wait(barrier, count - 1)

        @pl.loop(1, count)
        def _(step):
            copy(step).start()

        local.wait()

        @pl.loop(1, count)
        def _(step):
            copy(step).wait()

    return pl.pallas_call(
        body,
        out_shape=jax.ShapeDtypeStruct((count,) + block, x.dtype),
        in_specs=[HBM],
        out_specs=HBM,
        scratch_shapes=[
            pltpu.SemaphoreType.DMA((count,)),
            pltpu.SemaphoreType.DMA((count,)),
            pltpu.SemaphoreType.DMA,
        ],
        compiler_params=pltpu.CompilerParams(collective_id=call_id, has_side_effects=True),
    )(x)


def from_peer(x, axis, span, size, step):
    pairs = []
    for at in range(lax.axis_size(axis)):
        digit = at // span % size
        pairs.append((at, at + ((digit + step) % size - digit) * span))
    return lax.ppermute(x, axis, pairs)


def group_sum(x, dim, axis, span):
    size = x.shape[dim]
    at = lax.rem(lax.axis_index(axis) // span, size)
    total = lax.dynamic_index_in_dim(x, at, dim, False).astype(f32)
    for step in range(1, size):
        block = lax.dynamic_index_in_dim(x, lax.rem(at + step, size), dim, False)
        total = total + from_peer(block, axis, span, size, step).astype(f32)
    return total.astype(bf16)


def group_join(x, dim, axis, span, size):
    at = lax.rem(lax.axis_index(axis) // span, size)
    parts = [x] + [from_peer(x, axis, span, size, size - step) for step in range(1, size)]
    if size == 2:
        first = jnp.where(at == 0, parts[0], parts[1])
        second = jnp.where(at == 0, parts[1], parts[0])
        return jnp.stack([first, second], axis=dim)
    turned = jnp.stack(parts + parts, axis=dim)
    return lax.dynamic_slice_in_dim(turned, size - at, size, dim)


def settle(grads, given, vector, n_x, n_y, n_z, call_id):
    n_dp, _, _, chunks, height, width = grads.shape
    n_seq = 2 * n_x
    count = n_dp * n_seq
    near = n_dp * 2
    n_most = max(n_x, n_y)
    blocks = n_x * n_y * n_z

    def body(g_ref, e_ref, v_ref, o_ref, came_ref, vec_ref, *scratch):
        own, got, first, second, third = scratch[:5]
        v_core, v_x, v_y, v_z = scratch[5:9]
        core_out, core_in, core_own = scratch[9:12]
        one_out, one_in, two_out, two_in, three_out, three_in = scratch[12:18]
        x_out, x_in, pair_out, pair_in, last_own = scratch[18:23]
        e_out, e_in, far_out, far_in, v_out, v_in, side_own = scratch[23:]
        dp_at, seq_at = lax.axis_index("dp"), lax.axis_index("seq")
        x_at, c_at = seq_at // 2, lax.rem(seq_at, 2)
        z_at, y_at = dp_at // n_y, lax.rem(dp_at, n_y)
        partner = {"seq": x_at * 2 + 1 - c_at}

        def send(source, target, out_sem, in_sem, device):
            copy = pltpu.make_async_remote_copy(
                source, target, out_sem, in_sem, device_id=device, device_id_type=MESH
            )
            copy.start()
            return copy

        barrier = pltpu.get_barrier_semaphore()

        @pl.loop(1, count)
        def _(step):
            seq_to = lax.rem(seq_at + lax.rem(step, n_seq), n_seq)
            peer = {"dp": lax.rem(dp_at + step // n_seq, n_dp), "seq": seq_to}
            pl.semaphore_signal(barrier, inc=1, device_id=peer, device_id_type=MESH)

        def x_first(chunk):
            return chunk % 2 == 1

        def order(chunk):
            return (n_x, x_at, n_y, y_at) if x_first(chunk) else (n_y, y_at, n_x, x_at)

        def places(chunk, block):
            z, y, x = block // (n_y * n_x), lax.rem(block // n_x, n_y), lax.rem(block, n_x)
            at = (x * n_y + y) * n_z + z if x_first(chunk) else (y * n_x + x) * n_z + z
            return z * n_y + y, x, at

        for chunk in range(chunks):

            @pl.loop(0, blocks)
            def _(block):
                owner, x, at = places(chunk, block)
                source = g_ref.at[owner, c_at, x, chunk]
                pltpu.make_async_copy(source, own.at[chunk, at], core_own.at[chunk]).start()

        v_core[c_at] = v_ref[...]
        mine = came_ref.at[dp_at * n_seq + seq_at]
        side = pltpu.make_async_copy(e_ref.at[dp_at * 2 + c_at], mine, side_own)
        side.start()
        pl.semaphore_wait(barrier, count - 1)
        for chunk in range(chunks):

            @pl.loop(0, blocks)
            def _(block):
                owner, x, at = places(chunk, block)
                source = g_ref.at[owner, 1 - c_at, x, chunk]
                send(source, got.at[chunk, at], core_out.at[chunk], core_in.at[chunk], partner)

        v_turn = [
            (v_core, c_at, 2, lambda to: {"seq": x_at * 2 + to}),
            (v_x, x_at, n_x, lambda to: {"seq": to * 2 + c_at}),
            (v_y, y_at, n_y, lambda to: {"dp": z_at * n_y + to}),
            (v_z, z_at, n_z, lambda to: {"dp": to * n_y + y_at}),
        ]

        def vector_out(turn):
            buffer, at, size, device = v_turn[turn]
            return [
                send(
                    buffer.at[at],
                    buffer.at[at],
                    v_out.at[turn, step - 1],
                    v_in.at[turn, step - 1],
                    device(lax.rem(at + step, size)),
                )
                for step in range(1, size)
            ]

        def vector_sum(turn, copies):
            buffer, _, size, _ = v_turn[turn]
            for copy in copies:
                copy.wait()
            total = buffer[0]
            for place in range(1, size):
                total = total + buffer[place]
            return total

        v_copies = vector_out(0)

        def near_copy(step):
            owner = lax.rem(dp_at + step // 2, n_dp)
            core = lax.rem(c_at + lax.rem(step, 2), 2)
            return pltpu.make_async_remote_copy(
                e_ref.at[owner * 2 + core],
                mine,
                e_out.at[step],
                e_in.at[step],
                device_id={"dp": owner, "seq": x_at * 2 + core},
                device_id_type=MESH,
            )

        def far_copy(step, turn):
            origin = lax.rem(dp_at + n_dp - step // 2, n_dp)
            core = lax.rem(c_at + lax.rem(step, 2), 2)
            block = came_ref.at[origin * n_seq + x_at * 2 + core]
            to = lax.rem(x_at + turn, n_x) * 2 + c_at
            return pltpu.make_async_remote_copy(
                block,
                block,
                far_out.at[step, turn - 1],
                far_in.at[step, turn - 1],
                device_id={"seq": to},
                device_id_type=MESH,
            )

        @pl.loop(1, near)
        def _(step):
            near_copy(step).start()

        kept = {}
        for chunk in range(chunks):
            n_first, at_first, n_second, at_second = order(chunk)
            span = n_second * n_z
            whole = own.at[chunk]
            pltpu.make_async_copy(whole, whole, core_own.at[chunk]).wait()
            pltpu.make_async_remote_copy(
                whole, whole, core_out.at[chunk], core_in.at[chunk], device_id=partner, device_id_type=MESH
            ).wait()

            @pl.loop(0, blocks)
            def _(block):
                total = own[chunk, block].astype(f32) + got[chunk, block].astype(f32)
                own[chunk, block] = total.astype(bf16)

            for step in range(1, n_first):
                to = lax.rem(at_first + step, n_first)
                if x_first(chunk):
                    device = {"seq": to * 2 + c_at}
                else:
                    device = {"dp": z_at * n_y + to}
                copy = send(
                    own.at[chunk, pl.ds(to * span, span)],
                    first.at[chunk, step - 1, pl.ds(0, span)],
                    one_out.at[chunk, step - 1],
                    one_in.at[chunk, step - 1],
                    device,
                )
                kept[1, chunk, step] = copy
        v_x[x_at] = vector_sum(0, v_copies)
        v_copies = vector_out(1)
        side.wait()
        for turn in range(1, n_x):
            far_copy(0, turn).start()
        for chunk in range(chunks):
            n_first, at_first, n_second, at_second = order(chunk)
            span = n_second * n_z
            for step in range(1, n_first):
                kept[1, chunk, step].wait_recv()
            base = at_first * span

            @pl.loop(0, span)
            def _(block):
                total = own[chunk, base + block].astype(f32)
                for step in range(1, n_first):
                    total = total + first[chunk, step - 1, block].astype(f32)
                own[chunk, base + block] = total.astype(bf16)

            for step in range(1, n_second):
                to = lax.rem(at_second + step, n_second)
                if x_first(chunk):
                    device = {"dp": z_at * n_y + to}
                else:
                    device = {"seq": to * 2 + c_at}
                kept[2, chunk, step] = send(
                    own.at[chunk, pl.ds(base + to * n_z, n_z)],
                    second.at[chunk, step - 1],
                    two_out.at[chunk, step - 1],
                    two_in.at[chunk, step - 1],
                    device,
                )
            if chunk == 0:
                v_y[y_at] = vector_sum(1, v_copies)
                v_copies = vector_out(2)

                @pl.loop(1, near)
                def _(step):
                    near_copy(step).wait()
                    for turn in range(1, n_x):
                        far_copy(step, turn).start()

        v_z[z_at] = vector_sum(2, v_copies)
        v_copies = vector_out(3)
        for chunk in range(chunks):
            n_first, at_first, n_second, at_second = order(chunk)
            for step in range(1, n_second):
                kept[2, chunk, step].wait_recv()
            base = (at_first * n_second + at_second) * n_z

            @pl.loop(0, n_z)
            def _(block):
                total = own[chunk, base + block].astype(f32)
                for step in range(1, n_second):
                    total = total + second[chunk, step - 1, block].astype(f32)
                own[chunk, base + block] = total.astype(bf16)

            for step in range(1, n_z):
                to = lax.rem(z_at + step, n_z)
                kept[3, chunk, step] = send(
                    own.at[chunk, base + to],
                    third.at[chunk, step - 1],
                    three_out.at[chunk, step - 1],
                    three_in.at[chunk, step - 1],
                    {"dp": to * n_y + y_at},
                )
        vec_ref[...] = vector_sum(3, v_copies)
        for chunk in range(chunks):
            n_first, at_first, n_second, at_second = order(chunk)
            for step in range(1, n_z):
                kept[3, chunk, step].wait_recv()
            here = (at_first * n_second + at_second) * n_z + z_at
            total = own[chunk, here].astype(f32)
            for step in range(1, n_z):
                total = total + third[chunk, step - 1].astype(f32)
            own[chunk, here] = total.astype(bf16)
            result = o_ref.at[c_at, x_at, chunk]
            copy = pltpu.make_async_copy(own.at[chunk, here], result, last_own.at[chunk])
            copy.start()
            kept[0, chunk] = copy
            for step in range(1, n_x):
                to = lax.rem(x_at + step, n_x)
                kept[4, chunk, step] = send(
                    own.at[chunk, here],
                    result,
                    x_out.at[chunk, step - 1],
                    x_in.at[chunk, step - 1],
                    {"seq": to * 2 + c_at},
                )
            kept[5, chunk, 0] = send(
                own.at[chunk, here], result, pair_out.at[chunk, 0], pair_in.at[chunk, 0], partner
            )
        for chunk in range(chunks):
            for step in range(1, n_x):
                kept[4, chunk, step].wait_recv()
                origin = lax.rem(x_at + n_x - step, n_x)
                piece = o_ref.at[c_at, origin, chunk]
                kept[5, chunk, step] = send(
                    piece, piece, pair_out.at[chunk, step], pair_in.at[chunk, step], partner
                )

        @pl.loop(0, near)
        def _(step):
            for turn in range(1, n_x):
                far_copy(step, turn).wait()

        for chunk in range(chunks):
            kept[0, chunk].wait()
            for step in range(n_x):
                kept[5, chunk, step].wait()
        for key, copy in kept.items():
            if 1 <= key[0] <= 4:
                copy.wait_send()

    def dma(*shape):
        return pltpu.SemaphoreType.DMA(shape)

    most = n_most * n_z
    return pl.pallas_call(
        body,
        out_shape=(
            jax.ShapeDtypeStruct((2, n_x, chunks, height, width), bf16),
            jax.ShapeDtypeStruct((count,) + given.shape[1:], given.dtype),
            jax.ShapeDtypeStruct(vector.shape, vector.dtype),
        ),
        in_specs=[HBM, HBM, VMEM],
        out_specs=(HBM, HBM, VMEM),
        scratch_shapes=[
            pltpu.VMEM((chunks, blocks, height, width), bf16),
            pltpu.VMEM((chunks, blocks, height, width), bf16),
            pltpu.VMEM((chunks, n_most - 1, most, height, width), bf16),
            pltpu.VMEM((chunks, n_most - 1, n_z, height, width), bf16),
            pltpu.VMEM((chunks, n_z - 1, height, width), bf16),
            pltpu.VMEM((2,) + vector.shape, f32),
            pltpu.VMEM((n_x,) + vector.shape, f32),
            pltpu.VMEM((n_y,) + vector.shape, f32),
            pltpu.VMEM((n_z,) + vector.shape, f32),
            dma(chunks),
            dma(chunks),
            dma(chunks),
            dma(chunks, n_most - 1),
            dma(chunks, n_most - 1),
            dma(chunks, n_most - 1),
            dma(chunks, n_most - 1),
            dma(chunks, n_z - 1),
            dma(chunks, n_z - 1),
            dma(chunks, n_x - 1),
            dma(chunks, n_x - 1),
            dma(chunks, n_x),
            dma(chunks, n_x),
            dma(chunks),
            dma(near),
            dma(near),
            dma(near, n_x - 1),
            dma(near, n_x - 1),
            dma(4, max(n_most, n_z) - 1),
            dma(4, max(n_most, n_z) - 1),
            pltpu.SemaphoreType.DMA,
        ],
        compiler_params=pltpu.CompilerParams(
            collective_id=call_id, has_side_effects=True, vmem_limit_bytes=48 << 20
        ),
    )(grads, given, vector)


def read_heads(source, table_low, targets, vocab_part, chunk, n_y, n_z, call_id):
    n_pick, width = source.shape
    size = table_low.shape[0]
    n_dp = n_y * n_z
    chunks = size // chunk

    def body(s_ref, t_ref, target_ref, e_ref, h_ref, m_ref, stat_ref, e_buf, h_buf, t_buf, told, came, *sems):
        z_out, z_in, y_out, y_in, stat_out, stat_in, e_sem, load_sem, h_sem = sems
        dp_at = lax.axis_index("dp")
        z_at, y_at = dp_at // n_y, lax.rem(dp_at, n_y)
        load = pltpu.make_async_copy(t_ref, t_buf, load_sem)
        load.start()
        h_buf[dp_at] = s_ref[...]
        barrier = pltpu.get_barrier_semaphore()

        @pl.loop(1, n_dp)
        def _(step):
            to = lax.rem(dp_at + step, n_dp)
            pl.semaphore_signal(barrier, inc=1, device_id={"dp": to}, device_id_type=MESH)

        pl.semaphore_wait(barrier, n_dp - 1)

        def z_copy(step):
            mine = h_buf.at[dp_at]
            to = lax.rem(z_at + step, n_z) * n_y + y_at
            return pltpu.make_async_remote_copy(
                mine, mine, z_out.at[step], z_in.at[step], device_id={"dp": to}, device_id_type=MESH
            )

        def y_copy(turn, step):
            block = h_buf.at[lax.rem(z_at + n_z - turn, n_z) * n_y + y_at]
            to = z_at * n_y + lax.rem(y_at + step, n_y)
            return pltpu.make_async_remote_copy(
                block,
                block,
                y_out.at[turn, step],
                y_in.at[turn, step],
                device_id={"dp": to},
                device_id_type=MESH,
            )

        for step in range(1, n_y):
            y_copy(0, step).start()
        for step in range(1, n_z):
            z_copy(step).start()
        load.wait()

        def logits(rows, index):
            part = t_buf[index * chunk : (index + 1) * chunk]
            return lax.dot_general(part, rows, (((1,), (1,)), ((), ())), preferred_element_type=f32)

        @pl.loop(0, n_dp)
        def _(turn):
            z_turn, y_turn = turn // n_y, lax.rem(turn, n_y)

            @pl.when((y_turn == 0) & (z_turn > 0))
            def _():
                z_copy(z_turn).wait_recv()
                for step in range(1, n_y):
                    y_copy(z_turn, step).start()

            @pl.when(y_turn > 0)
            def _():
                y_copy(z_turn, y_turn).wait_recv()

            origin = lax.rem(z_at + n_z - z_turn, n_z) * n_y + lax.rem(y_at + n_y - y_turn, n_y)
            rows = h_buf[origin]
            target = target_ref[origin]
            row = lax.broadcasted_iota(i32, (chunk // 8, 8, n_pick), 0) * 8
            row = row + lax.broadcasted_iota(i32, (chunk // 8, 8, n_pick), 1)
            top = summed = hit = None
            ahead = logits(rows, 0)
            for index in range(chunks):
                now = ahead.reshape(chunk // 8, 8, n_pick)
                if index + 1 < chunks:
                    ahead = logits(rows, index + 1)
                first = index * chunk
                if first + chunk > vocab_part:
                    now = jnp.where(row < vocab_part - first, now, -jnp.inf)
                chunk_top = jnp.max(now, axis=0)
                new_top = chunk_top if top is None else jnp.maximum(top, chunk_top)
                grown = jnp.exp(now - new_top[None])
                chunk_sum = jnp.sum(grown, axis=0)
                chunk_hit = jnp.sum(jnp.where(row == (target - first)[None], now, 0.0), axis=0)
                if top is None:
                    summed, hit = chunk_sum, chunk_hit
                else:
                    summed = summed * jnp.exp(top - new_top) + chunk_sum
                    hit = hit + chunk_hit
                top = new_top
                e_buf[origin, first : first + chunk] = grown.reshape(chunk, n_pick).astype(bf16)
                m_ref[origin, index] = top
            best = jnp.max(top, axis=0, keepdims=True)
            told[origin] = jnp.zeros((8, n_pick), f32)
            told[origin, 0:1] = best
            told[origin, 1:2] = jnp.sum(summed * jnp.exp(top - best), axis=0, keepdims=True)
            told[origin, 2:3] = jnp.sum(hit, axis=0, keepdims=True)
            pltpu.make_async_copy(e_buf.at[origin], e_ref.at[origin], e_sem.at[origin]).start()

        def stat_copy(step):
            to = lax.rem(dp_at + step, n_dp)
            return pltpu.make_async_remote_copy(
                told,
                came.at[dp_at],
                stat_out.at[step],
                stat_in.at[step],
                device_id={"dp": to},
                device_id_type=MESH,
            )

        @pl.loop(1, n_dp)
        def _(step):
            stat_copy(step).start()

        came[dp_at] = told[...]
        keep = pltpu.make_async_copy(h_buf, h_ref, h_sem)
        keep.start()
        for step in range(1, n_z):
            z_copy(step).wait_send()
        for turn in range(n_z):
            for step in range(1, n_y):
                y_copy(turn, step).wait_send()

        @pl.loop(0, n_dp)
        def _(origin):
            pltpu.make_async_copy(e_buf.at[origin], e_ref.at[origin], e_sem.at[origin]).wait()

        @pl.loop(1, n_dp)
        def _(step):
            stat_copy(step).wait()

        keep.wait()
        stat_ref[...] = came[...]

    def dma(*shape):
        return pltpu.SemaphoreType.DMA(shape)

    return pl.pallas_call(
        body,
        out_shape=(
            jax.ShapeDtypeStruct((n_dp, size, n_pick), bf16),
            jax.ShapeDtypeStruct((n_dp, n_pick, width), bf16),
            jax.ShapeDtypeStruct((n_dp, chunks, 8, n_pick), f32),
            jax.ShapeDtypeStruct((n_dp, n_dp, 8, n_pick), f32),
        ),
        in_specs=[VMEM, HBM, VMEM],
        out_specs=(HBM, HBM, VMEM, VMEM),
        scratch_shapes=[
            pltpu.VMEM((n_dp, size, n_pick), bf16),
            pltpu.VMEM((n_dp, n_pick, width), bf16),
            pltpu.VMEM((size, width), bf16),
            pltpu.VMEM((n_dp, 8, n_pick), f32),
            pltpu.VMEM((n_dp, n_dp, 8, n_pick), f32),
            dma(n_z),
            dma(n_z),
            dma(n_z, n_y),
            dma(n_z, n_y),
            dma(n_dp),
            dma(n_dp),
            dma(n_dp),
            pltpu.SemaphoreType.DMA,
            pltpu.SemaphoreType.DMA,
        ],
        compiler_params=pltpu.CompilerParams(
            collective_id=call_id, has_side_effects=True, vmem_limit_bytes=56 << 20
        ),
    )(source, table_low, targets)


def write_heads(grown, heads, turned, tops, stats, targets, weights, chunk, n_x, call_id):
    n_dp, size, n_pick = grown.shape
    width = heads.shape[2]
    chunks = size // chunk
    turns = chunks // 2
    part = size // 2 // n_x
    block = math.gcd(chunk, part)

    def body(e_ref, h_ref, t_ref, m_ref, stat_ref, target_ref, w_ref, d_ref, log_ref, *refs):
        part_refs, scratch = refs[:n_x], refs[n_x:]
        buf, t_buf, df_buf, out_buf, got, res = scratch[:6]
        e_sem, t_sem, df_out, df_in, df_own, pair_out, pair_in, res_sem = scratch[6:]
        dp_at, seq_at = lax.axis_index("dp"), lax.axis_index("seq")
        core = lax.rem(seq_at, 2)
        partner = {"seq": seq_at + 1 - 2 * core}
        load = pltpu.make_async_copy(t_ref, t_buf, t_sem)

        def e_copy(turn):
            origin = lax.rem(dp_at + 1 + turn, n_dp)
            return pltpu.make_async_copy(e_ref.at[origin], buf.at[origin], e_sem.at[turn])

        e_copy(0).start()
        load.start()

        @pl.loop(1, n_dp)
        def _(turn):
            e_copy(turn).start()

        barrier = pltpu.get_barrier_semaphore()

        @pl.loop(1, n_dp)
        def _(step):
            to = lax.rem(dp_at + step, n_dp)
            pl.semaphore_signal(barrier, inc=1, device_id={"dp": to}, device_id_type=MESH)

        pl.semaphore_signal(barrier, inc=1, device_id=partner, device_id_type=MESH)

        @pl.loop(0, n_dp)
        def _(origin):
            top = stat_ref[0, origin, 0:1]
            for sender in range(1, n_dp):
                top = jnp.maximum(top, stat_ref[sender, origin, 0:1])
            total = jnp.zeros((1, n_pick), f32)
            hit = jnp.zeros((1, n_pick), f32)
            for sender in range(n_dp):
                total = total + stat_ref[sender, origin, 1:2] * jnp.exp(stat_ref[sender, origin, 0:1] - top)
                hit = hit + stat_ref[sender, origin, 2:3]
            log_ref[0, origin] = top + jnp.log(total)
            log_ref[1, origin] = hit

        load.wait()
        pl.semaphore_wait(barrier, n_dp)

        def df_copy(turn):
            to = lax.rem(dp_at + 1 + turn, n_dp)
            return pltpu.make_async_remote_copy(
                df_buf.at[to],
                d_ref.at[dp_at],
                df_out.at[turn],
                df_in.at[turn],
                device_id={"dp": to},
                device_id_type=MESH,
            )

        @pl.loop(0, n_dp)
        def _(turn):
            origin = lax.rem(dp_at + 1 + turn, n_dp)
            e_copy(turn).wait()
            log_total = log_ref[0, origin]
            weight = w_ref[origin]
            target = target_ref[origin]
            row = lax.broadcasted_iota(i32, (chunk // 8, 8, n_pick), 0) * 8
            row = row + lax.broadcasted_iota(i32, (chunk // 8, 8, n_pick), 1)

            def gradient(index):
                rows = pl.ds(index * chunk, chunk)
                scale = jnp.exp(m_ref[origin, index] - log_total) * weight
                part = buf[origin, rows].astype(f32).reshape(chunk // 8, 8, n_pick) * scale[None]
                at_target = row == (target - index * chunk)[None]
                part = part - jnp.where(at_target, weight[None], 0.0)
                part = part.reshape(chunk, n_pick).astype(bf16)
                buf[origin, rows] = part
                return part

            total = None
            ahead = gradient(0)
            for index in range(chunks):
                now = ahead
                if index + 1 < chunks:
                    ahead = gradient(index + 1)
                columns = t_buf[:, index * chunk : (index + 1) * chunk]
                part = jnp.dot(columns, now, preferred_element_type=f32)
                total = part if total is None else total + part
            df_buf[origin] = total.astype(bf16)

            @pl.when(turn < n_dp - 1)
            def _():
                df_copy(turn).start()

        local = pltpu.make_async_copy(df_buf.at[dp_at], d_ref.at[dp_at], df_own)
        local.start()

        def table_part(index):
            first = pl.multiple_of(index * chunk, chunk)
            part = jnp.concatenate([buf[origin, pl.ds(first, chunk)] for origin in range(n_dp)], axis=1)
            return jnp.dot(part, h_ref[...], preferred_element_type=f32)

        def pair_copy(turn):
            return pltpu.make_async_remote_copy(
                out_buf.at[turn],
                got.at[turn],
                pair_out.at[turn],
                pair_in.at[turn],
                device_id=partner,
                device_id_type=MESH,
            )

        @pl.loop(0, turns)
        def _(turn):
            out_buf[turn] = table_part((1 - core) * turns + turn).astype(bf16)
            pair_copy(turn).start()

        def res_out(turn):
            for index in range(chunk // block):
                at = turn * (chunk // block) + index
                rows = pl.ds(pl.multiple_of(lax.rem(at, part // block) * block, block), block)
                slot = lax.rem(at // (part // block) + n_x - seq_at // 2, n_x)
                for place in range(n_x):

                    @pl.when(slot == place)
                    def _():
                        pltpu.make_async_copy(
                            res.at[turn, pl.ds(index * block, block)], part_refs[place].at[rows], res_sem.at[turn]
                        ).start()

        @pl.loop(0, turns)
        def _(turn):
            total = table_part(core * turns + turn)
            pair_copy(turn).wait()
            res[turn] = (total + got[turn].astype(f32)).astype(bf16)
            res_out(turn)

        @pl.loop(0, turns)
        def _(turn):
            pltpu.make_async_copy(res.at[turn], res.at[turn], res_sem.at[turn]).wait()

        local.wait()

        @pl.loop(0, n_dp - 1)
        def _(turn):
            df_copy(turn).wait()

    def dma(*shape):
        return pltpu.SemaphoreType.DMA(shape)

    return pl.pallas_call(
        body,
        out_shape=(
            jax.ShapeDtypeStruct((n_dp, width, n_pick), bf16),
            jax.ShapeDtypeStruct((2, n_dp, 1, n_pick), f32),
        )
        + (jax.ShapeDtypeStruct((part, width), bf16),) * n_x,
        in_specs=[HBM, VMEM, HBM, VMEM, VMEM, VMEM, VMEM],
        out_specs=(HBM, VMEM) + (HBM,) * n_x,
        scratch_shapes=[
            pltpu.VMEM((n_dp, size, n_pick), bf16),
            pltpu.VMEM((width, size), bf16),
            pltpu.VMEM((n_dp, width, n_pick), bf16),
            pltpu.VMEM((turns, chunk, width), bf16),
            pltpu.VMEM((turns, chunk, width), bf16),
            pltpu.VMEM((turns, chunk, width), bf16),
            dma(n_dp),
            pltpu.SemaphoreType.DMA,
            dma(n_dp),
            dma(n_dp),
            pltpu.SemaphoreType.DMA,
            dma(turns),
            dma(turns),
            dma(turns),
        ],
        compiler_params=pltpu.CompilerParams(
            collective_id=call_id, has_side_effects=True, vmem_limit_bytes=62 << 20
        ),
    )(grown, heads.reshape(n_dp * n_pick, width), turned, tops, stats, targets, weights)


def staged(work, ins, small, outs, temps, limit, buffers_of=(), pieces=None, eager=2):
    n_in, n_small, n_out = len(ins), len(small), len(outs)
    packed, places = ((), {}) if pieces is None else ((pieces[0],), pieces[1])

    def body(*refs):
        packed_refs, refs = refs[: len(packed)], refs[len(packed) :]
        in_refs, small_refs, refs = refs[:n_in], refs[n_in : n_in + n_small], refs[n_in + n_small :]
        out_refs, in_bufs, refs = refs[:n_out], refs[n_out : n_out + n_in], refs[n_out + n_in :]
        out_bufs, (in_sem, out_sem), temp_refs = refs[:n_out], refs[n_out : n_out + 2], refs[n_out + 2 :]
        loads = {}
        names = list(ins)

        def start(at):
            name = names[at]
            loads[name] = pltpu.make_async_copy(in_refs[at], in_bufs[at], in_sem.at[at])
            if name not in places:
                loads[name].start()
                return
            loads[name] = pltpu.make_async_copy(in_bufs[at], in_bufs[at], in_sem.at[at])
            for source, target in places[name]:
                pltpu.make_async_copy(
                    packed_refs[0].at[source], in_bufs[at].at[target], in_sem.at[at]
                ).start()

        for at in range(eager):
            start(at)
        buffers = dict(zip(ins, in_bufs))
        pending, sent = list(ins), []

        def get(name):
            if name in pending:
                pending.remove(name)
                loads[name].wait()
                if name == names[eager - 1]:
                    for at in range(eager, n_in):
                        start(at)
            return buffers[name]

        def put(name, begin=0, count=None):
            at = list(outs).index(name)
            source, target = out_bufs[at], out_refs[at]
            if count is not None:
                source, target = source.at[:, pl.ds(0, count)], target.at[:, pl.ds(begin, count)]
            copy = pltpu.make_async_copy(source, target, out_sem.at[len(sent)])
            copy.start()
            sent.append(copy)
            return copy

        def done(copy):
            copy.wait()
            sent[sent.index(copy)] = None

        work(get, dict(zip(small, small_refs)), dict(zip(outs, out_bufs)), (put, done), temp_refs)
        for name in list(pending):
            get(name)
        for copy in sent:
            if copy is not None:
                copy.wait()

    def scratch(value):
        return pltpu.VMEM(value.shape, value.dtype)

    def refs_of(name, value):
        return jnp.zeros((8, 128), value.dtype) if name in places else value

    return pl.pallas_call(
        body,
        out_shape=tuple(outs.values()),
        in_specs=[HBM] * (len(packed) + n_in) + [VMEM] * n_small,
        out_specs=(HBM,) * n_out,
        scratch_shapes=[scratch(value) for value in ins.values()]
        + [scratch(dict(buffers_of).get(name, value)) for name, value in outs.items()]
        + [pltpu.SemaphoreType.DMA((n_in,)), pltpu.SemaphoreType.DMA((n_out + 2,))]
        + temps,
        compiler_params=pltpu.CompilerParams(vmem_limit_bytes=limit << 20),
        cost_estimate=pl.CostEstimate(flops=0, bytes_accessed=0, transcendentals=0),
    )(*packed, *[refs_of(name, value) for name, value in ins.items()], *small.values())


def dot(left, right, left_dim=1, right_dim=0):
    return lax.dot_general(
        left, right, (((left_dim,), (right_dim,)), ((), ())), preferred_element_type=f32
    )


def norm_parts(x):
    centre = x - jnp.mean(x, axis=-1, keepdims=True)
    scale = lax.rsqrt(jnp.mean(centre * centre, axis=-1, keepdims=True) + 1e-05)
    return centre * scale, scale


def norm_back(x, gain, grad):
    unit, scale = norm_parts(x)
    d_gain = jnp.sum(grad * unit, axis=0, keepdims=True)
    d_shift = jnp.sum(grad, axis=0, keepdims=True)
    inner = grad * gain
    pull = jnp.mean(inner, axis=-1, keepdims=True)
    pull = pull + unit * jnp.mean(inner * unit, axis=-1, keepdims=True)
    return scale * (inner - pull), d_gain, d_shift


def iota(shape, dim):
    return lax.broadcasted_iota(i32, shape, dim)


def flat(ref):
    value = ref[...]
    return value.reshape(-1, value.shape[-1])


def column_block(ref, block, size):
    if len(ref.shape) == 2:
        return ref[:, block * size : (block + 1) * size]
    return flat(ref.at[block])


def row_block(ref, block, size):
    first = block * size
    if len(ref.shape) == 2:
        return ref[first : first + size]
    _, inner, rows, _ = ref.shape
    if inner * rows <= size:
        per = inner * rows
        return flat(ref.at[pl.ds(first // per, size // per)])
    owner, first = divmod(first, inner * rows)
    return flat(ref.at[owner, pl.ds(first // rows, size // rows)])


def split_three(x):
    high = x.astype(bf16)
    rest = x - high.astype(f32)
    middle = rest.astype(bf16)
    return high, middle, (rest - middle.astype(f32)).astype(bf16)


def layer_forward(embedded, pos, w_in, w_out, w_up, w_down, vectors, picks, row_length, pieces):
    length, model = embedded.shape
    n_pick = picks.shape[0]
    lanes = 128
    groups = model // lanes
    head_dim = model // H
    per = lanes // head_dim

    def work(get, small, out, moves, temps):
        put, _ = moves
        vec = small["vectors"]
        v_turned, o_turned = temps
        emb, pos_rows = get("emb"), get("pos")
        start = emb[...].astype(f32) + flat(pos_rows).astype(f32)
        unit, _ = norm_parts(start)
        out["a"][...] = (unit * vec[0:1] + vec[1:2]).astype(bf16)
        put("a")
        chosen = jnp.where(small["pick_col"][...] - 1 == iota((n_pick, length), 1), 1.0, 0.0).astype(bf16)
        start_picked = dot(chosen, emb[...]) + dot(chosen, flat(pos_rows))
        w = get("w_in")
        out["k"][...] = dot(out["a"][...], column_block(w, 1, model)).astype(bf16)
        put("k")
        out["v"][...] = (dot(out["a"][...], column_block(w, 2, model)) + vec[7:8]).astype(bf16)
        put("v")
        a_picked = dot(chosen, out["a"][...]).astype(bf16)
        out["q"][...] = (dot(a_picked, column_block(w, 0, model)) + vec[6:7]).astype(bf16)
        put("q")
        keep = iota((length, n_pick), 0) < small["length"][0, 0]

        @pl.loop(0, groups)
        def _(group):
            place = pl.ds(pl.multiple_of(group * lanes, lanes), lanes)
            v_turned[...] = out["v"][:, place].T
            q_pair, k_pair = out["q"][:, place], out["k"][:, place]
            mixed = None
            for j in range(per):
                q_head = jnp.where(iota((n_pick, lanes), 1) // head_dim == j, q_pair, jnp.zeros_like(q_pair))
                score = jnp.where(keep, dot(k_pair, q_head, 1, 1) * 0.125, mask_fill)
                top = jnp.max(score, axis=0, keepdims=True)
                grown = jnp.exp(score - top)
                total = jnp.sum(grown, axis=0, keepdims=True)
                out["lse"][group * per + j] = top + jnp.log(total)
                probs = (grown * (1.0 / total)).astype(bf16)
                part = dot(v_turned[...], probs)
                mixed = part if mixed is None else jnp.where(iota((lanes, n_pick), 0) // head_dim == j, part, mixed)
            o_turned[pl.ds(pl.multiple_of(group * lanes, lanes), lanes)] = mixed

        out["o"][...] = o_turned[...].T.astype(bf16)
        put("lse")
        put("o")
        x1 = start_picked + dot(out["o"][...], flat(get("w_out"))) + vec[8:9]
        out["x1"][...] = x1
        put("x1")
        unit, _ = norm_parts(x1)
        out["m"][...] = (unit * vec[2:3] + vec[3:4]).astype(bf16)
        put("m")
        up, down = get("w_up"), get("w_down")
        x2 = x1 + vec[9:10]
        for block in range(vectors.shape[0] - 10):
            u1 = dot(out["m"][...], column_block(up, block, model)) + vec[10 + block : 11 + block]
            x2 = x2 + dot(gelu_fn(u1).astype(bf16), row_block(down, block, model))
        out["x2"][...] = x2
        put("x2")
        unit, _ = norm_parts(x2)
        out["f"][...] = (unit * vec[4:5] + vec[5:6]).astype(bf16)
        put("f")

    def shape(rows, dtype):
        return jax.ShapeDtypeStruct((rows, model), dtype)

    outs = {
        "a": shape(length, bf16),
        "k": shape(length, bf16),
        "v": shape(length, bf16),
        "q": shape(n_pick, bf16),
        "lse": jax.ShapeDtypeStruct((H, 1, n_pick), f32),
        "o": shape(n_pick, bf16),
        "x1": shape(n_pick, f32),
        "m": shape(n_pick, bf16),
        "x2": shape(n_pick, f32),
        "f": shape(n_pick, bf16),
    }
    values = staged(
        work,
        {"emb": embedded, "pos": pos, "w_in": w_in, "w_out": w_out, "w_up": w_up, "w_down": w_down},
        {"vectors": vectors, "pick_col": picks[:, None], "length": row_length.reshape(1, 1)},
        outs,
        [pltpu.VMEM((lanes, length), bf16), pltpu.VMEM((model, n_pick), f32)],
        60,
        pieces=pieces,
    )
    return dict(zip(outs, values))


def layer_backward(
    final_grad, kept, embedded, pos, weights, vectors, picks, spots, row_length, loss, n_dp, pieces
):
    length, model = embedded.shape
    n_pick = picks.shape[0]
    lanes = 128
    groups = model // lanes
    head_dim = model // H
    per = lanes // head_dim
    w_in, w_out, w_up, w_down = weights
    wide = vectors.shape[0] - 10
    hidden = wide * model
    thick, long, n_place = model // n_dp, hidden // n_dp, spots[1]
    first_rows = 2 * long
    last_rows = 4 * thick + length // n_dp

    def work(get, small, out, moves, temps):
        put, done = moves
        vec, d_vec = small["vectors"], out["vec"]
        dqkv, dq, d_mixed = temps
        whole = out["whole"]

        def rows_of(first, count, values):
            values = values.astype(bf16)
            for owner in range(n_dp):
                whole[owner, first : first + count] = values[owner * count : (owner + 1) * count]

        x2, dfin = get("x2"), get("dfin")
        dx2, d_vec[4:5], d_vec[5:6] = norm_back(x2[...], vec[4:5], dfin[...])
        dy2 = dx2.astype(bf16)
        d_vec[9:10] = jnp.sum(dy2.astype(f32), axis=0, keepdims=True)
        m, up, down = get("m"), get("w_up"), get("w_down")
        m_turned = m[...].T
        dm = None
        for block in range(wide):
            u1 = dot(m[...], column_block(up, block, model)) + vec[10 + block : 11 + block]
            act, gelu_back = jax.vjp(gelu_fn, u1)
            part = dot(act.astype(bf16).T, dy2).astype(bf16)
            run = min(long, model)
            for at in range(0, model, run):
                owner, row = divmod(block * model + at, long)
                whole[owner, row : row + run] = part[at : at + run]
            du1 = gelu_back(dot(dy2, row_block(down, block, model), 1, 1))[0].astype(bf16)
            d_vec[10 + block : 11 + block] = jnp.sum(du1.astype(f32), axis=0, keepdims=True)
            rows_of(long + block * thick, thick, dot(m_turned, du1))
            part = dot(du1, column_block(up, block, model), 1, 1)
            dm = part if dm is None else dm + part
        first_out = put("whole", 0, first_rows)
        dx1, d_vec[2:3], d_vec[3:4] = norm_back(get("x1")[...], vec[2:3], dm)
        dx1 = dx2 + dx1
        dy1 = dx1.astype(bf16)
        d_vec[8:9] = jnp.sum(dy1.astype(f32), axis=0, keepdims=True)
        done(first_out)
        rows_of(0, thick, dot(get("o")[...].T, dy1))
        d_mixed[...] = dot(dy1, flat(get("w_out")), 1, 1).astype(bf16)
        keep = iota((length, n_pick), 0) < small["length"][0, 0]
        q, k, v, lse = get("q"), get("k"), get("v"), small["lse"]

        @pl.loop(0, groups)
        def _(group):
            def place(part):
                return pl.ds(pl.multiple_of(part * model + group * lanes, lanes), lanes)

            q_pair, k_pair, v_pair, d_pair = q[:, place(0)], k[:, place(0)], v[:, place(0)], d_mixed[:, place(0)]
            k_turned = k_pair.T
            sums = None
            for j in range(per):
                lane = iota((n_pick, lanes), 1) // head_dim == j
                q_head = jnp.where(lane, q_pair, jnp.zeros_like(q_pair))
                d_head = jnp.where(lane, d_pair, jnp.zeros_like(d_pair))
                score = jnp.where(keep, dot(k_pair, q_head, 1, 1) * 0.125, mask_fill)
                probs = jnp.exp(score - lse[group * per + j])
                dp = dot(v_pair, d_head, 1, 1)
                ds = (probs * (dp - jnp.sum(dp * probs, axis=0, keepdims=True))).astype(bf16)
                parts = (dot(k_turned, ds), dot(ds, q_pair), dot(probs.astype(bf16), d_pair))
                if sums is None:
                    sums = parts
                else:
                    rows = iota((lanes, n_pick), 0) // head_dim == j
                    columns = iota((length, lanes), 1) // head_dim == j
                    sums = (
                        jnp.where(rows, parts[0], sums[0]),
                        jnp.where(columns, parts[1], sums[1]),
                        jnp.where(columns, parts[2], sums[2]),
                    )
            dq[:, place(0)] = (sums[0] * 0.125).T.astype(bf16)
            dqkv[:, place(1)] = (sums[1] * 0.125).astype(bf16)
            dqkv[:, place(2)] = sums[2].astype(bf16)

        chosen = jnp.where(small["pick_row"][...] - 1 == iota((length, n_pick), 0), 1.0, 0.0).astype(bf16)
        dqkv[:, :model] = dot(chosen, dq[...]).astype(bf16)
        d_vec[6:7] = jnp.sum(dq[...].astype(f32), axis=0, keepdims=True)
        d_vec[7:8] = jnp.sum(dqkv[:, 2 * model :].astype(f32), axis=0, keepdims=True)
        a_turned = get("a")[...].T
        for part in range(3):
            rows_of((1 + part) * thick, thick, dot(a_turned, dqkv[:, part * model : (part + 1) * model]))
        w = get("w_in")
        da = dot(dqkv[:, :model], column_block(w, 0, model), 1, 1)
        for part in range(1, 3):
            da = da + dot(dqkv[:, part * model : (part + 1) * model], column_block(w, part, model), 1, 1)
        start = get("emb")[...].astype(f32) + flat(get("pos")).astype(f32)
        dx0, d_vec[0:1], d_vec[1:2] = norm_back(start, vec[0:1], da)
        for part in split_three(dx1):
            dx0 = dx0 + dot(chosen, part)
        rows_of(4 * thick, length // n_dp, dx0)
        put("whole", first_rows, last_rows)
        d_vec[14:15] = small["loss"][...]
        d_vec[15:16] = jnp.zeros((1, model), f32)
        put("vec")
        out["low"][...] = dx0.astype(bf16)
        put("low")
        step = min(n_place, 512)
        for first in range(0, n_place, step):
            where = jnp.where(small["spots"][...] == iota((step, length), 0) + first, 1.0, 0.0).astype(bf16)
            out["given"][first : first + step] = dot(where, out["low"][...]).astype(bf16)
        put("given")

    outs = {
        "whole": jax.ShapeDtypeStruct((n_dp, first_rows + last_rows, model), bf16),
        "vec": jax.ShapeDtypeStruct((16, model), f32),
        "low": jax.ShapeDtypeStruct((length, model), bf16),
        "given": jax.ShapeDtypeStruct((n_place, model), bf16),
    }
    ins = {
        "x2": kept["x2"],
        "dfin": final_grad,
        "m": kept["m"],
        "w_up": w_up,
        "w_down": w_down,
        "x1": kept["x1"],
        "o": kept["o"],
        "w_out": w_out,
        "q": kept["q"],
        "k": kept["k"],
        "v": kept["v"],
        "a": kept["a"],
        "w_in": w_in,
        "emb": embedded,
        "pos": pos,
    }
    small = {
        "vectors": vectors,
        "lse": kept["lse"],
        "pick_row": picks[None, :],
        "spots": spots[0][None, :],
        "length": row_length.reshape(1, 1),
        "loss": jnp.full((1, model), loss),
    }
    temps = [
        pltpu.VMEM((length, 3 * model), bf16),
        pltpu.VMEM((n_pick, model), bf16),
        pltpu.VMEM((n_pick, model), bf16),
    ]
    buffer = jax.ShapeDtypeStruct((n_dp, max(first_rows, last_rows), model), bf16)
    return staged(work, ins, small, outs, temps, 62, {"whole": buffer}, pieces, 5)


def table_forms(table, size, chunk):
    count, width = table.shape

    def body(t_ref, low_ref, turned_ref):
        row = iota((chunk, width), 0) + pl.program_id(0) * chunk
        value = jnp.where(row < count, t_ref[...], 0.0)
        low_ref[...] = value.astype(bf16)
        turned_ref[...] = value.T.astype(bf16)

    return pl.pallas_call(
        body,
        grid=(size // chunk,),
        in_specs=[pl.BlockSpec((chunk, width), lambda step: (step, 0))],
        out_specs=(
            pl.BlockSpec((chunk, width), lambda step: (step, 0)),
            pl.BlockSpec((width, chunk), lambda step: (0, step)),
        ),
        out_shape=(
            jax.ShapeDtypeStruct((size, width), bf16),
            jax.ShapeDtypeStruct((width, size), bf16),
        ),
        compiler_params=pltpu.CompilerParams(vmem_limit_bytes=32 << 20),
    )(table)


def close_half(own, other, names, values, layer, share, tile):
    half, width = own.shape
    count = min(names.shape[1], 2048)
    parts = names.shape[1] // count

    def body(own_ref, other_ref, names_ref, values_ref, layer_ref, o_ref, square_ref, total):
        step, part = pl.program_id(0), pl.program_id(1)

        @pl.when(part == 0)
        def _():
            total[...] = own_ref[...].astype(f32) + other_ref[...].astype(f32)

        row = iota((tile, count), 0) + step * tile
        where = jnp.where(row == names_ref[...], 1.0, 0.0).astype(bf16)
        total[...] += jnp.dot(where, values_ref[...], preferred_element_type=f32)

        @pl.when((step == 0) & (part == 0))
        def _():
            layer_part = layer_ref[...].astype(f32)
            square_ref[...] = jnp.sum(layer_part * layer_part, axis=0, keepdims=True) * share

        @pl.when(part == parts - 1)
        def _():
            o_ref[...] = total[...].astype(bf16)
            square_ref[...] += jnp.sum(total[...] * total[...], axis=0, keepdims=True)

    rows = pl.BlockSpec((tile, width), lambda step, part: (step, 0))
    return pl.pallas_call(
        body,
        grid=(half // tile, parts),
        in_specs=[
            rows,
            rows,
            pl.BlockSpec((1, count), lambda step, part: (0, part)),
            pl.BlockSpec((count, width), lambda step, part: (part, 0)),
            pl.BlockSpec(layer.shape, lambda step, part: (0, 0)),
        ],
        out_specs=(rows, pl.BlockSpec((1, width), lambda step, part: (0, 0))),
        out_shape=(jax.ShapeDtypeStruct((half, width), bf16), jax.ShapeDtypeStruct((1, width), f32)),
        scratch_shapes=[pltpu.VMEM((tile, width), f32)],
        compiler_params=pltpu.CompilerParams(vmem_limit_bytes=48 << 20),
        cost_estimate=pl.CostEstimate(flops=0, bytes_accessed=0, transcendentals=0),
    )(own, other, names, values, layer)


def adam_table(at, squares, vector, weights, mine, other, tile, half, n_x, steps, done):
    size, width = weights[0].shape
    per_half, per_part = half // tile, half // n_x // tile
    turns = len(steps) * per_part
    first_step = steps[0]

    def body(at_ref, square_ref, vec_ref, w_ref, m_ref, v_ref, mine_ref, other_ref, *refs):
        new_w, new_m, new_v, token, factor = refs[-5:]

        @pl.when(pl.program_id(0) == 0)
        def _():
            squares = jnp.sum(square_ref[...], axis=0)[0:1, 0:1]
            row = jnp.sum(vec_ref[...] * vec_ref[...], axis=0, keepdims=True)
            norm = jnp.sqrt(squares + jnp.sum(row, axis=1, keepdims=True))
            factor[...] = jnp.broadcast_to(clip_at / jnp.maximum(norm, clip_at), factor.shape)
            token[...] = jnp.zeros_like(token)

        from_mine = pl.program_id(0) < turns
        grad = jnp.where(from_mine, mine_ref[...], other_ref[...]).astype(f32) * factor[0:1, 0:1]
        new_w[...], new_m[...], new_v[...] = adam_update(
            w_ref[...], grad, m_ref[...], v_ref[...], 0.1, 0.1
        )

    def row_at(step, at_ref):
        core = lax.rem(at_ref[0] + step // turns, 2)
        turn = lax.rem(step, turns)
        x = lax.rem(at_ref[1] + n_x - (first_step + turn // per_part), n_x)
        return (core * per_half + x * per_part + lax.rem(turn, per_part), 0)

    def mine_at(step, at_ref):
        return (jnp.minimum(step, turns - 1), 0)

    def other_at(step, at_ref):
        return (jnp.maximum(step - turns, 0), 0)

    rows = pl.BlockSpec((tile, width), row_at)
    done = () if done is None else done
    return pl.pallas_call(
        body,
        grid_spec=pltpu.PrefetchScalarGridSpec(
            num_scalar_prefetch=1,
            grid=(2 * turns,),
            in_specs=[VMEM, VMEM, rows, rows, rows, pl.BlockSpec((tile, width), mine_at), pl.BlockSpec((tile, width), other_at)]
            + [HBM] * len(done),
            out_specs=(rows, rows, rows, pl.BlockSpec((8, 128), lambda *_: (0, 0))),
            scratch_shapes=[pltpu.VMEM((8, 128), f32)],
        ),
        out_shape=(jax.ShapeDtypeStruct((size, width), f32),) * 3 + (jax.ShapeDtypeStruct((8, 128), f32),),
        input_output_aliases={8 + index: index for index in range(len(done))},
        compiler_params=pltpu.CompilerParams(vmem_limit_bytes=56 << 20),
        cost_estimate=pl.CostEstimate(flops=0, bytes_accessed=0, transcendentals=0),
    )(at, squares, vector, *weights, mine, other, *done)


def update_layer(factor, grads, weights, firsts, seconds):
    steps = 4 if all(weight.shape[0] % 32 == 0 for weight in weights) else 1
    count = len(weights)

    def body(factor_ref, *refs):
        grad_refs, refs = refs[:count], refs[count:]
        ins, outs = refs[: 3 * count], refs[3 * count :]
        for index, grad in enumerate(grad_refs):
            for block in range(grad.shape[0]):
                columns = slice(block * grad.shape[2], (block + 1) * grad.shape[2])
                w, m, v = (ins[index + kind * count][:, columns] for kind in range(3))
                new = adam_update(w, grad[block] * factor_ref[0:1, 0:1], m, v, 0.1, 0.1)
                for kind in range(3):
                    outs[index + kind * count][:, columns] = new[kind]

    def rows(value):
        return pl.BlockSpec((value.shape[0] // steps, value.shape[1]), lambda step: (step, 0))

    def blocks(value):
        return pl.BlockSpec((value.shape[0], value.shape[1] // steps, value.shape[2]), lambda step: (0, step, 0))

    states = (*weights, *firsts, *seconds)
    news = pl.pallas_call(
        body,
        grid=(steps,),
        in_specs=[VMEM] + [blocks(grad) for grad in grads] + [rows(value) for value in states],
        out_specs=tuple(rows(value) for value in states),
        out_shape=tuple(jax.ShapeDtypeStruct(value.shape, f32) for value in states),
        compiler_params=pltpu.CompilerParams(vmem_limit_bytes=56 << 20),
        cost_estimate=pl.CostEstimate(flops=0, bytes_accessed=0, transcendentals=0),
    )(factor, *grads, *states)
    return [news[index::count] for index in range(count)]


def layer_norm(x, gain, shift):
    centre = x - jnp.mean(x, axis=-1, keepdims=True)
    var = jnp.mean(centre * centre, axis=-1, keepdims=True)
    return centre * lax.rsqrt(var + 1e-05) * gain + shift


def gelu_fn(x):
    return jax.nn.gelu(x, approximate=True)


def adam_update(weight, grad, first, second, rate, decay):
    first_new = beta_one * first + (1.0 - beta_one) * grad
    second_new = beta_two * second + (1.0 - beta_two) * grad * grad
    mhat = first_new / (1.0 - beta_one**STEP)
    vhat = second_new / (1.0 - beta_two**STEP)
    return (
        weight - rate * (mhat / (jnp.sqrt(vhat) + adam_eps) + decay * weight),
        first_new,
        second_new,
    )


def as_rows(flat):
    return jnp.pad(flat, (0, -flat.size % 1024)).reshape(-1, 128)


def on_device(
    clean_ids,
    lengths,
    masked,
    attn_in,
    attn_out,
    mlp_in,
    mlp_out,
    table,
    positions,
    vectors,
    first_attn_in,
    first_attn_out,
    first_mlp_in,
    first_mlp_out,
    first_table,
    first_positions,
    first_vectors,
    second_attn_in,
    second_attn_out,
    second_mlp_in,
    second_mlp_out,
    second_table,
    second_positions,
    second_vectors,
):
    rows, slots = clean_ids.shape
    n_dp = lax.axis_size("dp")
    n_seq = lax.axis_size("seq")
    dp_at = lax.axis_index("dp")
    seq_at = lax.axis_index("seq")
    core = lax.rem(seq_at, 2)
    length = slots * n_seq
    vocab_part, model = table.shape
    vocab = vocab_part * n_dp
    head_dim = model // H
    sharers = max(1, n_seq // rows)
    n_pick = masked.shape[1] // sharers
    row_at = seq_at // sharers
    share = lax.rem(seq_at, sharers)
    half = -(-vocab_part // 256) * 128
    tile = 128 * max(count for count in range(1, 8) if half % (128 * count) == 0)
    n_x = n_seq // 2
    n_y = 1 << (n_dp.bit_length() - 1) // 2
    n_z = n_dp // n_y

    def piece_of(weight):
        piece = weight.shape[0] // n_seq
        return lax.dynamic_slice_in_dim(weight, seq_at * piece, piece, 0).astype(bf16)

    thick = attn_in.shape[0]
    hidden = mlp_in.shape[1]
    blocks = 4
    split = n_seq // blocks
    thin = thick // split

    def block_of(weights):
        wide = [weight[:, at : at + model] for weight in weights for at in range(0, weight.shape[1], model)]
        wide = jnp.stack(wide).reshape(n_seq, thin, model)
        return lax.dynamic_index_in_dim(wide, seq_at, 0, False).astype(bf16)

    given_rows = [block_of((attn_in, attn_out)), block_of((mlp_in,)), piece_of(mlp_out), piece_of(positions)]
    ends = [0]
    for piece in given_rows:
        ends.append(ends[-1] + piece.shape[0])
    long, some = ends[3] - ends[2], ends[4] - ends[3]
    packed = lax.all_gather(jnp.concatenate(given_rows), ("dp", "seq")).reshape(n_dp, n_seq, -1, model)
    if thin % 16 == 0 and some % 16 == 0 and split == 1:

        def rows_at(part):
            return pl.ds(ends[part], ends[part + 1] - ends[part])

        def blocks_at(part, blocks):
            return [
                ((slice(None), block, rows_at(part)), (at,))
                for at, block in enumerate(blocks)
            ]

        def all_at(part):
            return [((slice(None), slice(None), rows_at(part)), (slice(None),))]

        weight_pieces = (
            packed,
            {
                "pos": all_at(3),
                "w_in": blocks_at(0, range(3)),
                "w_out": [((slice(None), 3, rows_at(0)), (slice(None),))],
                "w_up": blocks_at(1, range(4)),
                "w_down": all_at(2),
            },
        )

        def shape(*dims):
            return jax.ShapeDtypeStruct(dims, bf16)

        pos_all, w_in, w_out = shape(n_dp, n_seq, some, model), shape(3, n_dp, thick, model), shape(n_dp, thick, model)
        w_up, w_down = shape(4, n_dp, thick, model), shape(n_dp, n_seq, long, model)
    else:
        weight_pieces = None

        def columns_of(part, block):
            got = packed[:, block * split : (block + 1) * split, ends[part] : ends[part + 1]]
            return got.reshape(-1, model)

        w_in = jnp.concatenate([columns_of(0, block) for block in range(3)], axis=1)
        w_out = columns_of(0, 3)
        w_up = jnp.concatenate([columns_of(1, block) for block in range(4)], axis=1)
        w_down = packed[:, :, ends[2] : ends[3]].reshape(hidden, model)
        pos_all = packed[:, :, ends[3] :].reshape(length, model)

    all_rows = deliver(clean_ids, ("seq",), 1)
    row_ids = lax.dynamic_index_in_dim(all_rows, row_at, 1, keepdims=False).reshape(length)
    row = dp_at * rows + row_at
    row_length = lax.dynamic_index_in_dim(lengths, row, 0, keepdims=False)
    row_masked = lax.dynamic_index_in_dim(masked, row, 0, keepdims=False)
    picks = lax.dynamic_slice_in_dim(row_masked, share * n_pick, n_pick, 0)
    slot = jnp.arange(length, dtype=i32)
    is_masked = jnp.any(slot[:, None] == row_masked[None, :], axis=1)
    noisy = jnp.where(is_masked, vocab - 1, row_ids)
    targets = jnp.sum(jnp.where(picks[:, None] == slot[None, :], row_ids[None, :], 0), axis=1)
    valid_all = ((masked >= 1) & (masked < lengths[:, None])).astype(f32)
    masked_count = jnp.sum(valid_all)

    owner = noisy // vocab_part
    within = noisy - owner * vocab_part
    owner_half = owner * 2 + (within >= half).astype(i32)
    within_half = jnp.where(within >= half, within - half, within)
    same = noisy[:, None] == noisy[None, :]
    leader = jnp.min(jnp.where(same, slot[None, :], length), axis=1)
    leads = leader == slot
    before = (slot[None, :] < slot[:, None]) & leads[None, :]
    rank = jnp.sum((before & (owner[:, None] == owner[None, :])).astype(i32), axis=1)
    rank_half = jnp.sum((before & (owner_half[:, None] == owner_half[None, :])).astype(i32), axis=1)
    lead_of = leader[:, None] == slot[None, :]
    place = jnp.sum(jnp.where(lead_of, rank[None, :], 0), axis=1)
    place_half = jnp.sum(jnp.where(lead_of, rank_half[None, :], 0), axis=1)

    def asked(owners, ranks, names, count, size, turn):
        spot = jnp.where(ranks // size == turn, owners * size + lax.rem(ranks, size), -1)
        spots = jnp.arange(count * size, dtype=i32)
        listed = leads[None, :] & (spots[:, None] == spot[None, :])
        return spot, jnp.sum(jnp.where(listed, names[None, :], 0), axis=1)

    spot, ask = asked(owner, place, within, n_dp, FETCH, 0)
    spot_half, ask_half = asked(owner_half, place_half, within_half, 2 * n_dp, GIVE, 0)
    turns = jnp.stack([jnp.max(place) // FETCH + 1, jnp.max(place_half) // GIVE + 1])
    pieces = [as_rows(piece) for piece in (ask, ask_half, targets, turns)]
    ends = [0]
    for piece in pieces:
        ends.append(ends[-1] + piece.shape[0])
    told = deliver(jnp.concatenate(pieces), ("dp", "seq"), 2)

    def heard(index, size):
        return told[:, ends[index] : ends[index + 1]].reshape(n_dp * n_seq, -1)[:, :size]

    turns = jnp.max(heard(3, 2), axis=0)
    asks = lax.dynamic_index_in_dim(heard(0, n_dp * FETCH).reshape(n_dp, n_seq, n_dp, FETCH), seq_at, 1, False)
    asks = lax.dynamic_index_in_dim(asks, dp_at, 1, False)
    half_at = dp_at * 2 + core
    asks_half = lax.dynamic_index_in_dim(heard(1, 2 * n_dp * GIVE).reshape(-1, 2 * n_dp, GIVE), half_at, 1, False)
    all_targets = lax.dynamic_index_in_dim(heard(2, n_pick).reshape(n_dp, n_seq, n_pick), seq_at, 1, False)

    def one_hot(spots, count):
        return (spots[:, None] == jnp.arange(count, dtype=i32)[None, :]).astype(bf16)

    table_low, table_turned = table_forms(table, 2 * half, tile)
    found = jnp.take(table_low, asks, axis=0)
    fetched = deliver(found, ("dp",), 3, lambda place: place[0]).reshape(n_dp * FETCH, model)
    embedded = jnp.dot(one_hot(spot, n_dp * FETCH), fetched, preferred_element_type=f32)

    def fetch_more(state):
        turn, total = state
        next_spot, next_ask = asked(owner, place, within, n_dp, FETCH, turn)
        wanted = lax.all_to_all(next_ask.reshape(n_dp, FETCH), "dp", 0, 0)
        sent = jnp.take(table_low, wanted, axis=0)
        got = lax.all_to_all(sent, "dp", 0, 0).reshape(n_dp * FETCH, model)
        return turn + 1, total + jnp.dot(one_hot(next_spot, n_dp * FETCH), got, preferred_element_type=f32)

    _, embedded = lax.while_loop(lambda state: state[0] < turns[0], fetch_more, (jnp.int32(1), embedded))

    embedded = embedded.astype(bf16)
    kept = layer_forward(
        embedded, pos_all, w_in, w_out, w_up, w_down, vectors, picks, row_length, weight_pieces
    )
    sources = kept["f"]

    flat_targets = (all_targets - dp_at * vocab_part).reshape(n_dp, 1, n_pick)
    flat_targets = jnp.where(flat_targets < vocab_part, flat_targets, -1)
    rows_here = valid_all.reshape(n_dp, rows, sharers, n_pick)
    rows_here = lax.dynamic_index_in_dim(rows_here, row_at, 1, False)
    flat_valid = lax.dynamic_index_in_dim(rows_here, share, 1, False).reshape(n_dp, 1, n_pick)
    grown, heads, tops, stats = read_heads(
        sources, table_low, flat_targets, vocab_part, tile, n_y, n_z, 9
    )
    final_grad, logs, *half_parts = write_heads(
        grown, heads, table_turned, tops, stats, flat_targets, flat_valid / masked_count, tile, n_x, 5
    )
    loss_group = jnp.sum(flat_valid * (logs[0] - logs[1]))
    final_grad = jnp.sum(final_grad.astype(f32), axis=0).T
    part = half // n_x
    slab = 16 * max(count for count in range(1, 26) if part % (16 * count) == 0)
    x_at = seq_at // 2

    part_came = [from_peer(half_parts[step], "seq", 2, n_x, step) for step in range(1, n_x)]
    if n_x > 2:
        part_came = [sum(came.astype(f32) for came in part_came).astype(bf16)]

    whole, vec_grad, start_grad_low, first_given = layer_backward(
        final_grad,
        kept,
        embedded,
        pos_all,
        (w_in, w_out, w_up, w_down),
        vectors,
        picks,
        (spot_half, 2 * n_dp * GIVE),
        row_length,
        loss_group,
        n_dp,
        weight_pieces,
    )

    def given(spots):
        summed_ids = jnp.einsum(
            "ts,td->sd", one_hot(spots, 2 * n_dp * GIVE), start_grad_low, preferred_element_type=f32
        )
        return summed_ids.astype(bf16).reshape(2 * n_dp, GIVE, model)

    chunks = 5
    layer_sum, came, vec_total = settle(
        whole.reshape(n_dp, 2, n_x, chunks, -1, model),
        first_given.reshape(2 * n_dp, GIVE, model),
        vec_grad,
        n_x,
        n_y,
        n_z,
        7,
    )
    layer_sum = layer_sum.reshape(-1, model)

    def give_more(state):
        turn, total, _ = state
        next_spot, next_ask = asked(owner_half, place_half, within_half, 2 * n_dp, GIVE, turn)
        names = lax.all_gather(next_ask.reshape(2 * n_dp, GIVE), ("dp", "seq"))
        names = lax.dynamic_index_in_dim(names, half_at, 1, False).reshape(1, -1) - x_at * part
        sent = given(next_spot).reshape(n_dp, 1, 2, GIVE, model)
        sent = jnp.broadcast_to(sent, (n_dp, n_x, 2, GIVE, model)).reshape(-1, GIVE, model)
        got = lax.all_to_all(sent, ("dp", "seq"), 0, 0).reshape(-1, model)
        total, squares = close_half(
            total, jnp.zeros_like(total), names, got, layer_sum, 1.0 / n_seq, slab
        )
        return turn + 1, total, jnp.sum(squares)

    names = asks_half.reshape(1, -1) - x_at * part
    values = came.reshape(-1, model)
    part_own, squares_own = close_half(
        half_parts[0], part_came[0], names, values, layer_sum, 1.0 / n_seq, slab
    )
    _, part_own, part_square = lax.while_loop(
        lambda state: state[0] < turns[1], give_more, (jnp.int32(1), part_own, jnp.sum(squares_own))
    )
    loss_sum = vec_total[14, 0] / n_dp
    vec_total = vec_total[:14]

    said = jnp.where(jnp.arange(8)[:, None] == 0, part_square, jnp.zeros((8, 128), f32))
    told_squares = deliver(said, ("seq",), 8)
    zero = told_squares[0, 1, 0].astype(bf16)
    far_out = part_own + zero
    far_own = [from_peer(far_out, "seq", 2, n_x, step) for step in range(1, n_x)]
    far_own = far_own[0] if n_x == 2 else jnp.concatenate(far_own)
    part_pair = from_peer(part_own, "seq", 1, 2, 1)
    told_squares = deliver(jnp.sum(told_squares, axis=0), ("dp",), 4)
    square_total = jnp.sum(told_squares[:, 0, 0])
    grad_norm = jnp.sqrt(square_total + jnp.sum(vec_total * vec_total))
    factor = clip_at / jnp.maximum(grad_norm, clip_at)
    state = (table, first_table, second_table)
    at = jnp.stack([core, x_at])
    *near, token = adam_table(
        at, told_squares, vec_total, state, part_own, part_pair, slab, half, n_x, (0,), None
    )
    layer_sum = layer_sum.astype(f32) + token[0, 0]
    ends = [0]
    for count in (mlp_out.shape[0], hidden // model * thick, thick, 3 * thick, positions.shape[0]):
        ends.append(ends[-1] + count)
    g_down, g_up, g_out, g_in, g_pos = [layer_sum[begin:end] for begin, end in zip(ends, ends[1:])]
    layer_grads = (
        g_in.reshape(3, thick, model),
        g_out[None],
        g_up.reshape(-1, thick, model),
        g_down[None],
        g_pos[None],
    )
    far_own = far_own + token[0, 0].astype(bf16)
    far_pair = from_peer(far_own, "seq", 1, 2, 1)
    held = jnp.minimum(jnp.abs(far_own[0, 0].astype(f32)), 0.0)
    updates = update_layer(
        (factor + held).reshape(1, 1),
        layer_grads,
        (attn_in, attn_out, mlp_in, mlp_out, positions),
        (first_attn_in, first_attn_out, first_mlp_in, first_mlp_out, first_positions),
        (second_attn_in, second_attn_out, second_mlp_in, second_mlp_out, second_positions),
    )
    results = dict(zip((0, 1, 2, 3, 5), updates))
    results[6] = adam_update(vectors, vec_total * factor, first_vectors, second_vectors, 1.0, 0.0)
    far_steps = tuple(range(1, n_x))
    *results[4], _ = adam_table(
        at, told_squares, vec_total, state, far_own, far_pair, slab, half, n_x, far_steps, near
    )
    news, moments, squares = zip(*(results[index] for index in range(7)))
    return (*news, *moments, *squares, loss_sum, masked_count, grad_norm)


def solution(mesh):
    part = P("dp", None)
    six = (part,) * 6 + (P(),)
    return jax.shard_map(
        on_device,
        mesh=mesh,
        in_specs=(P("dp", "seq"), P(), P()) + six * 3,
        out_specs=six * 3 + (P(), P(), P()),
        check_vma=False,
    )
```
